32 devices in a mesh: dp: 16 (over z, x, core), mp: 2 (over y).
Axes of the slice: x: 2, y: 2, z: 4, core: 2. Of those that a mesh axis runs over, the one named last changes fastest.
Arguments:
- tokens: bfloat16 [32, 680, 1024], P('dp', 'mp'), may hold values from -6 to 6
- condition: bfloat16 [32, 1024], P('dp'), may hold values from -6 to 6
- scale_lengths: int32 [32, 10], P('dp'), may hold values from 1 to 256, 680 in all within a row
- order: int32 [16, 2], P('dp'), may hold values from 0 to 1, each once within a row
- cotangent: bfloat16 [32, 680, 1024], P('dp', 'mp'), may hold values from -6 to 6
- ada_weight: bfloat16 [1024, 6, 1024], P('dp', None, 'mp'), may hold values from -0.1875 to 0.1875
- ada_bias: bfloat16 [6, 16, 64], P(None, 'mp', 'dp'), may hold values from -3 to 3
- qkv_weight: bfloat16 [3, 1024, 1024], P(None, 'dp', 'mp'), may hold values from -0.1875 to 0.1875
- qv_bias: bfloat16 [2, 16, 64], P(None, 'mp', 'dp'), may hold values from -3 to 3
- head_log_scale: float32 [16], P('mp'), may hold values from 2.1 to 3.2
- proj_weight: bfloat16 [1024, 1024], P('mp', 'dp'), may hold values from -1 to 1
- out_bias: bfloat16 [2, 16, 64], P(None, 'mp', 'dp'), may hold values from -2 to 2
- fc1_weight: bfloat16 [1024, 4096], P('dp', 'mp'), may hold values from -0.1875 to 0.1875
- fc1_bias: bfloat16 [64, 64], P('mp', 'dp'), may hold values from -3 to 3
- fc2_weight: bfloat16 [4096, 1024], P('mp', 'dp'), may hold values from -0.09375 to 0.09375
Outputs:
- activations: bfloat16 [32, 680, 1024], P('dp', 'mp')
- tokens_grad: bfloat16 [32, 680, 1024], P('dp', 'mp')
- condition_grad: bfloat16 [32, 1024], P('dp')
- ada_weight_grad: float32 [1024, 6, 1024], P('dp', None, 'mp')
- ada_bias_grad: float32 [6, 16, 64], P(None, 'mp', 'dp')
- qkv_weight_grad: float32 [3, 1024, 1024], P(None, 'dp', 'mp')
- qv_bias_grad: float32 [2, 16, 64], P(None, 'mp', 'dp')
- head_scale_grad: float32 [16], P('mp')
- proj_weight_grad: float32 [1024, 1024], P('mp', 'dp')
- out_bias_grad: float32 [2, 16, 64], P(None, 'mp', 'dp')
- fc1_weight_grad: float32 [1024, 4096], P('dp', 'mp')
- fc1_bias_grad: float32 [64, 64], P('mp', 'dp')
- fc2_weight_grad: float32 [4096, 1024], P('mp', 'dp')
The draws below stay inside these ranges and needn't reach their ends.
Inputs may be any that keep to these rules, and one draw needn't show every extreme that they name: `scale_lengths`: the 10 lengths of every image sum to 680, and one of them equals 256. Each row of order holds every number of 0 to 1 once.
All inputs are finite; a program needn't handle non-finite values.
Results may differ from the reference program's by a relative error of at most 0.02.
Values may be sent and summed in bfloat16 or wider, within the bound.
A program may use at most 192 MiB of HBM per device.

```python
import math
from functools import partial
import jax
import jax.numpy as jnp
import numpy as np
from jax import lax

D = 1024
HEADS = 16
HD = 64
FF = 4096
SEQ = 680
SCALES = 10
MOST = 256
IMG_DEV = 2
IMAGES = 32
N_DP = 16


def levels(own_key, extent, pieces, least, high):
    factor_of = 1.0
    for axis_at, blocks in pieces:
        draws = jax.random.uniform(jax.random.fold_in(jax.random.fold_in(own_key, 6), axis_at), (blocks,), jnp.float32, least / len(pieces), high / len(pieces))
        factor_of = factor_of * jnp.repeat(jnp.exp(draws), extent[axis_at] // blocks).reshape((-1,) + (1,) * (len(extent) - 1 - axis_at))
    return factor_of


def profile(count, total, bound, slope):
    portions = [(1 << 20) // math.isqrt(rank ** slope) + 1 for rank in range(2, count + 1)]
    spare, counts = total - bound - (count - 1), [1] * (count - 1)
    while spare > 0:
        candidates = [i for i in range(count - 1) if counts[i] < bound]
        pool, remaining = sum([portions[i] for i in candidates]), spare
        for i in candidates:
            extra = min(bound - counts[i], max(1, remaining * portions[i] // pool), spare)
            counts[i] = counts[i] + extra
            spare = spare - extra
    return np.array([bound] + counts)


def uneven_parts(own_key, amount, total, bound, lean):
    if amount == 2:
        one = jax.random.randint(own_key, (), max(1, total - bound), min(bound, total - 1) + 1)
        return jnp.stack([one, total - one])
    tallies = jnp.asarray(profile(amount, total, bound, lean), jnp.int32)
    twos = (amount - 1) // 2
    donor, taker = tallies[1:1 + 2 * twos:2], tallies[2:2 + 2 * twos:2]
    room = jnp.minimum(donor - 1, bound - taker)
    moved = jax.random.randint(jax.random.fold_in(own_key, 1), (twos,), 0, 1 << 20) % (room + 1)
    tallies = tallies.at[1:1 + 2 * twos:2].set(donor - moved).at[2:2 + 2 * twos:2].set(taker + moved)
    return tallies[jax.random.permutation(jax.random.fold_in(own_key, 2), amount)]


def scatter_about(own_key, extent, deviation, limit, cuts=(), held_as=jnp.bfloat16):
    values = jax.random.normal(own_key, extent, jnp.float32) * deviation
    if len(cuts) > 0:
        values = levels(own_key, extent, cuts, -0.22, 0.18) * values
    return jnp.clip(values, min=-limit, max=limit).astype(held_as)


def setup_inputs(seed: int = 0) -> dict:
    streams_of = jax.random.split(jax.random.key(seed), 16)
    return {
        "tokens": scatter_about(streams_of[0], (IMAGES, SEQ, D), 1.0, 6.0, ((0, 16), (1, 2))),
        "condition": scatter_about(streams_of[1], (IMAGES, D), 1.0, 6.0, ((0, 16),)),
        "scale_lengths": jax.vmap(lambda own: uneven_parts(own, SCALES, SEQ, MOST, 2))(jax.random.split(streams_of[2], IMAGES)).reshape((IMAGES, SCALES)).astype(jnp.int32),
        "order": jax.vmap(lambda own: jax.random.permutation(own, IMG_DEV))(jax.random.split(streams_of[3], N_DP)).reshape((N_DP, IMG_DEV)).astype(jnp.int32),
        "cotangent": scatter_about(streams_of[4], (IMAGES, SEQ, D), 1.0, 6.0, ((0, 16), (1, 2))),
        "ada_weight": scatter_about(streams_of[5], (D, 6, D), D ** -0.5, 0.1875, ((0, 16), (2, 2))),
        "ada_bias": scatter_about(streams_of[6], (6, HEADS, HD), 0.5, 3.0, ((1, 2), (2, 16))),
        "qkv_weight": scatter_about(streams_of[7], (3, D, D), D ** -0.5, 0.1875, ((1, 16), (2, 2))),
        "qv_bias": scatter_about(streams_of[8], (2, HEADS, HD), 0.5, 3.0, ((1, 2), (2, 16))),
        "head_log_scale": jnp.clip(2.1 + 1.1000001 * jax.random.uniform(streams_of[9], (HEADS,), jnp.float32) ** levels(streams_of[9], (HEADS,), ((0, 2),), -0.2, 0.2), 2.1, 3.2),
        "proj_weight": scatter_about(streams_of[10], (D, D), 32 ** -0.5, 1.0, ((0, 2), (1, 16))),
        "out_bias": scatter_about(streams_of[11], (2, HEADS, HD), 0.3, 2.0, ((1, 2), (2, 16))),
        "fc1_weight": scatter_about(streams_of[12], (D, FF), D ** -0.5, 0.1875, ((0, 16), (1, 2))),
        "fc1_bias": scatter_about(streams_of[13], (FF // HD, HD), 0.5, 3.0, ((0, 2), (1, 16))),
        "fc2_weight": scatter_about(streams_of[14], (FF, D), FF ** -0.5, 0.09375, ((0, 2), (1, 16))),
    }


@jax.custom_vjp
def low(v):
    return lax.optimization_barrier(v.astype(jnp.bfloat16)).astype(jnp.float32)

@jax.custom_vjp
def low_back(v):
    return v

def low_keep(v):
    return (low(v), None)

def low_pass(kept, grad):
    return (grad,)

def back_keep(v):
    return (v, None)

def back_low(kept, grad):
    return (low(grad),)
low.defvjp(low_keep, low_pass)
low_back.defvjp(back_keep, back_low)
precise = lax.Precision.HIGHEST

def matmul_exact(left_side, right_side):
    return jnp.dot(left_side, right_side, precision=precise, preferred_element_type=jnp.float32)

def normalize_rows(values):
    centre = lax.optimization_barrier(jnp.mean(values, -1, keepdims=True))
    shifted = values - centre
    return shifted * lax.rsqrt(lax.optimization_barrier(jnp.mean(shifted * shifted, -1, keepdims=True)) + 1e-06)

def one_image(weights, image):
    qkv_full, qv_full, head_scale, proj_full, outb_full, fc1_full, fc1b_full, fc2_full = weights
    residual, image_mods, lengths = image
    token_count, model_width = residual.shape
    head_count = head_scale.shape[0]
    head_width = model_width // head_count
    scale_ends = jnp.cumsum(lengths)
    positions = jnp.arange(token_count, dtype=jnp.int32)
    scale_of = lax.optimization_barrier(jnp.sum((positions[:, None] >= scale_ends[None, :]).astype(jnp.int32), 1))
    allowed = scale_of[None, :] <= scale_of[:, None]
    input_one = low(normalize_rows(residual) * (1.0 + image_mods[2]) + image_mods[4])
    queries = low_back(matmul_exact(input_one, qkv_full[0]) + qv_full[0]).reshape(token_count, head_count, head_width)
    keys_raw = low_back(matmul_exact(input_one, qkv_full[1])).reshape(token_count, head_count, head_width)
    values_raw = low_back(matmul_exact(input_one, qkv_full[2]) + qv_full[1]).reshape(token_count, head_count, head_width)
    query_low = low(queries * lax.rsqrt(lax.optimization_barrier(jnp.sum(queries * queries, -1, keepdims=True)) + 1e-06) * jnp.exp(head_scale)[None, :, None])
    key_low = low(keys_raw * lax.rsqrt(lax.optimization_barrier(jnp.sum(keys_raw * keys_raw, -1, keepdims=True)) + 1e-06))
    value_low = low(values_raw)
    scores = low_back(jnp.einsum('qhd,khd->hqk', query_low, key_low, precision=precise))
    scores = jnp.where(allowed[None], scores, -1e+30)
    soft_low = low(jax.nn.softmax(scores, -1))
    mixed_heads = low(low_back(jnp.einsum('hqk,khd->qhd', soft_low, value_low, precision=precise))).reshape(token_count, model_width)
    attended = low_back(matmul_exact(mixed_heads, proj_full) + outb_full[0])
    middle = residual + image_mods[0] * attended
    input_two = low(normalize_rows(middle) * (1.0 + image_mods[3]) + image_mods[5])
    hidden = low_back(matmul_exact(input_two, fc1_full) + fc1b_full)
    activated = low(jax.nn.gelu(hidden, approximate=True))
    branch_out = low_back(matmul_exact(activated, fc2_full) + outb_full[1])
    return middle + image_mods[1] * branch_out

def reference(tokens, condition, scale_lengths, order, cotangent, ada_weight, ada_bias, qkv_weight, qv_bias, head_log_scale, proj_weight, out_bias, fc1_weight, fc1_bias, fc2_weight):
    model_width = tokens.shape[2]
    picked = (jnp.arange(N_DP, dtype=jnp.int32)[:, None] * IMG_DEV + order.astype(jnp.int32)).reshape(-1)
    picked_lengths = scale_lengths[picked]
    floats = tuple((member.astype(jnp.float32) for member in (tokens, condition, ada_weight, ada_bias, qkv_weight, qv_bias, head_log_scale, proj_weight, out_bias, fc1_weight, fc1_bias, fc2_weight)))

    def forward(tokens_in, cond_in, ada_w, ada_b, qkv_w, qv_b, scale_w, proj_w, outb_w, fc1_w, fc1b_w, fc2_w):
        signal = low(jax.nn.silu(cond_in))
        modulation = (matmul_exact(signal, ada_w.reshape(model_width, 6 * model_width)) + ada_b.reshape(6 * model_width)).reshape(-1, 6, model_width)
        weights = (qkv_w, qv_b.reshape(2, model_width), scale_w, proj_w, outb_w.reshape(2, model_width), fc1_w, fc1b_w.reshape(-1), fc2_w)
        image_step = jax.checkpoint(partial(one_image, weights))
        return lax.map(image_step, (tokens_in[picked], modulation[picked], picked_lengths))
    result, pullback = jax.vjp(forward, *floats)
    grads = pullback(cotangent.astype(jnp.float32))
    return (result.astype(jnp.bfloat16), grads[0].astype(jnp.bfloat16), grads[1].astype(jnp.bfloat16), grads[2], grads[3], grads[4], grads[5], grads[6], grads[7], grads[8], grads[9], grads[10], grads[11])
```

```python
import functools
import jax
import jax.numpy as jnp
from jax import lax
from jax.experimental import pallas as pl
from jax.experimental.pallas import tpu as pltpu
from jax.sharding import PartitionSpec as P

F32 = jnp.float32
BF16 = jnp.bfloat16
MESH = pl.DeviceIdType.MESH
LOG2E = 1.4426950408889634
VMEM_LIMIT = 60 * 1024 * 1024


def mm(a, b):
    return jnp.dot(a, b, preferred_element_type=F32)


def mm_nt(a, b):
    return lax.dot_general(a, b, (((1,), (1,)), ((), ())), preferred_element_type=F32)


def mm_tn(a, b):
    return lax.dot_general(a, b, (((0,), (0,)), ((), ())), preferred_element_type=F32)


def norm_rows(values):
    centre = jnp.mean(values, -1, keepdims=True)
    shifted = values - centre
    inverse = lax.rsqrt(jnp.mean(shifted * shifted, -1, keepdims=True) + 1e-06)
    return shifted * inverse, inverse


def norm_rows_back(incoming, normed, inverse):
    return inverse * (
        incoming
        - jnp.mean(incoming, -1, keepdims=True)
        - normed * jnp.mean(incoming * normed, -1, keepdims=True)
    )


def split_three(values):
    high = values.astype(BF16)
    rest = values - high.astype(F32)
    middle = rest.astype(BF16)
    return high, middle, (rest - middle.astype(F32)).astype(BF16)


def forward_kernel(
    heads, width, x_ref, mod_ref, wq_ref, wk_ref, wv_ref, wp_ref, bias_ref, vec_ref, boost_ref,
    kmask_ref, qmask_ref,
    mid_ref, att_ref, two_ref, ql_ref, kl_ref, vl_ref, mix_ref, stat_ref,
    one_s, acc_s,
):
    step = pl.program_id(0)

    @pl.when(step == 0)
    def _():
        normed, _ = norm_rows(x_ref[...].astype(F32))
        one_s[...] = (normed * (1.0 + mod_ref[2:3]) + mod_ref[4:5]).astype(BF16)
        acc_s[...] = jnp.zeros_like(acc_s)

    one = one_s[...]
    queries = mm(one, wq_ref[0]) + bias_ref[0:1]
    keys = mm(one, wk_ref[0])
    values = (mm(one, wv_ref[0]) + bias_ref[1:2]).astype(BF16)
    vl_ref[...] = values
    q_turned = queries.T
    k_turned = keys.T
    boost = boost_ref[0]
    kmask = kmask_ref[...]
    qmask = qmask_ref[...]
    rows = q_turned.shape[1]
    ones = jnp.ones((rows, width), BF16)
    q_low, k_low, mixed = [], [], []
    q_inv, k_inv, totals = [], [], []
    for head in range(heads):
        part = slice(head * width, (head + 1) * width)
        q_now, k_now = q_turned[part], k_turned[part]
        q_scale = lax.rsqrt(jnp.sum(q_now * q_now, 0, keepdims=True) + 1e-06)
        k_scale = lax.rsqrt(jnp.sum(k_now * k_now, 0, keepdims=True) + 1e-06)
        q_bf = (q_now * q_scale * boost[0:1, head : head + 1]).astype(BF16)
        k_bf = (k_now * k_scale).astype(BF16)
        scaled = q_bf.astype(F32) * LOG2E
        high = scaled.astype(BF16)
        rest = (scaled - high.astype(F32)).astype(BF16)
        q_all = jnp.concatenate([high, rest, qmask], 0)
        k_all = jnp.concatenate([k_bf, k_bf, kmask], 0)
        weights = jnp.exp2(mm_tn(q_all, k_all)).astype(BF16)
        v_all = jnp.concatenate([values[:, part], ones], 1)
        summed = mm(weights, v_all)
        total = summed[:, width:]
        mixed.append((summed[:, :width] / total).astype(BF16))
        totals.append(total[:, 0:1])
        q_low.append(q_bf)
        k_low.append(k_bf)
        q_inv.append(q_scale)
        k_inv.append(k_scale)
    mixed_all = jnp.concatenate(mixed, 1)
    mix_ref[...] = mixed_all
    ql_ref[...] = jnp.concatenate(q_low, 0)
    kl_ref[...] = jnp.concatenate(k_low, 0)
    log_total = jnp.log2(jnp.concatenate(totals + totals, 1)).T
    stat_ref[0, 0] = jnp.concatenate(q_inv + k_inv, 0)
    stat_ref[0, 1] = log_total
    acc_s[...] += mm_nt(mixed_all, wp_ref[0])

    @pl.when(step == pl.num_programs(0) - 1)
    def _():
        attended = acc_s[...] + vec_ref[2:3]
        att_ref[...] = attended.astype(BF16)
        middle = x_ref[...].astype(F32) + mod_ref[0:1] * attended
        mid_ref[...] = middle
        normed, _ = norm_rows(middle)
        two_ref[...] = (normed * (1.0 + mod_ref[3:4]) + mod_ref[5:6]).astype(BF16)


def feed_kernel(
    two_ref, mid_ref, cot_ref, mod_ref, vec_ref, w1_ref, w2_ref, b1_ref,
    out_ref, gmid_ref, rows_ref, g1_ref, g2_ref, gb1_ref,
    back_s, backt_s, twot_s, acc_s, gacc_s,
):
    step = pl.program_id(0)

    @pl.when(step == 0)
    def _():
        back = (mod_ref[1:2] * cot_ref[...].astype(F32)).astype(BF16)
        back_s[...] = back
        backt_s[...] = back.T
        twot_s[...] = two_ref[...].T
        acc_s[...] = jnp.zeros_like(acc_s)
        gacc_s[...] = jnp.zeros_like(gacc_s)

    w1, w2 = w1_ref[0], w2_ref[0]
    hidden = mm(two_ref[...], w1) + b1_ref[0:1]
    square = hidden * hidden
    curve = jnp.tanh(0.7978845608028654 * hidden * (1.0 + 0.044715 * square))
    half = 0.5 * (1.0 + curve)
    activated = (hidden * half).astype(BF16)
    slope = half + 0.5 * hidden * (1.0 - curve * curve) * (
        0.7978845608028654 * (1.0 + 0.134145 * square)
    )
    acc_s[...] += mm_nt(activated, w2)
    g2_ref[0] = mm(backt_s[...], activated).astype(BF16)
    hidden_grad = (mm(back_s[...], w2) * slope).astype(BF16)
    g1_ref[0] = mm(twot_s[...], hidden_grad).astype(BF16)
    gb1_ref[...] = jnp.broadcast_to(
        jnp.sum(hidden_grad.astype(F32), 0, keepdims=True), gb1_ref.shape
    )
    gacc_s[...] += mm_nt(hidden_grad, w1)

    @pl.when(step == pl.num_programs(0) - 1)
    def _():
        middle = mid_ref[...]
        out_grad = cot_ref[...].astype(F32)
        branch = acc_s[...] + vec_ref[3:4]
        out_ref[...] = (middle + mod_ref[1:2] * branch).astype(BF16)
        normed, inverse = norm_rows(middle)
        grad = gacc_s[...]
        gmid_ref[...] = out_grad + norm_rows_back(grad * (1.0 + mod_ref[3:4]), normed, inverse)
        rows_ref[0:1] = jnp.sum(out_grad * branch, 0, keepdims=True)
        rows_ref[1:2] = jnp.sum(grad * normed, 0, keepdims=True)
        rows_ref[2:3] = jnp.sum(grad, 0, keepdims=True)
        rows_ref[3:4] = jnp.sum(back_s[...].astype(F32), 0, keepdims=True)
        rows_ref[4:8] = jnp.zeros((4, rows_ref.shape[1]), F32)


def backward_kernel(
    heads, width, levels, x_ref, gmid_ref, att_ref, mod_ref, ql_ref, kl_ref, vl_ref, mix_ref,
    stat_ref, wq_ref, wk_ref, wv_ref, wp_ref, boost_ref, kmask_ref, qmask_ref,
    tok_ref, rows_ref, gq_ref, gk_ref, gv_ref, gp_ref, sums_ref,
    ga_s, gat_s, onet_s, acc_s,
):
    step = pl.program_id(0)

    @pl.when(step == 0)
    def _():
        attend_grad = (mod_ref[0:1] * gmid_ref[...]).astype(BF16)
        ga_s[...] = attend_grad
        gat_s[...] = attend_grad.T
        normed, _ = norm_rows(x_ref[...].astype(F32))
        onet_s[...] = (normed * (1.0 + mod_ref[2:3]) + mod_ref[4:5]).astype(BF16).T
        acc_s[...] = jnp.zeros_like(acc_s)
        rows_ref[2:3] = jnp.sum(attend_grad.astype(F32), 0, keepdims=True)

    gp_ref[0] = mm(gat_s[...], mix_ref[...]).astype(BF16)
    mixed_grad = mm(ga_s[...], wp_ref[0]).astype(BF16)
    mixed_turned = mixed_grad.T
    v_turned = vl_ref[...].T
    q_plain = ql_ref[...].T
    boost = boost_ref[0]
    kmask, qmask = kmask_ref[...], qmask_ref[...]
    rows = kmask.shape[1]
    place = lax.broadcasted_iota(jnp.int32, (16, rows), 0)

    def pieces(row, first):
        high, mid, low = split_three(row)
        zero = jnp.zeros((16, rows), BF16)
        out = jnp.where(place == first, jnp.broadcast_to(high, zero.shape), zero)
        out = jnp.where(place == first + 1, jnp.broadcast_to(mid, zero.shape), out)
        return jnp.where(place == first + 2, jnp.broadcast_to(low, zero.shape), out)

    dq_rows, dk_rows, dv_cols, scales = [], [], [], []
    for head in range(heads):
        part = slice(head * width, (head + 1) * width)
        lift = boost[0:1, head : head + 1]
        q_bf, k_bf = ql_ref[part], kl_ref[part]
        q_float = q_bf.astype(F32)
        scaled = q_float * LOG2E
        high = scaled.astype(BF16)
        rest = (scaled - high.astype(F32)).astype(BF16)
        log_total = stat_ref[0, 1, head : head + 1]
        q_all = jnp.concatenate([high, rest, qmask + pieces(-log_total, levels + 1)], 0)
        k_all = jnp.concatenate([k_bf, k_bf, kmask], 0)
        soft = jnp.exp2(mm_tn(k_all, q_all))
        product = soft * mm_tn(v_turned[part], mixed_turned[part])
        delta = jnp.sum(product, 0, keepdims=True)
        scores_grad = (product - soft * delta).astype(BF16)
        dv_cols.append(mm(soft.astype(BF16), mixed_grad[:, part]))
        dq_low = mm(k_bf, scores_grad)
        dk_low = mm(scores_grad, q_plain[:, part]).T
        q_inv = stat_ref[0, 0, head : head + 1]
        k_inv = stat_ref[0, 0, heads + head : heads + head + 1]
        q_unit = q_float * (1.0 / lift)
        k_unit = k_bf.astype(F32)
        along = dq_low * q_float
        scales.append(jnp.broadcast_to(jnp.sum(along), (1, 128)))
        dq_unit = dq_low * lift
        dq_rows.append(q_inv * (dq_unit - q_unit * jnp.sum(along, 0, keepdims=True)))
        dk_rows.append(k_inv * (dk_low - k_unit * jnp.sum(dk_low * k_unit, 0, keepdims=True)))
    dq = jnp.concatenate(dq_rows, 0).T.astype(BF16)
    dk = jnp.concatenate(dk_rows, 0).T.astype(BF16)
    dv = jnp.concatenate(dv_cols, 1).astype(BF16)
    one_turned = onet_s[...]
    gq_ref[0] = mm(one_turned, dq).astype(BF16)
    gk_ref[0] = mm(one_turned, dk).astype(BF16)
    gv_ref[0] = mm(one_turned, dv).astype(BF16)
    acc_s[...] += mm_nt(dq, wq_ref[0]) + mm_nt(dk, wk_ref[0]) + mm_nt(dv, wv_ref[0])
    span = dq.shape[1]
    sums_ref[0, 0:1, :] = jnp.sum(dq.astype(F32), 0, keepdims=True)
    sums_ref[0, 1:2, :] = jnp.sum(dv.astype(F32), 0, keepdims=True)
    sums_ref[0, 2:4, :] = jnp.zeros((2, span), F32)
    for head in range(heads):
        sums_ref[0, 4 + head : 5 + head, :] = jnp.broadcast_to(scales[head][:, 0:1], (1, span))

    @pl.when(step == pl.num_programs(0) - 1)
    def _():
        grad = acc_s[...]
        normed, inverse = norm_rows(x_ref[...].astype(F32))
        middle_grad = gmid_ref[...]
        tok_ref[...] = (
            middle_grad + norm_rows_back(grad * (1.0 + mod_ref[2:3]), normed, inverse)
        ).astype(BF16)
        rows_ref[0:1] = jnp.sum(grad * normed, 0, keepdims=True)
        rows_ref[1:2] = jnp.sum(grad, 0, keepdims=True)
        rows_ref[3:4] = jnp.sum(middle_grad * att_ref[...].astype(F32), 0, keepdims=True)
        rows_ref[4:8] = jnp.zeros((4, rows_ref.shape[1]), F32)


def whole(shape):
    return pl.BlockSpec(shape, lambda g: (0,) * len(shape))


def run_forward(x, mods, qkv, projt, vecs, boosts, kmask, qmask, width=64):
    rows, model = x.shape
    heads = 256 // width
    groups = model // 256
    per = qkv.shape[2] // 3 // 256
    half = lambda base: pl.BlockSpec((1, model, 256), lambda g: (g // per, 0, base * per + g % per))
    return pl.pallas_call(
        functools.partial(forward_kernel, heads, width),
        grid=(groups,),
        in_specs=[
            whole(x.shape), whole(mods.shape), half(0), half(1), half(2), half(0),
            pl.BlockSpec((8, 256), lambda g: (0, g)), whole(vecs.shape),
            pl.BlockSpec((1, 8, 128), lambda g: (g, 0, 0)), whole(kmask.shape), whole(qmask.shape),
        ],
        out_shape=[
            jax.ShapeDtypeStruct((rows, model), F32),
            jax.ShapeDtypeStruct((rows, model), BF16),
            jax.ShapeDtypeStruct((rows, model), BF16),
            jax.ShapeDtypeStruct((model, rows), BF16),
            jax.ShapeDtypeStruct((model, rows), BF16),
            jax.ShapeDtypeStruct((rows, model), BF16),
            jax.ShapeDtypeStruct((rows, model), BF16),
            jax.ShapeDtypeStruct((groups, 2, 8, rows), F32),
        ],
        out_specs=[
            whole((rows, model)), whole((rows, model)), whole((rows, model)),
            pl.BlockSpec((256, rows), lambda g: (g, 0)),
            pl.BlockSpec((256, rows), lambda g: (g, 0)),
            pl.BlockSpec((rows, 256), lambda g: (0, g)),
            pl.BlockSpec((rows, 256), lambda g: (0, g)),
            pl.BlockSpec((1, 2, 8, rows), lambda g: (g, 0, 0, 0)),
        ],
        scratch_shapes=[pltpu.VMEM((rows, model), BF16), pltpu.VMEM((rows, model), F32)],
        compiler_params=pltpu.CompilerParams(vmem_limit_bytes=VMEM_LIMIT),
        name="attend",
    )(x, mods, qkv, qkv, qkv, projt, vecs, vecs, boosts, kmask, qmask)


def run_feed(two, middle, cot, mods, vecs, fc1, fc2t, b1, block=512):
    rows, model = two.shape
    cols = fc1.shape[2]
    per = cols // block
    steps = 2 * per
    weight = pl.BlockSpec((1, model, block), lambda g: (g // per, 0, g % per))
    return pl.pallas_call(
        feed_kernel,
        grid=(steps,),
        in_specs=[
            whole(two.shape), whole(middle.shape), whole(cot.shape), whole(mods.shape), whole(vecs.shape),
            weight, weight, pl.BlockSpec((8, block), lambda g: (0, g)),
        ],
        out_shape=[
            jax.ShapeDtypeStruct((rows, model), BF16),
            jax.ShapeDtypeStruct((rows, model), F32),
            jax.ShapeDtypeStruct((8, model), F32),
            jax.ShapeDtypeStruct(fc1.shape, BF16),
            jax.ShapeDtypeStruct(fc2t.shape, BF16),
            jax.ShapeDtypeStruct((8, 2 * cols), F32),
        ],
        out_specs=[
            whole((rows, model)), whole((rows, model)), whole((8, model)), weight, weight,
            pl.BlockSpec((8, block), lambda g: (0, g)),
        ],
        scratch_shapes=[
            pltpu.VMEM((rows, model), BF16), pltpu.VMEM((model, rows), BF16), pltpu.VMEM((model, rows), BF16),
            pltpu.VMEM((rows, model), F32), pltpu.VMEM((rows, model), F32),
        ],
        compiler_params=pltpu.CompilerParams(vmem_limit_bytes=VMEM_LIMIT),
        name="feed",
    )(two, middle, cot, mods, vecs, fc1, fc2t, b1)


def run_backward(levels, x, gmid, att, mods, saved, qkv, projt, boosts, kmask, qmask, width=64):
    q_low, k_low, v_low, mixed, stats = saved
    rows, model = x.shape
    heads = 256 // width
    groups = model // 256
    per = qkv.shape[2] // 3 // 256
    half = lambda base: pl.BlockSpec((1, model, 256), lambda g: (g // per, 0, base * per + g % per))
    turned = pl.BlockSpec((256, rows), lambda g: (g, 0))
    plain = pl.BlockSpec((rows, 256), lambda g: (0, g))
    grad = jax.ShapeDtypeStruct(projt.shape, BF16)
    return pl.pallas_call(
        functools.partial(backward_kernel, heads, width, levels),
        grid=(groups,),
        in_specs=[
            whole(x.shape), whole(gmid.shape), whole(att.shape), whole(mods.shape),
            turned, turned, plain, plain, pl.BlockSpec((1, 2, 8, rows), lambda g: (g, 0, 0, 0)),
            half(0), half(1), half(2), half(0),
            pl.BlockSpec((1, 8, 128), lambda g: (g, 0, 0)), whole(kmask.shape), whole(qmask.shape),
        ],
        out_shape=[
            jax.ShapeDtypeStruct((rows, model), BF16), jax.ShapeDtypeStruct((8, model), F32),
            grad, grad, grad, grad, jax.ShapeDtypeStruct((groups, 8, 256), F32),
        ],
        out_specs=[
            whole((rows, model)), whole((8, model)), half(0), half(0), half(0), half(0),
            pl.BlockSpec((1, 8, 256), lambda g: (g, 0, 0)),
        ],
        scratch_shapes=[
            pltpu.VMEM((rows, model), BF16), pltpu.VMEM((model, rows), BF16), pltpu.VMEM((model, rows), BF16),
            pltpu.VMEM((rows, model), F32),
        ],
        compiler_params=pltpu.CompilerParams(vmem_limit_bytes=VMEM_LIMIT),
        name="attend_back",
    )(x, gmid, att, mods, q_low, k_low, v_low, mixed, stats, qkv, qkv, qkv, projt, boosts, kmask, qmask)


def build_masks(lengths, half_rows, padded):
    count = lengths.shape[0]
    steps = jnp.arange(count, dtype=jnp.int32)
    ends = jnp.sum(jnp.where(steps[None, :] <= steps[:, None], lengths[None, :], 0), 1)
    place = jnp.arange(2 * padded, dtype=jnp.int32)
    part, inside = place // padded, place % padded
    token = part * half_rows + inside
    level = jnp.sum((token[None, :] >= ends[:, None]).astype(jnp.int32), 0)
    real = inside < half_rows
    entry = jnp.arange(16, dtype=jnp.int32)[:, None]
    key_level = jnp.where(real, level, count)[None]
    kmask = (entry == key_level) | ((entry > count) & (entry < count + 4))
    query_level = jnp.where(real, level, count - 1)[None]
    qmask = (entry > query_level) & (entry <= count)
    return kmask.astype(BF16), jnp.where(qmask, -32768.0, 0.0).astype(BF16)


def where_am_i():
    dp, y = lax.axis_index("dp"), lax.axis_index("mp")
    return dp // 4, (dp // 2) % 2, dp % 2, y


def device(z, x, c, y):
    return (z * 4 + x * 2 + c, y)


def greet(line, z, x, c, y):
    barrier = pltpu.get_barrier_semaphore()

    def signal(target):
        pl.semaphore_signal(barrier, inc=1, device_id=target, device_id_type=MESH)

    signal(device(z, x, 1 - c, y))
    signal(device(z, 1 - x, c, y))
    signal(device(z, x, c, 1 - y))

    @pl.when(z > 0)
    def _():
        signal(device(z - 1, x, c, y))

    @pl.when(z < line - 1)
    def _():
        signal(device(z + 1, x, c, y))

    ends = (z == 0).astype(jnp.int32) + (z == line - 1).astype(jnp.int32)
    pl.semaphore_wait(barrier, 5 - ends)


def run_ticks(count, stages):
    for tick in range(count + len(stages) - 1):
        for at, stage in enumerate(stages):
            if 0 <= tick - at < count:
                stage(tick - at)


def gather_kernel(chunks, line, n_seg, n_pair, *refs):
    ins, pair_in = refs[:n_seg], refs[n_seg : n_seg + n_pair]
    outs = refs[n_seg + n_pair : 2 * n_seg + n_pair]
    pair_out = refs[2 * n_seg + n_pair : 2 * (n_seg + n_pair)]
    local_sem, pair_local, pair_send, pair_recv, z_send, z_recv, send_sem, recv_sem = refs[2 * (n_seg + n_pair) :]
    z, x, c, y = where_am_i()
    own = [pltpu.make_async_copy(i, o.at[y, z, x, c], local_sem.at[s]) for s, (i, o) in enumerate(zip(ins, outs))]
    for copy in own:
        copy.start()
    greet(line, z, x, c, y)
    pairs = []
    for p in range(n_pair):
        pairs.append(pltpu.make_async_copy(pair_in[p].at[y], pair_out[p].at[y], pair_local.at[p]))
        pairs.append(
            pltpu.make_async_remote_copy(
                pair_in[p].at[1 - y], pair_out[p].at[y], pair_send.at[p], pair_recv.at[p],
                device_id=device(z, x, c, 1 - y), device_id_type=MESH,
            )
        )
    for copy in own:
        copy.wait()

    def hop(k, way, j):
        seg, _, start, cols = chunks[k]
        out, step = outs[seg], 1 - 2 * way
        going, coming = z - step * j, z - step * (j + 1)
        sends = (going >= 0) & (going < line) & (z + step >= 0) & (z + step < line)
        receives = (coming >= 0) & (coming < line)

        def copy(owner):
            ref = out.at[y, owner, x, c, :, pl.ds(start, cols)]
            return pltpu.make_async_remote_copy(
                ref, ref, z_send.at[k, way, j], z_recv.at[k, way, j],
                device_id=device(z + step, x, c, y), device_id_type=MESH,
            )

        return sends, (lambda: copy(going)), receives, (lambda: copy(coming))

    def group(k, slot, yy, xx, target):
        seg, _, start, cols = chunks[k]
        ref = outs[seg].at[yy, :, xx, c, :, pl.ds(start, cols)]
        return pltpu.make_async_remote_copy(
            ref, ref, send_sem.at[k, slot], recv_sem.at[k, slot], device_id=target, device_id_type=MESH
        )

    x_side, y_side, sibling = device(z, 1 - x, c, y), device(z, x, c, 1 - y), device(z, x, 1 - c, y)

    def groups(k):
        if chunks[k][1] == 0:
            return [(y, x), (y, 1 - x), (1 - y, x), (1 - y, 1 - x)], x_side, y_side
        return [(y, x), (1 - y, x), (y, 1 - x), (1 - y, 1 - x)], y_side, x_side

    def z_stage(j):
        def stage(k):
            for way in range(2):
                if j > 0:
                    _, _, receives, landed = hop(k, way, j - 1)

                    @pl.when(receives)
                    def _():
                        landed().wait_recv()

                if j < line - 1:
                    sends, copy, _, _ = hop(k, way, j)

                    @pl.when(sends)
                    def _():
                        copy().start()

        return stage

    def first_stage(k):
        order, first, second = groups(k)
        group(k, 0, *order[0], first).start()
        group(k, 1, *order[0], second).start()
        group(k, 3, *order[0], sibling).start()

    def second_stage(k):
        order, first, second = groups(k)
        group(k, 0, *order[1], first).wait_recv()
        group(k, 2, *order[1], second).start()
        group(k, 4, *order[1], sibling).start()

    def last_stage(k):
        order, first, second = groups(k)
        group(k, 1, *order[2], second).wait_recv()
        group(k, 5, *order[2], sibling).start()
        group(k, 2, *order[3], second).wait_recv()
        group(k, 6, *order[3], sibling).start()

    def first_with_pairs(k):
        first_stage(k)
        if k == 1:
            for copy in pairs:
                copy.start()

    def z_last_and_first(k):
        z_stage(line - 1)(k)
        first_with_pairs(k)

    run_ticks(len(chunks), [z_stage(j) for j in range(line - 1)] + [z_last_and_first, second_stage, last_stage])
    for copy in pairs:
        copy.wait()
    for k in range(len(chunks)):
        order, first, second = groups(k)
        for way in range(2):
            for j in range(line - 1):
                sends, copy, _, _ = hop(k, way, j)

                @pl.when(sends)
                def _():
                    copy().wait_send()

        for slot, at in ((0, 0), (1, 0), (2, 1), (3, 0), (4, 1), (5, 2), (6, 3)):
            group(k, slot, *order[at], sibling).wait_send()
        for slot, at in ((3, 0), (4, 1), (5, 2), (6, 3)):
            group(k, slot, *order[at], sibling).wait_recv()


def run_gather(chunks, segments, pairs, line, collective_id):
    n_seg, n_pair, count = len(segments), len(pairs), len(chunks)
    anywhere = pl.BlockSpec(memory_space=pl.ANY)
    made = pl.pallas_call(
        functools.partial(gather_kernel, chunks, line, n_seg, n_pair),
        out_shape=[jax.ShapeDtypeStruct((2, line, 2, 2) + s.shape, s.dtype) for s in segments]
        + [jax.ShapeDtypeStruct(p.shape, p.dtype) for p in pairs],
        in_specs=[anywhere] * (n_seg + n_pair),
        out_specs=[anywhere] * (n_seg + n_pair),
        scratch_shapes=[
            pltpu.SemaphoreType.DMA((n_seg,)), pltpu.SemaphoreType.DMA((n_pair,)),
            pltpu.SemaphoreType.DMA((n_pair,)), pltpu.SemaphoreType.DMA((n_pair,)),
            pltpu.SemaphoreType.DMA((count, 2, line - 1)), pltpu.SemaphoreType.DMA((count, 2, line - 1)),
            pltpu.SemaphoreType.DMA((count, 7)), pltpu.SemaphoreType.DMA((count, 7)),
        ],
        compiler_params=pltpu.CompilerParams(collective_id=collective_id, has_side_effects=True),
        name="gather_weights",
    )(*segments, *pairs)
    return made[:n_seg], made[n_seg:]


def add_into(target, source, pieces, target_at, source_at):
    def body(i, carry):
        t, s = target_at(i), source_at(i)
        target[t] = target[t] + source[s]
        return carry

    lax.fori_loop(0, pieces, body, 0)


def scatter_kernel(chunks, line, n_seg, n_pair, *refs):
    count = len(chunks)
    ins, pair_in = refs[:n_seg], refs[n_seg : n_seg + n_pair]
    outs = refs[n_seg + n_pair : 2 * n_seg + n_pair]
    pair_out = refs[2 * n_seg + n_pair : 2 * (n_seg + n_pair)]
    rest = refs[2 * (n_seg + n_pair) :]
    core_b, first_b, second_b, up_b, down_b, own_b = (rest[i * count : (i + 1) * count] for i in range(6))
    pair_local, pair_send, pair_recv, own_sem, send_sem, recv_sem, z_send, z_recv = rest[6 * count :]
    z, x, c, y = where_am_i()
    x_side, y_side, sibling = device(z, 1 - x, c, y), device(z, x, c, 1 - y), device(z, x, 1 - c, y)
    greet(line, z, x, c, y)

    def remote(source, target, send, recv, to):
        return pltpu.make_async_remote_copy(source, target, send, recv, device_id=to, device_id_type=MESH)

    pairs = []
    for p in range(n_pair):
        pairs.append(pltpu.make_async_copy(pair_in[p].at[y], pair_out[p].at[y], pair_local.at[p]))
        pairs.append(remote(pair_in[p].at[1 - y], pair_out[p].at[y], pair_send.at[p], pair_recv.at[p], y_side))

    def core_copy(k):
        seg, _, start, cols = chunks[k]
        source = ins[seg].at[:, :, :, 1 - c, :, pl.ds(start, cols)]
        return remote(source, core_b[k], send_sem.at[k, 0], recv_sem.at[k, 0], sibling)

    def own_copy(k):
        seg, _, start, cols = chunks[k]
        return pltpu.make_async_copy(ins[seg].at[:, :, :, c, :, pl.ds(start, cols)], own_b[k], own_sem.at[k])

    def first_copy(k):
        if chunks[k][1] == 0:
            return remote(core_b[k].at[1 - y], first_b[k], send_sem.at[k, 1], recv_sem.at[k, 1], y_side)
        return remote(core_b[k].at[:, :, 1 - x], first_b[k], send_sem.at[k, 1], recv_sem.at[k, 1], x_side)

    def second_copy(k):
        if chunks[k][1] == 0:
            return remote(first_b[k].at[:, 1 - x], second_b[k], send_sem.at[k, 2], recv_sem.at[k, 2], x_side)
        return remote(first_b[k].at[1 - y], second_b[k], send_sem.at[k, 2], recv_sem.at[k, 2], y_side)

    def line_copy(k, way, owner):
        landing = (up_b, down_b)[way][k]
        return remote(
            second_b[k].at[owner], landing.at[owner], z_send.at[k, way, owner], z_recv.at[k, way, owner],
            device(z + 1 - 2 * way, x, c, y),
        )

    def core_stage(k):
        core_copy(k).start()
        own_copy(k).start()

    def first_stage(k):
        core_copy(k).wait_recv()
        own_copy(k).wait()
        at = lambda i: (i // (2 * line), (i // 2) % line, i % 2)
        add_into(core_b[k], own_b[k], 4 * line, at, at)
        first_copy(k).start()

    def second_stage(k):
        first_copy(k).wait_recv()
        if chunks[k][1] == 0:
            add_into(first_b[k], core_b[k], 2 * line, lambda i: (i // 2, i % 2), lambda i: (y, i // 2, i % 2))
        else:
            add_into(first_b[k], core_b[k], 2 * line, lambda i: (i // line, i % line), lambda i: (i // line, i % line, x))
        second_copy(k).start()

    def third_stage(k):
        second_copy(k).wait_recv()
        if chunks[k][1] == 0:
            add_into(second_b[k], first_b[k], line, lambda i: (i,), lambda i: (i, x))
        else:
            add_into(second_b[k], first_b[k], line, lambda i: (i,), lambda i: (y, i))

    def line_stage(j):
        def stage(k):
            if j == 0:
                third_stage(k)
            for way in range(2):
                place = j if way == 0 else line - 1 - j
                owners = range(line - 1, place, -1) if way == 0 else range(place)

                @pl.when(z == place)
                def _():
                    for owner in owners:
                        if j > 0:
                            line_copy(k, way, owner).wait_recv()
                            second_b[k][owner] = second_b[k][owner] + (up_b, down_b)[way][k][owner]
                        line_copy(k, way, owner).start()

        return stage

    def last_stage(k):
        seg, _, start, cols = chunks[k]
        total = second_b[k].at[z]
        outs[seg][:, pl.ds(start, cols)] = total[...].astype(F32)
        for way in range(2):

            @pl.when((z > 0) if way == 0 else (z < line - 1))
            def _():
                line_copy(k, way, z).wait_recv()
                part = (up_b, down_b)[way][k][z]
                outs[seg][:, pl.ds(start, cols)] += part.astype(F32)

    def core_with_pairs(k):
        core_stage(k)
        if k == 1:
            for copy in pairs:
                copy.start()

    run_ticks(count, [core_with_pairs, first_stage, second_stage] + [line_stage(j) for j in range(line - 1)] + [last_stage])
    for copy in pairs:
        copy.wait()
    for k in range(count):
        core_copy(k).wait_send()
        first_copy(k).wait_send()
        second_copy(k).wait_send()
        for way in range(2):
            for owner in range(line):

                @pl.when((z < owner) if way == 0 else (z > owner))
                def _():
                    line_copy(k, way, owner).wait_send()


def run_scatter(chunks, segments, pairs, line, collective_id):
    n_seg, n_pair, count = len(segments), len(pairs), len(chunks)
    anywhere = pl.BlockSpec(memory_space=pl.ANY)
    inside = pl.BlockSpec(memory_space=pltpu.VMEM)
    core_b, first_b, second_b, own_b = [], [], [], []
    for seg, kind, _, cols in chunks:
        rows = segments[seg].shape[4]
        core_b.append(pltpu.VMEM((2, line, 2, rows, cols), BF16))
        first_b.append(pltpu.VMEM(((line, 2) if kind == 0 else (2, line)) + (rows, cols), BF16))
        second_b.append(pltpu.VMEM((line, rows, cols), BF16))
        own_b.append(pltpu.VMEM((2, line, 2, rows, cols), BF16))
    made = pl.pallas_call(
        functools.partial(scatter_kernel, chunks, line, n_seg, n_pair),
        out_shape=[jax.ShapeDtypeStruct(s.shape[4:], F32) for s in segments]
        + [jax.ShapeDtypeStruct(p.shape, p.dtype) for p in pairs],
        in_specs=[anywhere] * (n_seg + n_pair),
        out_specs=[inside] * n_seg + [anywhere] * n_pair,
        scratch_shapes=core_b + first_b + second_b + second_b + second_b + own_b
        + [
            pltpu.SemaphoreType.DMA((n_pair,)), pltpu.SemaphoreType.DMA((n_pair,)), pltpu.SemaphoreType.DMA((n_pair,)),
            pltpu.SemaphoreType.DMA((count,)),
            pltpu.SemaphoreType.DMA((count, 3)), pltpu.SemaphoreType.DMA((count, 3)),
            pltpu.SemaphoreType.DMA((count, 2, line)), pltpu.SemaphoreType.DMA((count, 2, line)),
        ],
        compiler_params=pltpu.CompilerParams(
            collective_id=collective_id, has_side_effects=True, vmem_limit_bytes=60 * 1024 * 1024
        ),
        name="scatter_grads",
    )(*segments, *pairs)
    return made[:n_seg], made[n_seg:]


def pad_rows(values, padded):
    return jnp.pad(values, ((0, 0), (0, padded - values.shape[1]), (0, 0)))


def chunk_list():
    return [(0, 0, 0, 128), (2, 0, 0, 256), (2, 1, 256, 256), (1, 0, 0, 768), (1, 1, 768, 768)] + [
        (segment, part % 2, part * 512, 512) for segment in (3, 4) for part in range(4)
    ]


def scatter_list():
    return [(segment, part % 2, part * 512, 512) for segment in (6, 5) for part in range(4)] + [
        (segment, part, part * 256, 256) for segment in (4, 1, 2, 3) for part in range(2)
    ] + [(0, 0, 0, 128)]


def on_device_paired(
    tokens, condition, scale_lengths, order, cotangent, ada_weight, ada_bias, qkv_weight, qv_bias,
    head_log_scale, proj_weight, out_bias, fc1_weight, fc1_bias, fc2_weight,
):
    n_dp, mine = lax.axis_size("dp"), lax.axis_index("mp")
    line = n_dp // 4
    slots, half_rows, model = tokens.shape
    padded = -(-half_rows // 16) * 16
    rows = 2 * padded
    local_heads, width = qv_bias.shape[1], 64
    own_cols = qkv_weight.shape[2]
    own_rows = qkv_weight.shape[1]
    hidden_cols = fc1_weight.shape[1]
    groups = 2 * own_cols // 256
    swap = order[0, 0] != 0

    def to_slots(values):
        return jnp.where(swap, values[::-1], values)

    scale_parts = split_three(head_log_scale)
    small = jnp.concatenate(
        [qv_bias.reshape(-1), out_bias.reshape(-1), fc1_bias.reshape(-1)] + list(scale_parts)
    )
    small = jnp.pad(small, (0, 16 * 128 - small.shape[0])).reshape(16, 128)
    segments = [
        small,
        jnp.concatenate([qkv_weight[0], qkv_weight[1], qkv_weight[2]], 1),
        proj_weight.T,
        fc1_weight,
        fc2_weight.T,
    ]
    full, pair = run_gather(
        chunk_list(), segments, [pad_rows(to_slots(tokens), padded), pad_rows(cotangent, padded)], line, 1
    )
    small_full = full[0].reshape(2, n_dp, 16 * 128)
    qkv, projt, fc1, fc2t = (f.reshape(2, model, f.shape[-1]) for f in full[1:])
    x, cot = (p.reshape(rows, model) for p in pair)
    entries = qv_bias.shape[2]
    vectors = (2 + 2) * local_heads + fc1_bias.shape[0]
    spread_small = small_full[:, :, : vectors * entries].reshape(2, n_dp, vectors, entries)
    spread_small = spread_small.transpose(0, 2, 1, 3).reshape(2, vectors, n_dp * entries).astype(F32)
    block_rows = spread_small[:, : 4 * local_heads].reshape(2, 4, own_cols).transpose(1, 0, 2).reshape(4, model)
    vecs = jnp.pad(block_rows, ((0, 4), (0, 0)))
    hidden_bias = jnp.broadcast_to(spread_small[:, 4 * local_heads :].reshape(1, 2 * hidden_cols), (8, 2 * hidden_cols))
    scale_at = vectors * entries
    scale_all = sum(
        small_full[:, 0, scale_at + i * local_heads : scale_at + (i + 1) * local_heads].astype(F32) for i in range(3)
    )
    boost = jnp.exp(scale_all.reshape(groups, -1))
    boosts = jnp.zeros((groups, 8, 128), F32).at[:, 0, : boost.shape[1]].set(boost)

    cond_slots = to_slots(condition).astype(F32)
    signal = jax.nn.silu(cond_slots).astype(BF16)
    signal_rows = lax.all_to_all(
        signal.reshape(slots, n_dp, own_rows).transpose(1, 0, 2), "dp", 0, 0, tiled=True
    ).reshape(n_dp * slots, own_rows)
    ada_flat = ada_weight.reshape(own_rows, 6 * own_cols)
    bias_own = lax.dynamic_update_slice(
        jnp.zeros((6, local_heads, width), F32), ada_bias.astype(F32), (0, 0, lax.axis_index("dp") * ada_bias.shape[2])
    )
    products = jnp.dot(signal_rows, ada_flat, preferred_element_type=F32) + bias_own.reshape(1, 6 * own_cols)
    arrived = lax.all_to_all(products, ("dp", "mp"), 0, 0, tiled=True)
    modulation = arrived.reshape(n_dp, 2, 6, own_cols).sum(0).transpose(1, 0, 2).reshape(6, model)
    mods = jnp.pad(modulation, ((0, 2), (0, 0)))

    lengths = lax.dynamic_index_in_dim(to_slots(scale_lengths), mine, 0, keepdims=False)
    kmask, qmask = build_masks(lengths, half_rows, padded)
    middle, attended, two, q_low, k_low, v_low, mixed, stats = run_forward(
        x, mods, qkv, projt, vecs, boosts, kmask, qmask, width
    )
    result, grad_middle, feed_rows, g_fc1, g_fc2t, g_hidden = run_feed(
        two, middle, cot, mods, vecs, fc1, fc2t, hidden_bias
    )
    token_grad, back_rows, g_q, g_k, g_v, g_projt, sums = run_backward(
        scale_lengths.shape[1], x, grad_middle, attended, mods, (q_low, k_low, v_low, mixed, stats), qkv, projt,
        boosts, kmask, qmask, width,
    )

    bias_grads = jnp.stack([sums[:, 0].reshape(model), sums[:, 1].reshape(model), back_rows[2], feed_rows[3]])
    bias_grads = bias_grads.reshape(4, 2, local_heads, n_dp, entries).transpose(1, 3, 0, 2, 4)
    hidden_grads = g_hidden[0].reshape(2, fc1_bias.shape[0], n_dp, entries).transpose(0, 2, 1, 3)
    scale_grads = jnp.broadcast_to(sums[:, 4:, 0].reshape(2, 1, local_heads), (2, n_dp, local_heads))
    small_grads = jnp.concatenate(
        [bias_grads.reshape(2, n_dp, -1), hidden_grads.reshape(2, n_dp, -1), scale_grads], 2
    ).astype(BF16)
    small_grads = jnp.pad(small_grads, ((0, 0), (0, 0), (0, 16 * 128 - small_grads.shape[2])))
    owned = [g.reshape(2, line, 2, 2, own_rows, g.shape[-1]) for g in (g_q, g_k, g_v, g_projt, g_fc1, g_fc2t)]
    totals, halves = run_scatter(
        scatter_list(), [small_grads.reshape(2, line, 2, 2, 16, 128)] + owned,
        [t.reshape(2, padded, model) for t in (result, token_grad)], line, 2,
    )
    small_total = totals[0].reshape(-1)
    bias_total = small_total[: 4 * local_heads * entries].reshape(2, 2, local_heads, entries)
    hidden_total = small_total[4 * local_heads * entries : scale_at].reshape(fc1_bias.shape)
    scale_total = small_total[scale_at : scale_at + local_heads]
    qkv_total = jnp.stack(totals[1:4])
    activations = halves[0][:, :half_rows]
    tokens_grad = to_slots(halves[1][:, :half_rows])

    grad_mods = jnp.stack(
        [back_rows[3], feed_rows[0], back_rows[0], feed_rows[1], back_rows[1], feed_rows[2]]
    ).reshape(6, 2, own_cols).transpose(1, 0, 2)
    both = lax.all_to_all(grad_mods, "mp", 0, 0, tiled=True)
    all_mods = lax.all_gather(both, "dp", axis=0, tiled=True).reshape(n_dp * slots, 6 * own_cols)
    ada_weight_grad = lax.dot_general(
        signal_rows.astype(F32), all_mods, (((0,), (0,)), ((), ())), precision=precise, preferred_element_type=F32
    ).reshape(ada_weight.shape)
    ada_bias_grad = lax.dynamic_slice_in_dim(
        jnp.sum(all_mods, 0).reshape(6, local_heads, width), lax.axis_index("dp") * entries, entries, 2
    )
    signal_part = lax.dot_general(
        all_mods, ada_flat.astype(F32), (((1,), (1,)), ((), ())), precision=precise, preferred_element_type=F32
    )
    signal_part = lax.psum(signal_part, "mp").reshape(n_dp, slots, own_rows)
    signal_grad = lax.all_to_all(signal_part, "dp", 0, 0, tiled=True).transpose(1, 0, 2).reshape(slots, model)
    pull = jax.vjp(jax.nn.silu, cond_slots)[1]
    condition_grad = to_slots(pull(signal_grad)[0]).astype(BF16)
    return (
        activations, tokens_grad, condition_grad, ada_weight_grad, ada_bias_grad, qkv_total, bias_total[0],
        scale_total, totals[4].T, bias_total[1], totals[5], hidden_total, totals[6].T,
    )


precise = lax.Precision.HIGHEST


def row_norm(values):
    centre = jnp.mean(values, -1, keepdims=True)
    shifted = values - centre
    inverse = lax.rsqrt(jnp.mean(shifted * shifted, -1, keepdims=True) + 1e-06)
    return (shifted * inverse, inverse)


def row_norm_back(incoming, normed, inverse):
    return inverse * (
        incoming
        - jnp.mean(incoming, -1, keepdims=True)
        - normed * jnp.mean(incoming * normed, -1, keepdims=True)
    )


def gelu_tanh(values):
    return jax.nn.gelu(values, approximate=True)


def spread(shard_rows):
    return lax.all_gather(shard_rows, "mp", axis=0, tiled=True)


def collect(partial_sum):
    return lax.psum_scatter(
        partial_sum.astype(jnp.bfloat16), "mp", scatter_dimension=0, tiled=True
    ).astype(jnp.float32)


def fetch(qkv_weight, qv_bias, proj_weight, out_bias, fc1_weight, fc1_bias, fc2_weight):
    return (
        lax.all_gather(qkv_weight, "dp", axis=1, tiled=True),
        lax.all_gather(qv_bias, "dp", axis=2, tiled=True),
        lax.all_gather(proj_weight, "dp", axis=1, tiled=True),
        lax.all_gather(out_bias, "dp", axis=2, tiled=True),
        lax.all_gather(fc1_weight, "dp", axis=0, tiled=True),
        lax.all_gather(fc1_bias, "dp", axis=1, tiled=True),
        lax.all_gather(fc2_weight, "dp", axis=1, tiled=True),
    )


def settle(grad_set):
    qkv_part, qv_part, proj_part, outb_part, fc1_part, fc1b_part, fc2_part = grad_set
    return (
        lax.psum_scatter(
            qkv_part.astype(jnp.bfloat16), "dp", scatter_dimension=1, tiled=True
        ).astype(jnp.float32),
        lax.psum_scatter(
            qv_part.astype(jnp.bfloat16), "dp", scatter_dimension=2, tiled=True
        ).astype(jnp.float32),
        lax.psum_scatter(
            proj_part.astype(jnp.bfloat16), "dp", scatter_dimension=1, tiled=True
        ).astype(jnp.float32),
        lax.psum_scatter(
            outb_part.astype(jnp.bfloat16), "dp", scatter_dimension=2, tiled=True
        ).astype(jnp.float32),
        lax.psum_scatter(
            fc1_part.astype(jnp.bfloat16), "dp", scatter_dimension=0, tiled=True
        ).astype(jnp.float32),
        lax.psum_scatter(
            fc1b_part.astype(jnp.bfloat16), "dp", scatter_dimension=1, tiled=True
        ).astype(jnp.float32),
        lax.psum_scatter(
            fc2_part.astype(jnp.bfloat16), "dp", scatter_dimension=1, tiled=True
        ).astype(jnp.float32),
    )


def on_device_shared(
    tokens,
    condition,
    scale_lengths,
    order,
    cotangent,
    ada_weight,
    ada_bias,
    qkv_weight,
    qv_bias,
    head_log_scale,
    proj_weight,
    out_bias,
    fc1_weight,
    fc1_bias,
    fc2_weight,
):
    image_count, shard_rows, model_width = tokens.shape
    column_count = qkv_weight.shape[2]
    local_heads = qv_bias.shape[1]
    head_width = column_count // local_heads
    hidden_cols = fc1_weight.shape[1]
    own_start = lax.axis_index("mp") * column_count
    token_count = shard_rows * lax.axis_size("mp")
    ada_full, ada_bias_full = (
        lax.all_gather(ada_weight, "dp", axis=0, tiled=True),
        lax.all_gather(ada_bias, "dp", axis=2, tiled=True),
    )
    cond_float = condition.astype(jnp.float32)
    signal = jax.nn.silu(cond_float).astype(jnp.bfloat16)
    ada_flat = ada_full.reshape(model_width, 6 * column_count)
    mod_share = jnp.dot(
        signal, ada_flat, preferred_element_type=jnp.float32
    ) + ada_bias_full.reshape(6 * column_count).astype(jnp.float32)
    modulation = lax.all_gather(
        mod_share.reshape(image_count, 6, column_count), "mp", axis=2, tiled=True
    )
    head_boost = jnp.exp(head_log_scale)[None, :, None]
    positions = jnp.arange(token_count, dtype=jnp.int32)

    def place(vector):
        return lax.dynamic_update_slice(
            jnp.zeros((model_width,), jnp.float32), vector, (own_start,)
        )

    def own_columns(matrix):
        return lax.dynamic_slice_in_dim(matrix, own_start, column_count, 1)

    def rows_now():
        return fetch(qkv_weight, qv_bias, proj_weight, out_bias, fc1_weight, fc1_bias, fc2_weight)

    full_shapes = (
        (3, model_width, column_count),
        (2, local_heads, head_width),
        (column_count, model_width),
        (2, local_heads, head_width),
        (model_width, hidden_cols),
        (hidden_cols // head_width, head_width),
        (hidden_cols, model_width),
    )
    grad_start = tuple((jnp.zeros(shape_item, jnp.float32) for shape_item in full_shapes))

    def micro_step(micro_at, state_now):
        outputs, token_grads, mod_grads, weight_grads, scale_grad = state_now
        image_at = order[0, micro_at]
        residual = lax.dynamic_index_in_dim(tokens, image_at, 0, keepdims=False).astype(jnp.float32)
        image_mods = lax.dynamic_index_in_dim(modulation, image_at, 0, keepdims=False)
        lengths = lax.dynamic_index_in_dim(scale_lengths, image_at, 0, keepdims=False)
        out_grad = lax.dynamic_index_in_dim(cotangent, micro_at, 0, keepdims=False).astype(
            jnp.float32
        )
        qkv_full, qv_full, proj_full, outb_full, fc1_full, fc1b_full, fc2_full = rows_now()
        steps = jnp.arange(lengths.shape[0], dtype=jnp.int32)
        scale_ends = jnp.sum(jnp.where(steps[None, :] <= steps[:, None], lengths[None, :], 0), 1)
        scale_of = jnp.sum((positions[:, None] >= scale_ends[None, :]).astype(jnp.int32), 1)
        allowed = (scale_of[None, :] <= scale_of[:, None])[None]
        normed_one, inverse_one = row_norm(residual)
        input_one = spread(
            (normed_one * (1.0 + image_mods[2]) + image_mods[4]).astype(jnp.bfloat16)
        )
        projected = jnp.einsum(
            "td,cde->cte", input_one, qkv_full, preferred_element_type=jnp.float32
        )
        bias_pair = qv_full.reshape(2, column_count).astype(jnp.float32)
        queries = (projected[0] + bias_pair[0]).reshape(token_count, local_heads, head_width)
        keys_raw = projected[1].reshape(token_count, local_heads, head_width)
        values_low = (
            (projected[2] + bias_pair[1])
            .astype(jnp.bfloat16)
            .reshape(token_count, local_heads, head_width)
        )
        query_inv = lax.rsqrt(jnp.sum(queries * queries, -1, keepdims=True) + 1e-06)
        key_inv = lax.rsqrt(jnp.sum(keys_raw * keys_raw, -1, keepdims=True) + 1e-06)
        query_unit = queries * query_inv
        key_unit = keys_raw * key_inv
        query_low = (query_unit * head_boost).astype(jnp.bfloat16)
        key_low = key_unit.astype(jnp.bfloat16)

        def masked_scores():
            raw_scores = jnp.einsum(
                "qhd,khd->hqk", query_low, key_low, preferred_element_type=jnp.float32
            )
            return jnp.where(allowed, raw_scores, -1e30)

        scores = masked_scores()
        row_peak = jnp.max(scores, -1, keepdims=True)
        exp_terms = jnp.exp(scores - row_peak)
        totals = jnp.sum(exp_terms, -1, keepdims=True)
        log_total = row_peak + jnp.log(totals)
        soft_weights = exp_terms / totals
        mixed_heads = (
            jnp.einsum(
                "hqk,khd->qhd",
                soft_weights.astype(jnp.bfloat16),
                values_low,
                preferred_element_type=jnp.float32,
            )
            .astype(jnp.bfloat16)
            .reshape(token_count, column_count)
        )
        attended = collect(
            jnp.dot(mixed_heads, proj_full, preferred_element_type=jnp.float32)
            + place(outb_full[0].reshape(column_count).astype(jnp.float32))
        )
        middle = residual + image_mods[0] * attended
        normed_two, inverse_two = row_norm(middle)
        input_two = spread(
            (normed_two * (1.0 + image_mods[3]) + image_mods[5]).astype(jnp.bfloat16)
        )
        hidden = jnp.dot(
            input_two, fc1_full, preferred_element_type=jnp.float32
        ) + fc1b_full.reshape(hidden_cols).astype(jnp.float32)
        activated = gelu_tanh(hidden).astype(jnp.bfloat16)
        branch_out = collect(
            jnp.dot(activated, fc2_full, preferred_element_type=jnp.float32)
            + place(outb_full[1].reshape(column_count).astype(jnp.float32))
        )
        result = (middle + image_mods[1] * branch_out).astype(jnp.bfloat16)
        outputs = lax.dynamic_update_index_in_dim(outputs, result, micro_at, 0)
        qkv_back, qv_back, proj_back, outb_back, fc1_back, fc1b_back, fc2_back = rows_now()
        grad_branch = spread((image_mods[1] * out_grad).astype(jnp.bfloat16))
        gamma_two_grad = jnp.sum(out_grad * branch_out, 0)
        fc2_grad = jnp.dot(activated.T, grad_branch, preferred_element_type=jnp.float32)
        bias_two_grad = jnp.sum(own_columns(grad_branch).astype(jnp.float32), 0)
        act_grad = jnp.dot(grad_branch, fc2_back.T, preferred_element_type=jnp.float32)
        gelu_pull = jax.vjp(gelu_tanh, hidden)[1]
        hidden_grad = gelu_pull(act_grad)[0].astype(jnp.bfloat16)
        fc1_grad = jnp.dot(input_two.T, hidden_grad, preferred_element_type=jnp.float32)
        fc1b_grad = jnp.sum(hidden_grad.astype(jnp.float32), 0).reshape(
            hidden_cols // head_width, head_width
        )
        input_two_grad = collect(
            jnp.dot(hidden_grad, fc1_back.T, preferred_element_type=jnp.float32)
        )
        scale_two_grad = jnp.sum(input_two_grad * normed_two, 0)
        shift_two_grad = jnp.sum(input_two_grad, 0)
        middle_grad = out_grad + row_norm_back(
            input_two_grad * (1.0 + image_mods[3]), normed_two, inverse_two
        )
        grad_attended = spread((image_mods[0] * middle_grad).astype(jnp.bfloat16))
        gamma_one_grad = jnp.sum(middle_grad * attended, 0)
        proj_grad = jnp.dot(mixed_heads.T, grad_attended, preferred_element_type=jnp.float32)
        bias_one_grad = jnp.sum(own_columns(grad_attended).astype(jnp.float32), 0)
        mixed_grad = (
            jnp.dot(grad_attended, proj_back.T, preferred_element_type=jnp.float32)
            .astype(jnp.bfloat16)
            .reshape(token_count, local_heads, head_width)
        )
        soft_again = jnp.exp(masked_scores() - log_total)
        value_grad = jnp.einsum(
            "hqk,qhd->khd",
            soft_again.astype(jnp.bfloat16),
            mixed_grad,
            preferred_element_type=jnp.float32,
        )
        soft_grad = jnp.einsum(
            "qhd,khd->hqk", mixed_grad, values_low, preferred_element_type=jnp.float32
        )
        score_grad = (
            soft_again * (soft_grad - jnp.sum(soft_again * soft_grad, -1, keepdims=True))
        ).astype(jnp.bfloat16)
        query_low_grad = jnp.einsum(
            "hqk,khd->qhd", score_grad, key_low, preferred_element_type=jnp.float32
        )
        key_low_grad = jnp.einsum(
            "hqk,qhd->khd", score_grad, query_low, preferred_element_type=jnp.float32
        )
        head_grad = jnp.sum(query_low_grad * query_unit * head_boost, (0, 2))
        query_unit_grad = query_low_grad * head_boost
        query_grad = query_inv * (
            query_unit_grad - query_unit * jnp.sum(query_unit_grad * query_unit, -1, keepdims=True)
        )
        key_grad = key_inv * (
            key_low_grad - key_unit * jnp.sum(key_low_grad * key_unit, -1, keepdims=True)
        )
        triple_grad = jnp.stack(
            [
                query_grad.reshape(token_count, column_count),
                key_grad.reshape(token_count, column_count),
                value_grad.reshape(token_count, column_count),
            ]
        ).astype(jnp.bfloat16)
        qkv_grad = jnp.einsum(
            "td,cte->cde", input_one, triple_grad, preferred_element_type=jnp.float32
        )
        pair_sums = jnp.sum(triple_grad.astype(jnp.float32), 1)
        qv_grad = jnp.stack([pair_sums[0], pair_sums[2]]).reshape(2, local_heads, head_width)
        input_one_grad = collect(
            jnp.einsum("cte,cde->td", triple_grad, qkv_back, preferred_element_type=jnp.float32)
        )
        scale_one_grad = jnp.sum(input_one_grad * normed_one, 0)
        shift_one_grad = jnp.sum(input_one_grad, 0)
        residual_grad = middle_grad + row_norm_back(
            input_one_grad * (1.0 + image_mods[2]), normed_one, inverse_one
        )
        token_grads = lax.dynamic_update_index_in_dim(
            token_grads, residual_grad.astype(jnp.bfloat16), image_at, 0
        )
        image_mod_grad = jnp.stack(
            [
                gamma_one_grad,
                gamma_two_grad,
                scale_one_grad,
                scale_two_grad,
                shift_one_grad,
                shift_two_grad,
            ]
        )
        mod_grads = lax.dynamic_update_index_in_dim(mod_grads, image_mod_grad, image_at, 0)
        outb_grad = jnp.stack([bias_one_grad, bias_two_grad]).reshape(2, local_heads, head_width)
        local_grads = (qkv_grad, qv_grad, proj_grad, outb_grad, fc1_grad, fc1b_grad, fc2_grad)
        weight_grads = tuple(
            (running + addend for running, addend in zip(weight_grads, local_grads))
        )
        return (outputs, token_grads, mod_grads, weight_grads, scale_grad + head_grad)

    start_state = (
        jnp.zeros(tokens.shape, jnp.bfloat16),
        jnp.zeros(tokens.shape, jnp.bfloat16),
        jnp.zeros((image_count, 6, model_width), jnp.float32),
        grad_start,
        jnp.zeros((local_heads,), jnp.float32),
    )
    outputs, token_grads, mod_grads, weight_grads, scale_grad = lax.fori_loop(
        0, image_count, micro_step, start_state
    )
    shard_grads = settle(weight_grads)
    mod_share_grad = lax.psum_scatter(
        mod_grads.astype(jnp.bfloat16), "mp", scatter_dimension=2, tiled=True
    ).astype(jnp.float32)
    flat_grad = mod_share_grad.reshape(image_count, 6 * column_count)
    ada_grad = jnp.dot(
        signal.astype(jnp.float32).T,
        flat_grad,
        precision=precise,
        preferred_element_type=jnp.float32,
    ).reshape(model_width, 6, column_count)
    ada_bias_grad = jnp.sum(mod_share_grad, 0).reshape(6, local_heads, head_width)
    signal_grad = lax.psum(
        jnp.dot(
            flat_grad,
            ada_flat.astype(jnp.float32).T,
            precision=precise,
            preferred_element_type=jnp.float32,
        ),
        "mp",
    )
    silu_pull = jax.vjp(jax.nn.silu, cond_float)[1]
    condition_grad = silu_pull(signal_grad)[0].astype(jnp.bfloat16)
    ada_shard, ada_bias_shard = (
        lax.psum_scatter(
            ada_grad.astype(jnp.bfloat16), "dp", scatter_dimension=0, tiled=True
        ).astype(jnp.float32),
        lax.psum_scatter(
            ada_bias_grad.astype(jnp.bfloat16), "dp", scatter_dimension=2, tiled=True
        ).astype(jnp.float32),
    )
    head_scale_grad = lax.psum(scale_grad, "dp")
    qkv_shard, qv_shard, proj_shard, outb_shard, fc1_shard, fc1b_shard, fc2_shard = shard_grads
    return (
        outputs,
        token_grads,
        condition_grad,
        ada_shard,
        ada_bias_shard,
        qkv_shard,
        qv_shard,
        head_scale_grad,
        proj_shard,
        outb_shard,
        fc1_shard,
        fc1b_shard,
        fc2_shard,
    )


def solution(mesh):
    in_specs = (
        P("dp", "mp", None),
        P("dp", None),
        P("dp", None),
        P("dp", None),
        P("dp", "mp", None),
        P("dp", None, "mp"),
        P(None, "mp", "dp"),
        P(None, "dp", "mp"),
        P(None, "mp", "dp"),
        P("mp"),
        P("mp", "dp"),
        P(None, "mp", "dp"),
        P("dp", "mp"),
        P("mp", "dp"),
        P("mp", "dp"),
    )
    out_specs = (
        P("dp", "mp", None),
        P("dp", "mp", None),
        P("dp", None),
        P("dp", None, "mp"),
        P(None, "mp", "dp"),
        P(None, "dp", "mp"),
        P(None, "mp", "dp"),
        P("mp"),
        P("mp", "dp"),
        P(None, "mp", "dp"),
        P("dp", "mp"),
        P("mp", "dp"),
        P("mp", "dp"),
    )
    line, spare = divmod(mesh.shape["dp"], 4)
    paired = mesh.shape["mp"] == 2 and spare == 0 and line > 1
    return jax.shard_map(
        on_device_paired if paired else on_device_shared, mesh=mesh, in_specs=in_specs, out_specs=out_specs, check_vma=False
    )
```

```python
import functools
import jax
import jax.numpy as jnp
from jax import lax
from jax.experimental import pallas as pl
from jax.experimental.pallas import tpu as pltpu
from jax.sharding import PartitionSpec as P

F32 = jnp.float32
BF16 = jnp.bfloat16
MESH = pl.DeviceIdType.MESH
LOG2E = 1.4426950408889634
VMEM_LIMIT = 60 * 1024 * 1024


def mm(a, b):
    return jnp.dot(a, b, preferred_element_type=F32)


def mm_nt(a, b):
    return lax.dot_general(a, b, (((1,), (1,)), ((), ())), preferred_element_type=F32)


def mm_tn(a, b):
    return lax.dot_general(a, b, (((0,), (0,)), ((), ())), preferred_element_type=F32)


def norm_rows(values):
    centre = jnp.mean(values, -1, keepdims=True)
    shifted = values - centre
    inverse = lax.rsqrt(jnp.mean(shifted * shifted, -1, keepdims=True) + 1e-06)
    return shifted * inverse, inverse


def norm_rows_back(incoming, normed, inverse):
    return inverse * (
        incoming
        - jnp.mean(incoming, -1, keepdims=True)
        - normed * jnp.mean(incoming * normed, -1, keepdims=True)
    )


def split_three(values):
    high = values.astype(BF16)
    rest = values - high.astype(F32)
    middle = rest.astype(BF16)
    return high, middle, (rest - middle.astype(F32)).astype(BF16)


def build_masks(lengths, half_rows, padded):
    count = lengths.shape[0]
    steps = jnp.arange(count, dtype=jnp.int32)
    ends = jnp.sum(jnp.where(steps[None, :] <= steps[:, None], lengths[None, :], 0), 1)
    place = jnp.arange(2 * padded, dtype=jnp.int32)
    part, inside = place // padded, place % padded
    token = part * half_rows + inside
    level = jnp.sum((token[None, :] >= ends[:, None]).astype(jnp.int32), 0)
    real = inside < half_rows
    entry = jnp.arange(16, dtype=jnp.int32)[:, None]
    key_level = jnp.where(real, level, count)[None]
    kmask = (entry == key_level) | ((entry > count) & (entry < count + 4))
    query_level = jnp.where(real, level, count - 1)[None]
    qmask = (entry > query_level) & (entry <= count)
    return kmask.astype(BF16), jnp.where(qmask, -32768.0, 0.0).astype(BF16)


def device(z, x, c, y):
    return (z * 4 + x * 2 + c, y)


def where_am_i():
    dp, y = lax.axis_index("dp"), lax.axis_index("mp")
    return dp // 4, (dp // 2) % 2, dp % 2, y


def remote(source, target, send, recv, to):
    return pltpu.make_async_remote_copy(source, target, send, recv, device_id=to, device_id_type=MESH)


def greet_all(total):
    me = lax.axis_index("dp") * 2 + lax.axis_index("mp")
    barrier = pltpu.get_barrier_semaphore()

    def signal(step, carry):
        to = lax.rem(me + step, total)
        pl.semaphore_signal(barrier, inc=1, device_id=(to // 2, to % 2), device_id_type=MESH)
        return carry

    lax.fori_loop(1, total, signal, 0)
    pl.semaphore_wait(barrier, total - 1)


class Exchange:
    def __init__(self, total, block_of, landing, send, recv):
        self.total, self.block_of, self.landing, self.send, self.recv = total, block_of, landing, send, recv
        self.me = lax.axis_index("dp") * 2 + lax.axis_index("mp")

    def copy(self, step):
        to = lax.rem(self.me + step, self.total)
        return remote(
            self.block_of(to), self.landing.at[self.me], self.send.at[step], self.recv.at[step], (to // 2, to % 2)
        )

    def own(self):
        return pltpu.make_async_copy(self.block_of(self.me), self.landing.at[self.me], self.send.at[0])

    def each(self, act):
        def body(step, carry):
            act(self.copy(step))
            return carry

        lax.fori_loop(1, self.total, body, 0)

    def start(self):
        self.own().start()
        self.each(lambda copy: copy.start())

    def wait(self):
        self.own().wait()
        self.each(lambda copy: copy.wait())


class Ticks:
    def __init__(self, count, stages):
        self.count, self.stages = count, stages
        self.total = count + len(stages) - 1

    def run(self, since, until):
        for tick in range(since, until):
            for at, stage in enumerate(self.stages):
                if 0 <= tick - at < self.count:
                    stage(tick - at)


class Gather:
    def __init__(self, chunks, line, outs, z_send, z_recv, send_sem, recv_sem):
        self.chunks, self.line, self.outs = chunks, line, outs
        self.z_send, self.z_recv, self.send_sem, self.recv_sem = z_send, z_recv, send_sem, recv_sem
        self.z, self.x, self.c, self.y = where_am_i()
        z, x, c, y = self.z, self.x, self.c, self.y
        self.x_side, self.y_side, self.sibling = device(z, 1 - x, c, y), device(z, x, c, 1 - y), device(z, x, 1 - c, y)

    def hop(self, k, way, j):
        seg, _, start, cols = self.chunks[k]
        z, x, c, y, line = self.z, self.x, self.c, self.y, self.line
        step = 1 - 2 * way
        going, coming = z - step * j, z - step * (j + 1)
        sends = (going >= 0) & (going < line) & (z + step >= 0) & (z + step < line)
        receives = (coming >= 0) & (coming < line)

        def copy(owner):
            ref = self.outs[seg].at[y, owner, x, c, :, pl.ds(start, cols)]
            return remote(ref, ref, self.z_send.at[k, way, j], self.z_recv.at[k, way, j], device(z + step, x, c, y))

        return sends, (lambda: copy(going)), receives, (lambda: copy(coming))

    def group(self, k, slot, at, target):
        seg, _, start, cols = self.chunks[k]
        ref = self.outs[seg].at[at[0], :, at[1], self.c, :, pl.ds(start, cols)]
        return remote(ref, ref, self.send_sem.at[k, slot], self.recv_sem.at[k, slot], target)

    def groups(self, k):
        x, y = self.x, self.y
        if self.chunks[k][1] == 0:
            return [(y, x), (y, 1 - x), (1 - y, x), (1 - y, 1 - x)], self.x_side, self.y_side
        return [(y, x), (1 - y, x), (y, 1 - x), (1 - y, 1 - x)], self.y_side, self.x_side

    def line_stage(self, j):
        def stage(k):
            for way in range(2):
                if j > 0:
                    _, _, receives, landed = self.hop(k, way, j - 1)

                    @pl.when(receives)
                    def _():
                        landed().wait_recv()

                if j < self.line - 1:
                    sends, copy, _, _ = self.hop(k, way, j)

                    @pl.when(sends)
                    def _():
                        copy().start()

        return stage

    def first_stage(self, k):
        self.line_stage(self.line - 1)(k)
        order, first, second = self.groups(k)
        self.group(k, 0, order[0], first).start()
        self.group(k, 1, order[0], second).start()
        self.group(k, 3, order[0], self.sibling).start()

    def second_stage(self, k):
        order, first, second = self.groups(k)
        self.group(k, 0, order[1], first).wait_recv()
        self.group(k, 2, order[1], second).start()
        self.group(k, 4, order[1], self.sibling).start()

    def last_stage(self, k):
        order, first, second = self.groups(k)
        self.group(k, 1, order[2], second).wait_recv()
        self.group(k, 5, order[2], self.sibling).start()
        self.group(k, 2, order[3], second).wait_recv()
        self.group(k, 6, order[3], self.sibling).start()

    def stages(self):
        return [self.line_stage(j) for j in range(self.line - 1)] + [self.first_stage, self.second_stage, self.last_stage]

    def finish(self, k):
        order, _, _ = self.groups(k)
        for slot, at in ((3, 0), (4, 1), (5, 2), (6, 3)):
            self.group(k, slot, order[at], self.sibling).wait_recv()

    def sent(self):
        for k in range(len(self.chunks)):
            order, _, _ = self.groups(k)
            for way in range(2):
                for j in range(self.line - 1):
                    sends, copy, _, _ = self.hop(k, way, j)

                    @pl.when(sends)
                    def _():
                        copy().wait_send()

            for slot, at in ((0, 0), (1, 0), (2, 1), (3, 0), (4, 1), (5, 2), (6, 3)):
                self.group(k, slot, order[at], self.sibling).wait_send()


def add_into(target, source, pieces, target_at, source_at):
    def body(i, carry):
        t, s = target_at(i), source_at(i)
        target[t] = target[t] + source[s]
        return carry

    lax.fori_loop(0, pieces, body, 0)


class Scatter:
    def __init__(self, chunks, line, sources, totals, landing, core_s, own_s, first_b, second_b, line_b, sems):
        self.chunks, self.line, self.sources, self.totals = chunks, line, sources, totals
        self.landing, self.core_s, self.own_s = landing, core_s, own_s
        self.first_b, self.second_b, self.line_b = first_b, second_b, line_b
        self.own_sem, self.load_sem, self.send_sem, self.recv_sem, self.z_send, self.z_recv = sems
        self.z, self.x, self.c, self.y = where_am_i()
        z, x, c, y = self.z, self.x, self.c, self.y
        self.x_side, self.y_side, self.sibling = device(z, 1 - x, c, y), device(z, x, c, 1 - y), device(z, x, 1 - c, y)

    def core_copy(self, k):
        seg, _, start, cols = self.chunks[k]
        source = self.sources[seg].at[:, :, :, 1 - self.c, :, pl.ds(start, cols)]
        return remote(source, self.landing[k], self.send_sem.at[k, 0], self.recv_sem.at[k, 0], self.sibling)

    def core(self, k):
        return self.core_s.at[k % 3, :, :, :, :, pl.ds(0, self.chunks[k][3])]

    def own(self, k):
        return self.own_s.at[k % 2, :, :, :, :, pl.ds(0, self.chunks[k][3])]

    def own_copy(self, k):
        seg, _, start, cols = self.chunks[k]
        source = self.sources[seg].at[:, :, :, self.c, :, pl.ds(start, cols)]
        return pltpu.make_async_copy(source, self.own(k), self.own_sem.at[k])

    def load_copy(self, k):
        return pltpu.make_async_copy(self.landing[k], self.core(k), self.load_sem.at[k])

    def first_copy(self, k):
        core, sems = self.core(k), (self.send_sem.at[k, 1], self.recv_sem.at[k, 1])
        if self.chunks[k][1] == 0:
            return remote(core.at[1 - self.y], self.first_b[k], *sems, self.y_side)
        return remote(core.at[:, :, 1 - self.x], self.first_b[k], *sems, self.x_side)

    def second_copy(self, k):
        first, sems = self.first_b[k], (self.send_sem.at[k, 2], self.recv_sem.at[k, 2])
        if self.chunks[k][1] == 0:
            return remote(first.at[:, 1 - self.x], self.second_b[k], *sems, self.x_side)
        return remote(first.at[1 - self.y], self.second_b[k], *sems, self.y_side)

    def line_copy(self, k, way, owner):
        to = device(self.z + 1 - 2 * way, self.x, self.c, self.y)
        return remote(
            self.second_b[k].at[owner], self.line_b[k].at[owner + 1 - way],
            self.z_send.at[k, way, owner], self.z_recv.at[k, way, owner], to,
        )

    def core_stage(self, k):
        self.core_copy(k).start()

    def load_stage(self, k):
        self.core_copy(k).wait_recv()
        self.load_copy(k).start()
        self.own_copy(k).start()

    def first_stage(self, k):
        line = self.line
        self.load_copy(k).wait()
        self.own_copy(k).wait()
        at = lambda i: (i // (2 * line), (i // 2) % line, i % 2)
        add_into(self.core(k), self.own(k), 4 * line, at, at)
        self.first_copy(k).start()

    def second_stage(self, k):
        line, x, y = self.line, self.x, self.y
        self.first_copy(k).wait_recv()
        if self.chunks[k][1] == 0:
            add_into(self.first_b[k], self.core(k), 2 * line, lambda i: (i // 2, i % 2), lambda i: (y, i // 2, i % 2))
        else:
            add_into(
                self.first_b[k], self.core(k), 2 * line,
                lambda i: (i // line, i % line), lambda i: (i // line, i % line, x),
            )
        self.second_copy(k).start()
        self.first_copy(k).wait_send()

    def third_stage(self, k):
        x, y = self.x, self.y
        self.second_copy(k).wait_recv()
        if self.chunks[k][1] == 0:
            add_into(self.second_b[k], self.first_b[k], self.line, lambda i: (i,), lambda i: (i, x))
        else:
            add_into(self.second_b[k], self.first_b[k], self.line, lambda i: (i,), lambda i: (y, i))

    def line_stage(self, j):
        def stage(k):
            if j == 0:
                self.third_stage(k)
            for way in range(2):
                place = j if way == 0 else self.line - 1 - j
                owners = range(self.line - 1, place, -1) if way == 0 else range(place)

                @pl.when(self.z == place)
                def _():
                    for owner in owners:
                        if j > 0:
                            self.line_copy(k, way, owner).wait_recv()
                            self.second_b[k][owner] = self.second_b[k][owner] + self.line_b[k][owner + 1 - way]
                        self.line_copy(k, way, owner).start()

        return stage

    def last_stage(self, k):
        seg, _, start, cols = self.chunks[k]
        z = self.z
        total = self.totals[seg]
        total[:, pl.ds(start, cols)] = self.second_b[k][z].astype(F32)
        for way in range(2):

            @pl.when((z > 0) if way == 0 else (z < self.line - 1))
            def _():
                self.line_copy(k, way, z).wait_recv()
                total[:, pl.ds(start, cols)] += self.line_b[k][z + 1 - way].astype(F32)

    def stages(self):
        return (
            [self.core_stage, self.load_stage, self.first_stage, self.second_stage]
            + [self.line_stage(j) for j in range(self.line - 1)]
            + [self.last_stage]
        )

    def sent(self):
        for k in range(len(self.chunks)):
            self.core_copy(k).wait_send()
            self.second_copy(k).wait_send()
            for way in range(2):
                for owner in range(self.line):

                    @pl.when((self.z < owner) if way == 0 else (self.z > owner))
                    def _():
                        self.line_copy(k, way, owner).wait_send()


def switch_on(index, cases):
    for at, act in cases.items():
        pl.when(index == at)(act)


def columns(start, size):
    return pl.ds(pl.multiple_of(start, 128), size)


def ahead_kernel(chunks, line, width, *refs):
    (products, seg_qkv, seg_proj, seg_fc1, seg_fc2, tok, cot, vecs, hidden_bias, boosts, kmask_ref, qmask_ref,
     qkv_f, proj_f, fc1_f, fc2_f, x_f, cot_f, g1_f, g2_f,
     mod_ref, ql_ref, kl_ref, vl_ref, mix_ref, stat_ref, out_ref, gmid_ref, rows_ref, gb1_ref,
     arrived, att_ref, x_s, cot_s, one_s, acc_s, mid_s, twot_s, back_s, backt_s, gacc_s, w_s, grad_s,
     a_send, a_recv, local_sem, pair_sem, z_send, z_recv, send_sem, recv_sem, load_sem, w_sem, grad_sem) = refs
    z, x, c, y = where_am_i()
    total = 8 * line
    padded, model = tok.shape[1], tok.shape[2]
    half_cols = mod_ref.shape[1] // 2
    heads = 256 // width
    outs = [qkv_f, proj_f, fc1_f, fc2_f]
    own = [
        pltpu.make_async_copy(i, o.at[y, z, x, c], local_sem.at[s])
        for s, (i, o) in enumerate(zip([seg_qkv, seg_proj, seg_fc1, seg_fc2], outs))
    ]
    for copy in own:
        copy.start()
    mine, others = pl.ds(y * padded, padded), pl.ds((1 - y) * padded, padded)
    pairs = []
    for p, (source, target, inside) in enumerate(((tok, x_f, x_s), (cot, cot_f, cot_s))):
        partner = device(z, x, c, 1 - y)
        pairs.append((
            pltpu.make_async_copy(source.at[y], target.at[mine], pair_sem.at[p, 0]),
            remote(source.at[1 - y], target.at[mine], pair_sem.at[p, 1], pair_sem.at[p, 2], partner),
            pltpu.make_async_copy(target, inside, pair_sem.at[p, 3]),
        ))
    exchange = Exchange(total, lambda to: products.at[to], arrived, a_send, a_recv)
    gather = Gather(chunks, line, outs, z_send, z_recv, send_sem, recv_sem)
    ticks = Ticks(len(chunks), gather.stages())
    greet_all(total)
    exchange.start()
    for copy in pairs[0][:2]:
        copy.start()
    for copy in own:
        copy.wait()

    def load_attend(i):
        half, sub, slot = i % 2, i // 2, i % 2
        return [
            pltpu.make_async_copy(
                qkv_f.at[half, :, :, :, :, pl.ds(sub * 768, 768)], w_s.at[slot, :, :, :, :, pl.ds(0, 768)],
                w_sem.at[slot, 0],
            ),
            pltpu.make_async_copy(
                proj_f.at[half, :, :, :, :, pl.ds(sub * 256, 256)], w_s.at[slot, :, :, :, :, pl.ds(768, 256)],
                w_sem.at[slot, 1],
            ),
        ]

    def load_feed(half, part):
        return [
            pltpu.make_async_copy(
                ref.at[half, :, :, :, :, columns(part * 512, 512)],
                w_s.at[half, :, :, :, :, pl.ds(at * 512, 512)], w_sem.at[half, at],
            )
            for at, ref in enumerate((fc1_f, fc2_f))
        ]

    def start_loads(copies):
        for copy in copies:
            copy.start()

    def wait_loads(copies):
        for copy in copies:
            copy.wait()

    ticks.run(0, 2)
    exchange.wait()
    parts = jnp.sum(arrived[...].reshape(total // 2, 2, 8, half_cols), 0)
    mod_ref[:, :half_cols] = parts[0]
    mod_ref[:, half_cols:] = parts[1]
    ticks.run(2, 4)
    wait_loads(pairs[0][:2])
    pairs[0][2].start()
    start_loads(pairs[1][:2])
    pairs[0][2].wait()
    ticks.run(4, 5)
    normed, _ = norm_rows(x_s[...].astype(F32))
    one_s[...] = (normed * (1.0 + mod_ref[2:3]) + mod_ref[4:5]).astype(BF16)
    acc_s[...] = jnp.zeros_like(acc_s)
    ticks.run(5, 7)
    gather.finish(0)
    gather.finish(1)
    start_loads(load_attend(0))
    start_loads(load_attend(1))
    ones = jnp.ones((x_s.shape[0], width), BF16)

    def attend(i, carry):
        def before_third():
            ticks.run(8, 9)
            gather.finish(2)
            gather.finish(3)
            start_loads(load_attend(2))
            start_loads(load_attend(3))

        switch_on(i, {1: lambda: ticks.run(7, 8), 2: before_third, 3: lambda: ticks.run(9, 10)})
        slot = lax.rem(i, 2)
        at = slot * 2 + i // 2
        wait_loads([
            pltpu.make_async_copy(
                qkv_f.at[0, :, :, :, :, pl.ds(0, 768)], w_s.at[slot, :, :, :, :, pl.ds(0, 768)], w_sem.at[slot, 0]
            ),
            pltpu.make_async_copy(
                proj_f.at[0, :, :, :, :, pl.ds(0, 256)], w_s.at[slot, :, :, :, :, pl.ds(768, 256)], w_sem.at[slot, 1]
            ),
        ])
        cols = columns(at * 256, 256)
        turned = pl.ds(pl.multiple_of(at * 256, 256), 256)
        weights = w_s[slot].reshape(model, 1024)
        projected = mm(one_s[...], weights[:, :768])
        queries = projected[:, :256] + vecs[0:1, cols]
        keys = projected[:, 256:512]
        values = (projected[:, 512:] + vecs[1:2, cols]).astype(BF16)
        vl_ref[:, cols] = values
        q_turned, k_turned = queries.T, keys.T
        boost = boosts[at]
        kmask, qmask = kmask_ref[...], qmask_ref[...]
        q_low, k_low, mixed, q_inv, k_inv, totals = [], [], [], [], [], []
        for head in range(heads):
            part = slice(head * width, (head + 1) * width)
            q_now, k_now = q_turned[part], k_turned[part]
            q_scale = lax.rsqrt(jnp.sum(q_now * q_now, 0, keepdims=True) + 1e-06)
            k_scale = lax.rsqrt(jnp.sum(k_now * k_now, 0, keepdims=True) + 1e-06)
            q_bf = (q_now * q_scale * boost[0:1, head : head + 1]).astype(BF16)
            k_bf = (k_now * k_scale).astype(BF16)
            scaled = q_bf.astype(F32) * LOG2E
            high = scaled.astype(BF16)
            rest = (scaled - high.astype(F32)).astype(BF16)
            q_all = jnp.concatenate([high, rest, qmask], 0)
            k_all = jnp.concatenate([k_bf, k_bf, kmask], 0)
            soft = jnp.exp2(mm_tn(q_all, k_all)).astype(BF16)
            summed = mm(soft, jnp.concatenate([values[:, part], ones], 1))
            total_now = summed[:, width:]
            mixed.append((summed[:, :width] / total_now).astype(BF16))
            totals.append(total_now[:, 0:1])
            q_low.append(q_bf)
            k_low.append(k_bf)
            q_inv.append(q_scale)
            k_inv.append(k_scale)
        mixed_all = jnp.concatenate(mixed, 1)
        mix_ref[:, cols] = mixed_all
        ql_ref[turned, :] = jnp.concatenate(q_low, 0)
        kl_ref[turned, :] = jnp.concatenate(k_low, 0)
        stat_ref[at, 0] = jnp.concatenate(q_inv + k_inv, 0)
        stat_ref[at, 1] = jnp.log2(jnp.concatenate(totals + totals, 1)).T
        acc_s[...] += mm_nt(mixed_all, weights[:, 768:])
        return carry

    lax.fori_loop(0, 4, attend, 0)
    ticks.run(10, 11)
    wait_loads(pairs[1][:2])
    pairs[1][2].start()
    attended = acc_s[...] + vecs[2:3]
    att_ref[...] = attended.astype(BF16)
    middle = x_s[...].astype(F32) + mod_ref[0:1] * attended
    mid_s[...] = middle
    normed, _ = norm_rows(middle)
    two = (normed * (1.0 + mod_ref[3:4]) + mod_ref[5:6]).astype(BF16)
    one_s[...] = two
    twot_s[...] = two.T
    pairs[1][2].wait()
    back = (mod_ref[1:2] * cot_s[...].astype(F32)).astype(BF16)
    back_s[...] = back
    backt_s[...] = back.T
    acc_s[...] = jnp.zeros_like(acc_s)
    gacc_s[...] = jnp.zeros_like(gacc_s)

    def store_feed(half, part):
        return [
            pltpu.make_async_copy(
                grad_s.at[half, at], ref.at[half, :, :, :, :, columns(part * 512, 512)], grad_sem.at[half, at]
            )
            for at, ref in enumerate((g1_f, g2_f))
        ]

    def feed(i, carry):
        half, part = lax.rem(i, 2), i // 2

        def before(p):
            def act():
                if p > 0:
                    ticks.run(10 + 2 * p, 11 + 2 * p)
                gather.finish(4 + 2 * p)
                gather.finish(5 + 2 * p)
                start_loads(load_feed(0, p))
                start_loads(load_feed(1, p))

            return act

        cases = {2 * p: before(p) for p in range(4)}
        cases.update({2 * p + 1: (lambda p=p: ticks.run(11 + 2 * p, 12 + 2 * p)) for p in range(3)})
        switch_on(i, cases)
        wait_loads(load_feed(half, part))
        weights = w_s[half].reshape(model, 1024)
        w1, w2 = weights[:, :512], weights[:, 512:]
        spot = columns(half * (hidden_bias.shape[1] // 2) + part * 512, 512)
        hidden = mm(one_s[...], w1) + hidden_bias[0:1, spot]
        square = hidden * hidden
        curve = jnp.tanh(0.7978845608028654 * hidden * (1.0 + 0.044715 * square))
        level = 0.5 * (1.0 + curve)
        activated = (hidden * level).astype(BF16)
        slope = level + 0.5 * hidden * (1.0 - curve * curve) * (
            0.7978845608028654 * (1.0 + 0.134145 * square)
        )
        acc_s[...] += mm_nt(activated, w2)

        @pl.when(i >= 2)
        def _():
            wait_loads(store_feed(half, part))

        grad_s[half, 1] = mm(backt_s[...], activated).astype(BF16).reshape(grad_s.shape[2:])
        hidden_grad = (mm(back_s[...], w2) * slope).astype(BF16)
        grad_s[half, 0] = mm(twot_s[...], hidden_grad).astype(BF16).reshape(grad_s.shape[2:])
        start_loads(store_feed(half, part))
        gb1_ref[0:1, spot] = jnp.sum(hidden_grad.astype(F32), 0, keepdims=True)
        gacc_s[...] += mm_nt(hidden_grad, w1)
        return carry

    lax.fori_loop(0, 8, feed, 0)
    middle = mid_s[...]
    out_grad = cot_s[...].astype(F32)
    branch = acc_s[...] + vecs[3:4]
    out_ref[...] = (middle + mod_ref[1:2] * branch).astype(BF16)
    normed, inverse = norm_rows(middle)
    grad = gacc_s[...]
    middle_grad = out_grad + norm_rows_back(grad * (1.0 + mod_ref[3:4]), normed, inverse)
    gmid_ref[...] = middle_grad
    rows_ref[0:1] = jnp.sum(out_grad * branch, 0, keepdims=True)
    rows_ref[1:2] = jnp.sum(grad * normed, 0, keepdims=True)
    rows_ref[2:3] = jnp.sum(grad, 0, keepdims=True)
    rows_ref[3:4] = jnp.sum(back_s[...].astype(F32), 0, keepdims=True)
    rows_ref[4:5] = jnp.sum(middle_grad * att_ref[...].astype(F32), 0, keepdims=True)
    rows_ref[5:8] = jnp.zeros((3, model), F32)
    gb1_ref[1:8] = jnp.zeros((7, gb1_ref.shape[1]), F32)
    for half in range(2):
        wait_loads(store_feed(half, 3))
    gather.sent()


def run_ahead(chunks, line, products, segments, tok, cot, vecs, hidden_bias, boosts, kmask, qmask, width, cid):
    padded, model = tok.shape[1:]
    rows = 2 * padded
    total, count = 8 * line, len(chunks)
    own_rows = segments[0].shape[0]
    hidden_cols = hidden_bias.shape[1]
    anywhere, inside = pl.BlockSpec(memory_space=pl.ANY), pl.BlockSpec(memory_space=pltpu.VMEM)
    full = [jax.ShapeDtypeStruct((2, line, 2, 2) + s.shape, BF16) for s in segments]
    flat = jax.ShapeDtypeStruct((rows, model), BF16)
    turned = jax.ShapeDtypeStruct((model, rows), BF16)
    block = (line, 2, 2, own_rows)
    dma = pltpu.SemaphoreType.DMA
    return pl.pallas_call(
        functools.partial(ahead_kernel, chunks, line, width),
        in_specs=[anywhere] * 7 + [inside] * 5,
        out_shape=full + [flat, flat, full[2], full[3]] + [
            jax.ShapeDtypeStruct((8, model), F32), turned, turned, flat, flat,
            jax.ShapeDtypeStruct((model // 256, 2, 8, rows), F32), flat,
            jax.ShapeDtypeStruct((rows, model), F32), jax.ShapeDtypeStruct((8, model), F32),
            jax.ShapeDtypeStruct((8, hidden_cols), F32),
        ],
        out_specs=[anywhere] * 8 + [inside] * 10,
        scratch_shapes=[
            pltpu.VMEM(products.shape, F32), pltpu.VMEM((rows, model), BF16),
            pltpu.VMEM((rows, model), BF16), pltpu.VMEM((rows, model), BF16),
            pltpu.VMEM((rows, model), BF16), pltpu.VMEM((rows, model), F32), pltpu.VMEM((rows, model), F32),
            pltpu.VMEM((model, rows), BF16), pltpu.VMEM((rows, model), BF16), pltpu.VMEM((model, rows), BF16),
            pltpu.VMEM((rows, model), F32), pltpu.VMEM((2,) + block + (1024,), BF16),
            pltpu.VMEM((2, 2) + block + (512,), BF16),
            dma((total,)), dma((total,)), dma((4,)), dma((2, 4)),
            dma((count, 2, line - 1)), dma((count, 2, line - 1)), dma((count, 7)), dma((count, 7)),
            dma((2,)), dma((2, 2)), dma((2, 2)),
        ],
        compiler_params=pltpu.CompilerParams(
            collective_id=cid, has_side_effects=True, vmem_limit_bytes=VMEM_LIMIT
        ),
        name="ahead",
    )(products, *segments, tok, cot, vecs, hidden_bias, boosts, kmask, qmask)


def behind_kernel(chunks, line, width, levels, *refs):
    count = len(chunks)
    (x_f, qkv_f, proj_f, g1_f, g2_f, result, ql_f, kl_f, vl_f, mix_f,
     gmid_ref, mod_ref, feed_rows, stat_ref, boosts, kmask_ref, qmask_ref) = refs[:17]
    (gqkv_f, gproj_f, act_pair, tok_pair) = refs[17:21]
    landing = refs[21 : 21 + count]
    (t_qkv, t_proj, t_fc1, t_fc2, sums_ref, rows_ref, mods_ref) = refs[21 + count : 28 + count]
    rest = refs[28 + count :]
    first_b, second_b, line_b = rest[:count], rest[count : 2 * count], rest[2 * count : 3 * count]
    (core_s, own_s, x_s, ga_s, gat_s, onet_s, acc_s, turn_s, flat_s, w_s, grad_s, gm_s,
     a_send, a_recv, pair_sem, x_sem, w_sem, grad_sem,
     own_sem, load_sem, send_sem, recv_sem, z_send, z_recv) = rest[3 * count :]
    z, x, c, y = where_am_i()
    total = 8 * line
    padded, model = result.shape[0] // 2, result.shape[1]
    half_cols = model // 2
    heads = 256 // width
    partner = device(z, x, c, 1 - y)
    scatter = Scatter(
        chunks, line, [gqkv_f, gproj_f, g1_f, g2_f], [t_qkv, t_proj, t_fc1, t_fc2], landing, core_s, own_s,
        first_b, second_b, line_b, (own_sem, load_sem, send_sem, recv_sem, z_send, z_recv),
    )
    ticks = Ticks(count, scatter.stages())
    mine, others = pl.ds(y * padded, padded), pl.ds((1 - y) * padded, padded)
    pairs = [
        (
            pltpu.make_async_copy(source.at[mine], target.at[y], pair_sem.at[p, 0]),
            remote(source.at[others], target.at[y], pair_sem.at[p, 1], pair_sem.at[p, 2], partner),
        )
        for p, (source, target) in enumerate(((result, act_pair), (x_s, tok_pair)))
    ]
    load_x = pltpu.make_async_copy(x_f, x_s, x_sem.at[0])
    load_x.start()
    greet_all(total)
    ticks.run(0, 1)

    def load_group(i):
        slot = lax.rem(i, 2)
        sub, at = i // 2, slot * 2 + i // 2
        turned = pl.ds(pl.multiple_of(at * 256, 256), 256)
        cols = columns(at * 256, 256)
        pieces = [
            (qkv_f.at[slot, :, :, :, :, columns(sub * 768, 768)], w_s.at[slot, :, :, :, :, pl.ds(0, 768)]),
            (proj_f.at[slot, :, :, :, :, columns(sub * 256, 256)], w_s.at[slot, :, :, :, :, pl.ds(768, 256)]),
            (ql_f.at[turned], turn_s.at[slot, 0]),
            (kl_f.at[turned], turn_s.at[slot, 1]),
            (vl_f.at[:, cols], flat_s.at[slot, 0]),
            (mix_f.at[:, cols], flat_s.at[slot, 1]),
        ]
        return [pltpu.make_async_copy(s, t, w_sem.at[slot, n]) for n, (s, t) in enumerate(pieces)]

    def store_group(i):
        half, sub = lax.rem(i, 2), i // 2
        return [
            pltpu.make_async_copy(
                grad_s.at[:, :, :, :, pl.ds(0, 768)], gqkv_f.at[half, :, :, :, :, columns(sub * 768, 768)],
                grad_sem.at[0],
            ),
            pltpu.make_async_copy(
                grad_s.at[:, :, :, :, pl.ds(768, 256)], gproj_f.at[half, :, :, :, :, columns(sub * 256, 256)],
                grad_sem.at[1],
            ),
        ]

    def start_loads(copies):
        for copy in copies:
            copy.start()

    def wait_loads(copies):
        for copy in copies:
            copy.wait()

    start_loads(load_group(0))
    ticks.run(1, 2)
    attend_grad = (mod_ref[0:1] * gmid_ref[...]).astype(BF16)
    ga_s[...] = attend_grad
    gat_s[...] = attend_grad.T
    rows_ref[2:3] = jnp.sum(attend_grad.astype(F32), 0, keepdims=True)
    ticks.run(2, 3)
    load_x.wait()
    normed, _ = norm_rows(x_s[...].astype(F32))
    onet_s[...] = (normed * (1.0 + mod_ref[2:3]) + mod_ref[4:5]).astype(BF16).T
    acc_s[...] = jnp.zeros_like(acc_s)
    kmask, qmask = kmask_ref[...], qmask_ref[...]
    rows = kmask.shape[1]
    place = lax.broadcasted_iota(jnp.int32, (16, rows), 0)

    def pieces_of(row, first):
        high, mid, low = split_three(row)
        zero = jnp.zeros((16, rows), BF16)
        out = jnp.where(place == first, jnp.broadcast_to(high, zero.shape), zero)
        out = jnp.where(place == first + 1, jnp.broadcast_to(mid, zero.shape), out)
        return jnp.where(place == first + 2, jnp.broadcast_to(low, zero.shape), out)

    def group(i, carry):
        slot = lax.rem(i, 2)
        at = slot * 2 + i // 2

        @pl.when(i < 3)
        def _():
            start_loads(load_group(i + 1))

        wait_loads(load_group(i))
        boost = boosts[at]
        weights = w_s[slot].reshape(model, 1024)
        mixed = flat_s[slot, 1]
        values = flat_s[slot, 0]
        q_all_low, k_all_low = turn_s[slot, 0], turn_s[slot, 1]
        mixed_grad = mm(ga_s[...], weights[:, 768:]).astype(BF16)
        mixed_turned, v_turned, q_plain = mixed_grad.T, values.T, q_all_low.T
        dq_rows, dk_rows, dv_cols, scales = [], [], [], []
        for head in range(heads):
            if head == 2:
                switch_on(i, {n: (lambda n=n: ticks.run(3 + 2 * n, 4 + 2 * n)) for n in range(4)})
            part = slice(head * width, (head + 1) * width)
            lift = boost[0:1, head : head + 1]
            q_bf, k_bf = q_all_low[part], k_all_low[part]
            q_float = q_bf.astype(F32)
            scaled = q_float * LOG2E
            high = scaled.astype(BF16)
            low = (scaled - high.astype(F32)).astype(BF16)
            log_total = stat_ref[at, 1, head : head + 1]
            q_all = jnp.concatenate([high, low, qmask + pieces_of(-log_total, levels + 1)], 0)
            k_all = jnp.concatenate([k_bf, k_bf, kmask], 0)
            soft = jnp.exp2(mm_tn(k_all, q_all))
            product = soft * mm_tn(v_turned[part], mixed_turned[part])
            delta = jnp.sum(product, 0, keepdims=True)
            scores_grad = (product - soft * delta).astype(BF16)
            dv_cols.append(mm(soft.astype(BF16), mixed_grad[:, part]))
            dq_low = mm(k_bf, scores_grad)
            dk_low = mm(scores_grad, q_plain[:, part]).T
            q_inv = stat_ref[at, 0, head : head + 1]
            k_inv = stat_ref[at, 0, heads + head : heads + head + 1]
            k_unit = k_bf.astype(F32)
            along = dq_low * q_float
            scales.append(jnp.sum(along, keepdims=True))
            dq_rows.append(
                q_inv * (dq_low * lift - q_float * (1.0 / lift) * jnp.sum(along, 0, keepdims=True))
            )
            dk_rows.append(k_inv * (dk_low - k_unit * jnp.sum(dk_low * k_unit, 0, keepdims=True)))
        dq = jnp.concatenate(dq_rows, 0).T.astype(BF16)
        dk = jnp.concatenate(dk_rows, 0).T.astype(BF16)
        dv = jnp.concatenate(dv_cols, 1).astype(BF16)
        triple = jnp.concatenate([dq, dk, dv], 1)

        @pl.when(i > 0)
        def _():
            wait_loads(store_group(i))

        shape = grad_s.shape[:4]
        grad_s[:, :, :, :, 0:768] = mm(onet_s[...], triple).astype(BF16).reshape(shape + (768,))
        grad_s[:, :, :, :, 768:1024] = mm(gat_s[...], mixed).astype(BF16).reshape(shape + (256,))
        start_loads(store_group(i))
        acc_s[...] += mm_nt(triple, weights[:, :768])
        sums_ref[at, 0:1, :] = jnp.sum(dq.astype(F32), 0, keepdims=True)
        sums_ref[at, 1:2, :] = jnp.sum(dv.astype(F32), 0, keepdims=True)
        sums_ref[at, 2:4, :] = jnp.zeros((2, 256), F32)
        for head in range(heads):
            sums_ref[at, 4 + head : 5 + head, :] = jnp.broadcast_to(scales[head], (1, 256))

        def end(n):
            def act():
                if n == 1:
                    start_loads(pairs[0])
                ticks.run(4 + 2 * n, 5 + 2 * n)

            return act

        switch_on(i, {n: end(n) for n in range(3)})
        return carry

    lax.fori_loop(0, 4, group, 0)
    wait_loads(store_group(3))
    ticks.run(10, 11)
    grad = acc_s[...]
    normed, inverse = norm_rows(x_s[...].astype(F32))
    x_s[...] = (
        gmid_ref[...] + norm_rows_back(grad * (1.0 + mod_ref[2:3]), normed, inverse)
    ).astype(BF16)
    start_loads(pairs[1])
    rows_ref[0:1] = jnp.sum(grad * normed, 0, keepdims=True)
    rows_ref[1:2] = jnp.sum(grad, 0, keepdims=True)
    rows_ref[3:8] = jnp.zeros((5, model), F32)
    for n, row in enumerate((feed_rows[4:5], feed_rows[0:1], rows_ref[0:1], feed_rows[1:2], rows_ref[1:2], feed_rows[2:3])):
        for half in range(2):
            gm_s[half, n : n + 1] = row[:, half * half_cols : (half + 1) * half_cols]
    gm_s[:, 6:8] = jnp.zeros((2, 2, half_cols), F32)
    exchange = Exchange(total, lambda to: gm_s.at[lax.rem(to, 2)], mods_ref, a_send, a_recv)
    exchange.start()
    ticks.run(11, ticks.total)
    exchange.wait()
    for pair in pairs:
        wait_loads(pair)
    scatter.sent()


def run_behind(chunks, line, levels, saved, inner, width, cid):
    x_f, qkv_f, proj_f, g1_f, g2_f, result, ql, kl, vl, mix = saved
    rows, model = x_f.shape
    total, count = 8 * line, len(chunks)
    own_rows = qkv_f.shape[4]
    anywhere, inside = pl.BlockSpec(memory_space=pl.ANY), pl.BlockSpec(memory_space=pltpu.VMEM)
    dma = pltpu.SemaphoreType.DMA
    landing, first_b, second_b, line_b = [], [], [], []
    for _, kind, _, cols in chunks:
        landing.append(jax.ShapeDtypeStruct((2, line, 2, own_rows, cols), BF16))
        first_b.append(pltpu.VMEM(((line, 2) if kind == 0 else (2, line)) + (own_rows, cols), BF16))
        second_b.append(pltpu.VMEM((line, own_rows, cols), BF16))
        line_b.append(pltpu.VMEM((line + 1, own_rows, cols), BF16))
    most = max(chunk[3] for chunk in chunks)
    sources = [qkv_f, proj_f, g1_f, g2_f]
    block = (line, 2, 2, own_rows)
    made = pl.pallas_call(
        functools.partial(behind_kernel, chunks, line, width, levels),
        in_specs=[anywhere] * 10 + [inside] * 7,
        out_shape=[jax.ShapeDtypeStruct(qkv_f.shape, BF16), jax.ShapeDtypeStruct(proj_f.shape, BF16)]
        + [jax.ShapeDtypeStruct((2, rows // 2, model), BF16)] * 2 + landing
        + [jax.ShapeDtypeStruct(s.shape[4:], F32) for s in sources]
        + [
            jax.ShapeDtypeStruct((model // 256, 8, 256), F32), jax.ShapeDtypeStruct((8, model), F32),
            jax.ShapeDtypeStruct((total, 8, model // 2), F32),
        ],
        out_specs=[anywhere] * (4 + count) + [inside] * 7,
        scratch_shapes=first_b + second_b + line_b + [
            pltpu.VMEM((3, 2, line, 2, own_rows, most), BF16), pltpu.VMEM((2, 2, line, 2, own_rows, most), BF16),
            pltpu.VMEM((rows, model), BF16), pltpu.VMEM((rows, model), BF16), pltpu.VMEM((model, rows), BF16),
            pltpu.VMEM((model, rows), BF16), pltpu.VMEM((rows, model), F32), pltpu.VMEM((2, 2, 256, rows), BF16),
            pltpu.VMEM((2, 2, rows, 256), BF16), pltpu.VMEM((2,) + block + (1024,), BF16),
            pltpu.VMEM(block + (1024,), BF16), pltpu.VMEM((2, 8, model // 2), F32),
            dma((total,)), dma((total,)), dma((2, 3)), dma((1,)), dma((2, 6)), dma((2,)),
            dma((count,)), dma((count,)), dma((count, 3)), dma((count, 3)),
            dma((count, 2, line)), dma((count, 2, line)),
        ],
        compiler_params=pltpu.CompilerParams(
            collective_id=cid, has_side_effects=True, vmem_limit_bytes=VMEM_LIMIT
        ),
        name="behind",
    )(*saved, *inner)
    return made[2], made[3], made[4 + count :]


def pad_rows(values, padded):
    return jnp.pad(values, ((0, 0), (0, padded - values.shape[1]), (0, 0)))


def gather_list():
    return [(0, 1, 0, 768), (1, 1, 0, 256), (0, 0, 768, 768), (1, 1, 256, 256)] + [
        (segment, int((segment, part) not in ((2, 1), (3, 3))), part * 512, 512) for part in range(4) for segment in (2, 3)
    ]


def scatter_list():
    return [
        (segment, int((segment, part) not in ((2, 1), (3, 3))), part * 512, 512) for part in range(4) for segment in (2, 3)
    ] + [(0, 0, 0, 512), (0, 1, 512, 256), (1, 1, 0, 256), (0, 1, 768, 512), (0, 1, 1280, 256), (1, 0, 256, 256)]


def on_device_paired(
    tokens, condition, scale_lengths, order, cotangent, ada_weight, ada_bias, qkv_weight, qv_bias,
    head_log_scale, proj_weight, out_bias, fc1_weight, fc1_bias, fc2_weight,
):
    n_dp, mine = lax.axis_size("dp"), lax.axis_index("mp")
    line = n_dp // 4
    slots, half_rows, model = tokens.shape
    padded = -(-half_rows // 16) * 16
    rows = 2 * padded
    local_heads, width = qv_bias.shape[1], 64
    own_cols = qkv_weight.shape[2]
    own_rows = qkv_weight.shape[1]
    hidden_cols = fc1_weight.shape[1]
    groups = 2 * own_cols // 256
    swap = order[0, 0] != 0
    entries = qv_bias.shape[2]
    vectors = 4 * local_heads + fc1_bias.shape[0]
    scale_at = vectors * entries
    n_dev = 2 * n_dp

    def to_slots(values):
        return jnp.stack([jnp.where(swap, values[1], values[0]), jnp.where(swap, values[0], values[1])])

    cond_slots = to_slots(condition).astype(F32)
    signal = jax.nn.silu(cond_slots).astype(BF16)
    small = jnp.concatenate(
        [qv_bias.reshape(-1), out_bias.reshape(-1), fc1_bias.reshape(-1)] + list(split_three(head_log_scale))
    )
    signal_out = signal.reshape(slots, n_dp, own_rows).transpose(1, 0, 2).reshape(n_dp, 1, slots * own_rows)
    letters = jnp.concatenate(
        [jnp.broadcast_to(signal_out, (n_dp, 2, slots * own_rows)), jnp.broadcast_to(small, (n_dp, 2) + small.shape)], 2
    ).reshape(n_dev, -1)
    letters = lax.all_to_all(letters, ("dp", "mp"), 0, 0, tiled=True).reshape(n_dp, 2, -1)
    signal_rows = letters[:, 0, : slots * own_rows].reshape(n_dev, own_rows)
    small_full = letters[:, :, slots * own_rows :].transpose(1, 0, 2)
    spread_small = small_full[:, :, :scale_at].reshape(2, n_dp, vectors, entries)
    spread_small = spread_small.transpose(0, 2, 1, 3).reshape(2, vectors, n_dp * entries).astype(F32)
    block_rows = spread_small[:, : 4 * local_heads].reshape(2, 4, own_cols).transpose(1, 0, 2).reshape(4, model)
    vecs = jnp.pad(block_rows, ((0, 4), (0, 0)))
    hidden_bias = spread_small[:, 4 * local_heads :].reshape(1, 2 * hidden_cols)
    scale_all = sum(
        small_full[:, 0, scale_at + i * local_heads : scale_at + (i + 1) * local_heads].astype(F32) for i in range(3)
    )
    boost = jnp.exp(scale_all.reshape(groups, -1))
    boosts = jnp.zeros((groups, 8, 128), F32).at[:, 0, : boost.shape[1]].set(boost)

    ada_flat = ada_weight.reshape(own_rows, 6 * own_cols)
    bias_own = lax.dynamic_update_slice(
        jnp.zeros((6, local_heads, width), F32), ada_bias.astype(F32), (0, 0, lax.axis_index("dp") * entries)
    )
    products = jnp.dot(signal_rows, ada_flat, preferred_element_type=F32) + bias_own.reshape(1, 6 * own_cols)
    products = jnp.pad(products.reshape(n_dev, 6, own_cols), ((0, 0), (0, 2), (0, 0)))

    lengths = lax.dynamic_index_in_dim(to_slots(scale_lengths), mine, 0, keepdims=False)
    kmask, qmask = build_masks(lengths, half_rows, padded)
    segments = [
        qkv_weight.reshape(3, own_rows, 2, 256).transpose(1, 2, 0, 3).reshape(own_rows, 3 * own_cols),
        proj_weight.T, fc1_weight, fc2_weight.T,
    ]
    (qkv_f, proj_f, _, _, x_f, _, g1_f, g2_f, mods, q_low, k_low, v_low, mixed, stats, result, grad_middle,
     feed_rows, g_hidden) = run_ahead(
        gather_list(), line, products, segments, pad_rows(to_slots(tokens), padded), pad_rows(cotangent, padded),
        vecs, hidden_bias, boosts, kmask, qmask, width, 1,
    )
    act_pair, tok_pair, (t_qkv, t_proj, t_fc1, t_fc2, sums, back_rows, arrived) = run_behind(
        scatter_list(), line, scale_lengths.shape[1],
        [x_f, qkv_f, proj_f, g1_f, g2_f, result, q_low, k_low, v_low, mixed],
        [grad_middle, mods, feed_rows, stats, boosts, kmask, qmask], width, 2,
    )
    qkv_total = t_qkv.reshape(own_rows, 2, 3, 256).transpose(2, 0, 1, 3).reshape(qkv_weight.shape)
    activations = act_pair[:, :half_rows]
    tokens_grad = to_slots(tok_pair[:, :half_rows])

    all_mods = arrived[:, :6].reshape(n_dev, 6 * own_cols)
    ada_weight_grad = lax.dot_general(
        signal_rows.astype(F32), all_mods, (((0,), (0,)), ((), ())), precision=precise, preferred_element_type=F32
    ).reshape(ada_weight.shape)
    ada_bias_grad = lax.dynamic_slice_in_dim(
        jnp.sum(all_mods, 0).reshape(6, local_heads, width), lax.axis_index("dp") * entries, entries, 2
    )
    signal_part = lax.dot_general(
        all_mods, ada_flat.astype(F32), (((1,), (1,)), ((), ())), precision=precise, preferred_element_type=F32
    )
    bias_grads = jnp.stack([sums[:, 0].reshape(model), sums[:, 1].reshape(model), back_rows[2], feed_rows[3]])
    bias_grads = bias_grads.reshape(4, 2, local_heads, n_dp, entries).transpose(3, 1, 0, 2, 4)
    hidden_grads = g_hidden[0].reshape(2, fc1_bias.shape[0], n_dp, entries).transpose(2, 0, 1, 3)
    scale_grads = jnp.broadcast_to(sums[:, 4:, 0].reshape(1, 2, local_heads), (n_dp, 2, local_heads))
    signal_part = jnp.broadcast_to(signal_part.reshape(n_dp, 1, slots * own_rows), (n_dp, 2, slots * own_rows))
    letters = jnp.concatenate(
        [signal_part, bias_grads.reshape(n_dp, 2, -1), hidden_grads.reshape(n_dp, 2, -1), scale_grads], 2
    ).reshape(n_dev, -1)
    letters = lax.all_to_all(letters, ("dp", "mp"), 0, 0, tiled=True).reshape(n_dp, 2, -1)
    signal_grad = letters[:, :, : slots * own_rows].sum(1).reshape(n_dp, slots, own_rows)
    signal_grad = signal_grad.transpose(1, 0, 2).reshape(slots, model)
    small_total = letters[:, :, slots * own_rows :].sum((0, 1))
    bias_total = small_total[: 4 * local_heads * entries].reshape(2, 2, local_heads, entries)
    hidden_total = small_total[4 * local_heads * entries : scale_at].reshape(fc1_bias.shape)
    pull = jax.vjp(jax.nn.silu, cond_slots)[1]
    condition_grad = to_slots(pull(signal_grad)[0]).astype(BF16)
    return (
        activations, tokens_grad, condition_grad, ada_weight_grad, ada_bias_grad, qkv_total, bias_total[0],
        small_total[scale_at:], t_proj.T, bias_total[1], t_fc1, hidden_total, t_fc2.T,
    )


precise = lax.Precision.HIGHEST


def row_norm(values):
    centre = jnp.mean(values, -1, keepdims=True)
    shifted = values - centre
    inverse = lax.rsqrt(jnp.mean(shifted * shifted, -1, keepdims=True) + 1e-06)
    return (shifted * inverse, inverse)


def row_norm_back(incoming, normed, inverse):
    return inverse * (
        incoming
        - jnp.mean(incoming, -1, keepdims=True)
        - normed * jnp.mean(incoming * normed, -1, keepdims=True)
    )


def gelu_tanh(values):
    return jax.nn.gelu(values, approximate=True)


def spread(shard_rows):
    return lax.all_gather(shard_rows, "mp", axis=0, tiled=True)


def collect(partial_sum):
    return lax.psum_scatter(
        partial_sum.astype(jnp.bfloat16), "mp", scatter_dimension=0, tiled=True
    ).astype(jnp.float32)


def fetch(qkv_weight, qv_bias, proj_weight, out_bias, fc1_weight, fc1_bias, fc2_weight):
    return (
        lax.all_gather(qkv_weight, "dp", axis=1, tiled=True),
        lax.all_gather(qv_bias, "dp", axis=2, tiled=True),
        lax.all_gather(proj_weight, "dp", axis=1, tiled=True),
        lax.all_gather(out_bias, "dp", axis=2, tiled=True),
        lax.all_gather(fc1_weight, "dp", axis=0, tiled=True),
        lax.all_gather(fc1_bias, "dp", axis=1, tiled=True),
        lax.all_gather(fc2_weight, "dp", axis=1, tiled=True),
    )


def settle(grad_set):
    qkv_part, qv_part, proj_part, outb_part, fc1_part, fc1b_part, fc2_part = grad_set
    return (
        lax.psum_scatter(
            qkv_part.astype(jnp.bfloat16), "dp", scatter_dimension=1, tiled=True
        ).astype(jnp.float32),
        lax.psum_scatter(
            qv_part.astype(jnp.bfloat16), "dp", scatter_dimension=2, tiled=True
        ).astype(jnp.float32),
        lax.psum_scatter(
            proj_part.astype(jnp.bfloat16), "dp", scatter_dimension=1, tiled=True
        ).astype(jnp.float32),
        lax.psum_scatter(
            outb_part.astype(jnp.bfloat16), "dp", scatter_dimension=2, tiled=True
        ).astype(jnp.float32),
        lax.psum_scatter(
            fc1_part.astype(jnp.bfloat16), "dp", scatter_dimension=0, tiled=True
        ).astype(jnp.float32),
        lax.psum_scatter(
            fc1b_part.astype(jnp.bfloat16), "dp", scatter_dimension=1, tiled=True
        ).astype(jnp.float32),
        lax.psum_scatter(
            fc2_part.astype(jnp.bfloat16), "dp", scatter_dimension=1, tiled=True
        ).astype(jnp.float32),
    )


def on_device_shared(
    tokens,
    condition,
    scale_lengths,
    order,
    cotangent,
    ada_weight,
    ada_bias,
    qkv_weight,
    qv_bias,
    head_log_scale,
    proj_weight,
    out_bias,
    fc1_weight,
    fc1_bias,
    fc2_weight,
):
    image_count, shard_rows, model_width = tokens.shape
    column_count = qkv_weight.shape[2]
    local_heads = qv_bias.shape[1]
    head_width = column_count // local_heads
    hidden_cols = fc1_weight.shape[1]
    own_start = lax.axis_index("mp") * column_count
    token_count = shard_rows * lax.axis_size("mp")
    ada_full, ada_bias_full = (
        lax.all_gather(ada_weight, "dp", axis=0, tiled=True),
        lax.all_gather(ada_bias, "dp", axis=2, tiled=True),
    )
    cond_float = condition.astype(jnp.float32)
    signal = jax.nn.silu(cond_float).astype(jnp.bfloat16)
    ada_flat = ada_full.reshape(model_width, 6 * column_count)
    mod_share = jnp.dot(
        signal, ada_flat, preferred_element_type=jnp.float32
    ) + ada_bias_full.reshape(6 * column_count).astype(jnp.float32)
    modulation = lax.all_gather(
        mod_share.reshape(image_count, 6, column_count), "mp", axis=2, tiled=True
    )
    head_boost = jnp.exp(head_log_scale)[None, :, None]
    positions = jnp.arange(token_count, dtype=jnp.int32)

    def place(vector):
        return lax.dynamic_update_slice(
            jnp.zeros((model_width,), jnp.float32), vector, (own_start,)
        )

    def own_columns(matrix):
        return lax.dynamic_slice_in_dim(matrix, own_start, column_count, 1)

    def rows_now():
        return fetch(qkv_weight, qv_bias, proj_weight, out_bias, fc1_weight, fc1_bias, fc2_weight)

    full_shapes = (
        (3, model_width, column_count),
        (2, local_heads, head_width),
        (column_count, model_width),
        (2, local_heads, head_width),
        (model_width, hidden_cols),
        (hidden_cols // head_width, head_width),
        (hidden_cols, model_width),
    )
    grad_start = tuple((jnp.zeros(shape_item, jnp.float32) for shape_item in full_shapes))

    def micro_step(micro_at, state_now):
        outputs, token_grads, mod_grads, weight_grads, scale_grad = state_now
        image_at = order[0, micro_at]
        residual = lax.dynamic_index_in_dim(tokens, image_at, 0, keepdims=False).astype(jnp.float32)
        image_mods = lax.dynamic_index_in_dim(modulation, image_at, 0, keepdims=False)
        lengths = lax.dynamic_index_in_dim(scale_lengths, image_at, 0, keepdims=False)
        out_grad = lax.dynamic_index_in_dim(cotangent, micro_at, 0, keepdims=False).astype(
            jnp.float32
        )
        qkv_full, qv_full, proj_full, outb_full, fc1_full, fc1b_full, fc2_full = rows_now()
        steps = jnp.arange(lengths.shape[0], dtype=jnp.int32)
        scale_ends = jnp.sum(jnp.where(steps[None, :] <= steps[:, None], lengths[None, :], 0), 1)
        scale_of = jnp.sum((positions[:, None] >= scale_ends[None, :]).astype(jnp.int32), 1)
        allowed = (scale_of[None, :] <= scale_of[:, None])[None]
        normed_one, inverse_one = row_norm(residual)
        input_one = spread(
            (normed_one * (1.0 + image_mods[2]) + image_mods[4]).astype(jnp.bfloat16)
        )
        projected = jnp.einsum(
            "td,cde->cte", input_one, qkv_full, preferred_element_type=jnp.float32
        )
        bias_pair = qv_full.reshape(2, column_count).astype(jnp.float32)
        queries = (projected[0] + bias_pair[0]).reshape(token_count, local_heads, head_width)
        keys_raw = projected[1].reshape(token_count, local_heads, head_width)
        values_low = (
            (projected[2] + bias_pair[1])
            .astype(jnp.bfloat16)
            .reshape(token_count, local_heads, head_width)
        )
        query_inv = lax.rsqrt(jnp.sum(queries * queries, -1, keepdims=True) + 1e-06)
        key_inv = lax.rsqrt(jnp.sum(keys_raw * keys_raw, -1, keepdims=True) + 1e-06)
        query_unit = queries * query_inv
        key_unit = keys_raw * key_inv
        query_low = (query_unit * head_boost).astype(jnp.bfloat16)
        key_low = key_unit.astype(jnp.bfloat16)

        def masked_scores():
            raw_scores = jnp.einsum(
                "qhd,khd->hqk", query_low, key_low, preferred_element_type=jnp.float32
            )
            return jnp.where(allowed, raw_scores, -1e30)

        scores = masked_scores()
        row_peak = jnp.max(scores, -1, keepdims=True)
        exp_terms = jnp.exp(scores - row_peak)
        totals = jnp.sum(exp_terms, -1, keepdims=True)
        log_total = row_peak + jnp.log(totals)
        soft_weights = exp_terms / totals
        mixed_heads = (
            jnp.einsum(
                "hqk,khd->qhd",
                soft_weights.astype(jnp.bfloat16),
                values_low,
                preferred_element_type=jnp.float32,
            )
            .astype(jnp.bfloat16)
            .reshape(token_count, column_count)
        )
        attended = collect(
            jnp.dot(mixed_heads, proj_full, preferred_element_type=jnp.float32)
            + place(outb_full[0].reshape(column_count).astype(jnp.float32))
        )
        middle = residual + image_mods[0] * attended
        normed_two, inverse_two = row_norm(middle)
        input_two = spread(
            (normed_two * (1.0 + image_mods[3]) + image_mods[5]).astype(jnp.bfloat16)
        )
        hidden = jnp.dot(
            input_two, fc1_full, preferred_element_type=jnp.float32
        ) + fc1b_full.reshape(hidden_cols).astype(jnp.float32)
        activated = gelu_tanh(hidden).astype(jnp.bfloat16)
        branch_out = collect(
            jnp.dot(activated, fc2_full, preferred_element_type=jnp.float32)
            + place(outb_full[1].reshape(column_count).astype(jnp.float32))
        )
        result = (middle + image_mods[1] * branch_out).astype(jnp.bfloat16)
        outputs = lax.dynamic_update_index_in_dim(outputs, result, micro_at, 0)
        qkv_back, qv_back, proj_back, outb_back, fc1_back, fc1b_back, fc2_back = rows_now()
        grad_branch = spread((image_mods[1] * out_grad).astype(jnp.bfloat16))
        gamma_two_grad = jnp.sum(out_grad * branch_out, 0)
        fc2_grad = jnp.dot(activated.T, grad_branch, preferred_element_type=jnp.float32)
        bias_two_grad = jnp.sum(own_columns(grad_branch).astype(jnp.float32), 0)
        act_grad = jnp.dot(grad_branch, fc2_back.T, preferred_element_type=jnp.float32)
        gelu_pull = jax.vjp(gelu_tanh, hidden)[1]
        hidden_grad = gelu_pull(act_grad)[0].astype(jnp.bfloat16)
        fc1_grad = jnp.dot(input_two.T, hidden_grad, preferred_element_type=jnp.float32)
        fc1b_grad = jnp.sum(hidden_grad.astype(jnp.float32), 0).reshape(
            hidden_cols // head_width, head_width
        )
        input_two_grad = collect(
            jnp.dot(hidden_grad, fc1_back.T, preferred_element_type=jnp.float32)
        )
        scale_two_grad = jnp.sum(input_two_grad * normed_two, 0)
        shift_two_grad = jnp.sum(input_two_grad, 0)
        middle_grad = out_grad + row_norm_back(
            input_two_grad * (1.0 + image_mods[3]), normed_two, inverse_two
        )
        grad_attended = spread((image_mods[0] * middle_grad).astype(jnp.bfloat16))
        gamma_one_grad = jnp.sum(middle_grad * attended, 0)
        proj_grad = jnp.dot(mixed_heads.T, grad_attended, preferred_element_type=jnp.float32)
        bias_one_grad = jnp.sum(own_columns(grad_attended).astype(jnp.float32), 0)
        mixed_grad = (
            jnp.dot(grad_attended, proj_back.T, preferred_element_type=jnp.float32)
            .astype(jnp.bfloat16)
            .reshape(token_count, local_heads, head_width)
        )
        soft_again = jnp.exp(masked_scores() - log_total)
        value_grad = jnp.einsum(
            "hqk,qhd->khd",
            soft_again.astype(jnp.bfloat16),
            mixed_grad,
            preferred_element_type=jnp.float32,
        )
        soft_grad = jnp.einsum(
            "qhd,khd->hqk", mixed_grad, values_low, preferred_element_type=jnp.float32
        )
        score_grad = (
            soft_again * (soft_grad - jnp.sum(soft_again * soft_grad, -1, keepdims=True))
        ).astype(jnp.bfloat16)
        query_low_grad = jnp.einsum(
            "hqk,khd->qhd", score_grad, key_low, preferred_element_type=jnp.float32
        )
        key_low_grad = jnp.einsum(
            "hqk,qhd->khd", score_grad, query_low, preferred_element_type=jnp.float32
        )
        head_grad = jnp.sum(query_low_grad * query_unit * head_boost, (0, 2))
        query_unit_grad = query_low_grad * head_boost
        query_grad = query_inv * (
            query_unit_grad - query_unit * jnp.sum(query_unit_grad * query_unit, -1, keepdims=True)
        )
        key_grad = key_inv * (
            key_low_grad - key_unit * jnp.sum(key_low_grad * key_unit, -1, keepdims=True)
        )
        triple_grad = jnp.stack(
            [
                query_grad.reshape(token_count, column_count),
                key_grad.reshape(token_count, column_count),
                value_grad.reshape(token_count, column_count),
            ]
        ).astype(jnp.bfloat16)
        qkv_grad = jnp.einsum(
            "td,cte->cde", input_one, triple_grad, preferred_element_type=jnp.float32
        )
        pair_sums = jnp.sum(triple_grad.astype(jnp.float32), 1)
        qv_grad = jnp.stack([pair_sums[0], pair_sums[2]]).reshape(2, local_heads, head_width)
        input_one_grad = collect(
            jnp.einsum("cte,cde->td", triple_grad, qkv_back, preferred_element_type=jnp.float32)
        )
        scale_one_grad = jnp.sum(input_one_grad * normed_one, 0)
        shift_one_grad = jnp.sum(input_one_grad, 0)
        residual_grad = middle_grad + row_norm_back(
            input_one_grad * (1.0 + image_mods[2]), normed_one, inverse_one
        )
        token_grads = lax.dynamic_update_index_in_dim(
            token_grads, residual_grad.astype(jnp.bfloat16), image_at, 0
        )
        image_mod_grad = jnp.stack(
            [
                gamma_one_grad,
                gamma_two_grad,
                scale_one_grad,
                scale_two_grad,
                shift_one_grad,
                shift_two_grad,
            ]
        )
        mod_grads = lax.dynamic_update_index_in_dim(mod_grads, image_mod_grad, image_at, 0)
        outb_grad = jnp.stack([bias_one_grad, bias_two_grad]).reshape(2, local_heads, head_width)
        local_grads = (qkv_grad, qv_grad, proj_grad, outb_grad, fc1_grad, fc1b_grad, fc2_grad)
        weight_grads = tuple(
            (running + addend for running, addend in zip(weight_grads, local_grads))
        )
        return (outputs, token_grads, mod_grads, weight_grads, scale_grad + head_grad)

    start_state = (
        jnp.zeros(tokens.shape, jnp.bfloat16),
        jnp.zeros(tokens.shape, jnp.bfloat16),
        jnp.zeros((image_count, 6, model_width), jnp.float32),
        grad_start,
        jnp.zeros((local_heads,), jnp.float32),
    )
    outputs, token_grads, mod_grads, weight_grads, scale_grad = lax.fori_loop(
        0, image_count, micro_step, start_state
    )
    shard_grads = settle(weight_grads)
    mod_share_grad = lax.psum_scatter(
        mod_grads.astype(jnp.bfloat16), "mp", scatter_dimension=2, tiled=True
    ).astype(jnp.float32)
    flat_grad = mod_share_grad.reshape(image_count, 6 * column_count)
    ada_grad = jnp.dot(
        signal.astype(jnp.float32).T,
        flat_grad,
        precision=precise,
        preferred_element_type=jnp.float32,
    ).reshape(model_width, 6, column_count)
    ada_bias_grad = jnp.sum(mod_share_grad, 0).reshape(6, local_heads, head_width)
    signal_grad = lax.psum(
        jnp.dot(
            flat_grad,
            ada_flat.astype(jnp.float32).T,
            precision=precise,
            preferred_element_type=jnp.float32,
        ),
        "mp",
    )
    silu_pull = jax.vjp(jax.nn.silu, cond_float)[1]
    condition_grad = silu_pull(signal_grad)[0].astype(jnp.bfloat16)
    ada_shard, ada_bias_shard = (
        lax.psum_scatter(
            ada_grad.astype(jnp.bfloat16), "dp", scatter_dimension=0, tiled=True
        ).astype(jnp.float32),
        lax.psum_scatter(
            ada_bias_grad.astype(jnp.bfloat16), "dp", scatter_dimension=2, tiled=True
        ).astype(jnp.float32),
    )
    head_scale_grad = lax.psum(scale_grad, "dp")
    qkv_shard, qv_shard, proj_shard, outb_shard, fc1_shard, fc1b_shard, fc2_shard = shard_grads
    return (
        outputs,
        token_grads,
        condition_grad,
        ada_shard,
        ada_bias_shard,
        qkv_shard,
        qv_shard,
        head_scale_grad,
        proj_shard,
        outb_shard,
        fc1_shard,
        fc1b_shard,
        fc2_shard,
    )


def solution(mesh):
    in_specs = (
        P("dp", "mp", None),
        P("dp", None),
        P("dp", None),
        P("dp", None),
        P("dp", "mp", None),
        P("dp", None, "mp"),
        P(None, "mp", "dp"),
        P(None, "dp", "mp"),
        P(None, "mp", "dp"),
        P("mp"),
        P("mp", "dp"),
        P(None, "mp", "dp"),
        P("dp", "mp"),
        P("mp", "dp"),
        P("mp", "dp"),
    )
    out_specs = (
        P("dp", "mp", None),
        P("dp", "mp", None),
        P("dp", None),
        P("dp", None, "mp"),
        P(None, "mp", "dp"),
        P(None, "dp", "mp"),
        P(None, "mp", "dp"),
        P("mp"),
        P("mp", "dp"),
        P(None, "mp", "dp"),
        P("dp", "mp"),
        P("mp", "dp"),
        P("mp", "dp"),
    )
    line, spare = divmod(mesh.shape["dp"], 4)
    paired = mesh.shape["mp"] == 2 and spare == 0 and line > 1
    return jax.shard_map(
        on_device_paired if paired else on_device_shared, mesh=mesh, in_specs=in_specs, out_specs=out_specs, check_vma=False
    )
```

```python
import functools
import jax
import jax.numpy as jnp
from jax import lax
from jax.experimental import pallas as pl
from jax.experimental.pallas import tpu as pltpu
from jax.sharding import PartitionSpec as P

F32 = jnp.float32
BF16 = jnp.bfloat16
MESH = pl.DeviceIdType.MESH
LOG2E = 1.4426950408889634
VMEM_LIMIT = 60 * 1024 * 1024


def mm(a, b):
    return jnp.dot(a, b, preferred_element_type=F32)


def mm_nt(a, b):
    return lax.dot_general(a, b, (((1,), (1,)), ((), ())), preferred_element_type=F32)


def mm_tn(a, b):
    return lax.dot_general(a, b, (((0,), (0,)), ((), ())), preferred_element_type=F32)


def norm_rows(values):
    centre = jnp.mean(values, -1, keepdims=True)
    shifted = values - centre
    inverse = lax.rsqrt(jnp.mean(shifted * shifted, -1, keepdims=True) + 1e-06)
    return shifted * inverse, inverse


def norm_rows_back(incoming, normed, inverse):
    return inverse * (
        incoming
        - jnp.mean(incoming, -1, keepdims=True)
        - normed * jnp.mean(incoming * normed, -1, keepdims=True)
    )


def split_three(values):
    high = values.astype(BF16)
    rest = values - high.astype(F32)
    middle = rest.astype(BF16)
    return high, middle, (rest - middle.astype(F32)).astype(BF16)


def build_masks(lengths, half_rows, padded):
    count = lengths.shape[0]
    steps = jnp.arange(count, dtype=jnp.int32)
    ends = jnp.sum(jnp.where(steps[None, :] <= steps[:, None], lengths[None, :], 0), 1)
    place = jnp.arange(2 * padded, dtype=jnp.int32)
    part, inside = place // padded, place % padded
    token = part * half_rows + inside
    level = jnp.sum((token[None, :] >= ends[:, None]).astype(jnp.int32), 0)
    real = inside < half_rows
    entry = jnp.arange(16, dtype=jnp.int32)[:, None]
    key_level = jnp.where(real, level, count)[None]
    kmask = (entry == key_level) | ((entry > count) & (entry < count + 4))
    query_level = jnp.where(real, level, count - 1)[None]
    qmask = (entry > query_level) & (entry <= count)
    return kmask.astype(BF16), jnp.where(qmask, -32768.0, 0.0).astype(BF16)


def device(z, x, c, y):
    return (z * 4 + x * 2 + c, y)


def where_am_i():
    dp, y = lax.axis_index("dp"), lax.axis_index("mp")
    return dp // 4, (dp // 2) % 2, dp % 2, y


def remote(source, target, send, recv, to):
    return pltpu.make_async_remote_copy(source, target, send, recv, device_id=to, device_id_type=MESH)


def greet_all(total):
    me = lax.axis_index("dp") * 2 + lax.axis_index("mp")
    barrier = pltpu.get_barrier_semaphore()

    def signal(step, carry):
        to = lax.rem(me + step, total)
        pl.semaphore_signal(barrier, inc=1, device_id=(to // 2, to % 2), device_id_type=MESH)
        return carry

    lax.fori_loop(1, total, signal, 0)
    pl.semaphore_wait(barrier, total - 1)


class Exchange:
    def __init__(self, total, block_of, landing, send, recv):
        self.total, self.block_of, self.landing, self.send, self.recv = total, block_of, landing, send, recv
        self.me = lax.axis_index("dp") * 2 + lax.axis_index("mp")

    def copy(self, step):
        to = lax.rem(self.me + step, self.total)
        return remote(
            self.block_of(to), self.landing, self.send.at[step], self.recv.at[step], (to // 2, to % 2)
        )

    def own(self):
        return pltpu.make_async_copy(self.block_of(self.me), self.landing, self.send.at[0])

    def each(self, act):
        def body(step, carry):
            act(self.copy(step))
            return carry

        lax.fori_loop(1, self.total, body, 0)

    def start(self):
        self.own().start()
        self.each(lambda copy: copy.start())

    def wait(self):
        self.own().wait()
        self.each(lambda copy: copy.wait())


class Ticks:
    def __init__(self, count, stages):
        self.count, self.stages = count, stages
        self.total = count + len(stages) - 1

    def run(self, since, until):
        for tick in range(since, until):
            for at, stage in enumerate(self.stages):
                if 0 <= tick - at < self.count:
                    stage(tick - at)


class Gather:
    def __init__(self, batches, line, sources, outs, z_send, z_recv, send_sem, recv_sem):
        self.batches, self.line, self.sources, self.outs = batches, line, sources, outs
        self.chunks = [chunk for batch in batches for chunk in batch]
        self.z_send, self.z_recv, self.send_sem, self.recv_sem = z_send, z_recv, send_sem, recv_sem
        self.z, self.x, self.c, self.y = where_am_i()
        z, x, c, y = self.z, self.x, self.c, self.y
        self.x_side, self.y_side, self.sibling = device(z, 1 - x, c, y), device(z, x, c, 1 - y), device(z, x, 1 - c, y)

    def part(self, k, yy, zz, xx):
        seg, _, start, cols, row, rows = self.chunks[k]
        return self.outs[seg].at[yy, zz, xx, self.c, pl.ds(row, rows), pl.ds(start, cols)]

    def along(self, k, step):
        seg, _, start, cols, row, rows = self.chunks[k]
        source = self.sources[seg].at[pl.ds(row, rows), pl.ds(start, cols)]
        to = device(lax.rem(self.z + step, self.line), self.x, self.c, self.y)
        return remote(
            source, self.part(k, self.y, self.z, self.x), self.z_send.at[k, step - 1], self.z_recv.at[k, step - 1], to
        )

    def group(self, k, slot, at, target):
        ref = self.part(k, at[0], slice(None), at[1])
        return remote(ref, ref, self.send_sem.at[k, slot], self.recv_sem.at[k, slot], target)

    def groups(self, k):
        x, y = self.x, self.y
        if self.chunks[k][1] == 0:
            return [(y, x), (y, 1 - x), (1 - y, x), (1 - y, 1 - x)], self.x_side, self.y_side
        return [(y, x), (1 - y, x), (y, 1 - x), (1 - y, 1 - x)], self.y_side, self.x_side

    def step(self, k, stage):
        order, first, second = self.groups(k)
        if stage == 0:
            for step in range(1, self.line):
                self.along(k, step).start()
        elif stage == 1:
            for step in range(1, self.line):
                self.along(k, step).wait_recv()
            self.group(k, 0, order[0], first).start()
            self.group(k, 1, order[0], second).start()
            self.group(k, 3, order[0], self.sibling).start()
        elif stage == 2:
            self.group(k, 0, order[1], first).wait_recv()
            self.group(k, 2, order[1], second).start()
            self.group(k, 4, order[1], self.sibling).start()
        else:
            self.group(k, 1, order[2], second).wait_recv()
            self.group(k, 5, order[2], self.sibling).start()
            self.group(k, 2, order[3], second).wait_recv()
            self.group(k, 6, order[3], self.sibling).start()

    def members(self, batch):
        before = sum(len(b) for b in self.batches[:batch])
        return range(before, before + len(self.batches[batch]))

    def stages(self):
        def make(stage):
            def act(batch):
                for k in self.members(batch):
                    self.step(k, stage)

            return act

        return [make(stage) for stage in range(4)]

    def finish(self, batch):
        for k in self.members(batch):
            order, _, _ = self.groups(k)
            for slot, at in ((3, 0), (4, 1), (5, 2), (6, 3)):
                self.group(k, slot, order[at], self.sibling).wait_recv()

    def sent(self):
        for k in range(len(self.chunks)):
            order, _, _ = self.groups(k)
            for step in range(1, self.line):
                self.along(k, step).wait_send()
            for slot, at in ((0, 0), (1, 0), (2, 1), (3, 0), (4, 1), (5, 2), (6, 3)):
                self.group(k, slot, order[at], self.sibling).wait_send()


def add_into(target, source, pieces, target_at, source_at):
    def body(i, carry):
        t, s = target_at(i), source_at(i)
        target[t] = target[t] + source[s]
        return carry

    lax.fori_loop(0, pieces, body, 0)


class Scatter:
    def __init__(self, batches, line, sources, totals, landing, core_s, own_s, first_b, second_b, line_b, sems):
        self.batches, self.line, self.sources, self.totals = batches, line, sources, totals
        self.chunks = [chunk for batch in batches for chunk in batch]
        self.landing, self.core_s, self.own_s = landing, core_s, own_s
        self.first_b, self.second_b, self.line_b = first_b, second_b, line_b
        self.own_sem, self.load_sem, self.send_sem, self.recv_sem, self.z_send, self.z_recv = sems
        self.z, self.x, self.c, self.y = where_am_i()
        z, x, c, y = self.z, self.x, self.c, self.y
        self.x_side, self.y_side, self.sibling = device(z, 1 - x, c, y), device(z, x, c, 1 - y), device(z, x, 1 - c, y)
        self.spot = {}
        for b, batch in enumerate(batches):
            column = 0
            for k in self.members(b):
                self.spot[k] = (b, column)
                column += self.chunks[k][3]

    def members(self, batch):
        before = sum(len(b) for b in self.batches[:batch])
        return range(before, before + len(self.batches[batch]))

    def source(self, k, c):
        seg, _, start, cols = self.chunks[k]
        return self.sources[seg].at[:, :, :, c, :, pl.ds(start, cols)]

    def core_copy(self, k):
        return remote(
            self.source(k, 1 - self.c), self.landing[k], self.send_sem.at[k, 0], self.recv_sem.at[k, 0], self.sibling
        )

    def core(self, k):
        batch, column = self.spot[k]
        return self.core_s.at[batch % 3, :, :, :, :, pl.ds(column, self.chunks[k][3])]

    def own(self, k):
        batch, column = self.spot[k]
        return self.own_s.at[batch % 2, :, :, :, :, pl.ds(column, self.chunks[k][3])]

    def own_copy(self, k):
        return pltpu.make_async_copy(self.source(k, self.c), self.own(k), self.own_sem.at[k])

    def load_copy(self, k):
        return pltpu.make_async_copy(self.landing[k], self.core(k), self.load_sem.at[k])

    def first_copy(self, k):
        core, sems = self.core(k), (self.send_sem.at[k, 1], self.recv_sem.at[k, 1])
        if self.chunks[k][1] == 0:
            return remote(core.at[1 - self.y], self.first_b[k], *sems, self.y_side)
        return remote(core.at[:, :, 1 - self.x], self.first_b[k], *sems, self.x_side)

    def second_copy(self, k):
        first, sems = self.first_b[k], (self.send_sem.at[k, 2], self.recv_sem.at[k, 2])
        if self.chunks[k][1] == 0:
            return remote(first.at[:, 1 - self.x], self.second_b[k], *sems, self.x_side)
        return remote(first.at[1 - self.y], self.second_b[k], *sems, self.y_side)

    def line_copy(self, k, step):
        owner = lax.rem(self.z + step, self.line)
        return remote(
            self.second_b[k].at[owner], self.line_b[k].at[step - 1],
            self.z_send.at[k, step - 1], self.z_recv.at[k, step - 1], device(owner, self.x, self.c, self.y),
        )

    def step(self, k, stage):
        line, x, y, z = self.line, self.x, self.y, self.z
        early = self.chunks[k][1] == 0
        if stage == 0:
            self.core_copy(k).start()
        elif stage == 1:
            self.core_copy(k).wait_recv()
            self.load_copy(k).start()
            self.own_copy(k).start()
        elif stage == 2:
            self.load_copy(k).wait()
            self.own_copy(k).wait()
            at = lambda i: (i // (2 * line), (i // 2) % line, i % 2)
            add_into(self.core(k), self.own(k), 4 * line, at, at)
            self.first_copy(k).start()
        elif stage == 3:
            self.first_copy(k).wait_recv()
            if early:
                there, here = (lambda i: (i // 2, i % 2)), (lambda i: (y, i // 2, i % 2))
            else:
                there, here = (lambda i: (i // line, i % line)), (lambda i: (i // line, i % line, x))
            add_into(self.first_b[k], self.core(k), 2 * line, there, here)
            self.second_copy(k).start()
            self.first_copy(k).wait_send()
        elif stage == 4:
            self.second_copy(k).wait_recv()
            here = (lambda i: (i, x)) if early else (lambda i: (y, i))
            add_into(self.second_b[k], self.first_b[k], line, lambda i: (i,), here)
            for step in range(1, line):
                self.line_copy(k, step).start()
        else:
            seg, _, start, cols = self.chunks[k]
            total = self.second_b[k][z].astype(F32)
            for step in range(1, line):
                self.line_copy(k, step).wait_recv()
                total = total + self.line_b[k][step - 1].astype(F32)
            self.totals[seg][:, pl.ds(start, cols)] = total

    def stages(self):
        def make(stage):
            def act(batch):
                for k in self.members(batch):
                    self.step(k, stage)

            return act

        return [make(stage) for stage in range(6)]

    def sent(self):
        for k in range(len(self.chunks)):
            self.core_copy(k).wait_send()
            self.second_copy(k).wait_send()
            for step in range(1, self.line):
                self.line_copy(k, step).wait_send()


def switch_on(index, cases):
    for at, act in cases.items():
        pl.when(index == at)(act)


def columns(start, size):
    return pl.ds(pl.multiple_of(start, 128), size)


def owner_maps(owners, entries, width, model):
    inner = model // width * entries
    at = lax.broadcasted_iota(jnp.int32, (inner, model), 1)
    place = lax.broadcasted_iota(jnp.int32, (inner, model), 0)
    spread = jnp.where(at // width * entries + at % entries == place, 1.0, 0.0).astype(BF16)
    at = lax.broadcasted_iota(jnp.int32, (owners, model), 1)
    owner = lax.broadcasted_iota(jnp.int32, (owners, model), 0)
    return spread, jnp.where(at % width // entries == owner, 1.0, 0.0)


def ahead_kernel(batches, line, width, *refs):
    (signals, ada, extra, seg_qkv, seg_proj, seg_fc1, seg_fc2, tok, cot, kmask_ref, qmask_ref,
     qkv_f, proj_f, fc1_f, fc2_f, g1_f, g2_f, ql_f, kl_f, vl_f, mix_f, x_f,
     boosts, mod_ref, stat_ref, out_ref, gmid_ref, rows_ref, gb1_ref, sig_s, ada_flat,
     products, arrived, vecs, hidden_bias, x_s, ql_ref, kl_ref, vl_ref, mix_ref, att_ref, cot_s, one_s, acc_s, mid_s, twot_s, back_s, backt_s, gacc_s, w_s, grad_s,
     a_send, a_recv, b_send, b_recv, save_sem, local_sem, pair_sem, z_send, z_recv, send_sem, recv_sem, w_sem, grad_sem) = refs
    z, x, c, y = where_am_i()
    total = 8 * line
    padded, model = tok.shape[1:]
    half_cols = mod_ref.shape[1] // 2
    heads = 256 // width
    outs = [qkv_f, proj_f, fc1_f, fc2_f]
    own = [
        pltpu.make_async_copy(i, o.at[y, z, x, c], local_sem.at[s])
        for s, (i, o) in enumerate(zip([seg_qkv, seg_proj, seg_fc1, seg_fc2], outs))
    ]
    for copy in own:
        copy.start()
    mine = pl.ds(y * padded, padded)
    pairs = [
        (
            pltpu.make_async_copy(source.at[y], inside.at[mine], pair_sem.at[p, 0]),
            remote(
                source.at[1 - y], inside.at[mine], pair_sem.at[p, 1], pair_sem.at[p, 2], device(z, x, c, 1 - y)
            ),
        )
        for p, (source, inside) in enumerate(((tok, x_s), (cot, cot_s)))
    ]
    me = (lax.axis_index("dp"), y)
    signal_exchange = Exchange(total, lambda to: signals.at[to // 2], sig_s.at[me], b_send, b_recv)
    exchange = Exchange(total, lambda to: products.at[to // 2, to % 2], arrived.at[me], a_send, a_recv)
    gather = Gather(
        batches, line, [seg_qkv, seg_proj, seg_fc1, seg_fc2], outs, z_send, z_recv, send_sem, recv_sem
    )
    ticks = Ticks(len(batches), gather.stages())
    greet_all(total)
    signal_exchange.start()
    ticks.run(0, 1)
    for copy in pairs[0]:
        copy.start()
    for copy in own:
        copy.wait()

    def load_attend(i):
        half, sub, slot = i % 2, i // 2, i % 2
        return [
            pltpu.make_async_copy(
                qkv_f.at[half, :, :, :, :, pl.ds(sub * 768, 768)], w_s.at[slot, :, :, :, :, pl.ds(0, 768)],
                w_sem.at[slot, 0],
            ),
            pltpu.make_async_copy(
                proj_f.at[half, :, :, :, :, pl.ds(sub * 256, 256)], w_s.at[slot, :, :, :, :, pl.ds(768, 256)],
                w_sem.at[slot, 1],
            ),
        ]

    def load_feed(half, part):
        return [
            pltpu.make_async_copy(
                ref.at[half, :, :, :, :, columns(part * 512, 512)],
                w_s.at[half, :, :, :, :, pl.ds(at * 512, 512)], w_sem.at[half, at],
            )
            for at, ref in enumerate((fc1_f, fc2_f))
        ]

    def start_loads(copies):
        for copy in copies:
            copy.start()

    def wait_loads(copies):
        for copy in copies:
            copy.wait()

    for j in range(6):
        ada_flat[:, j * half_cols : (j + 1) * half_cols] = ada[:, j, :]
    signal_exchange.wait()
    slots, owners = sig_s.shape[1], sig_s.shape[0]
    for slot in range(slots):
        rows_in = sig_s[:, 0, slot, : ada.shape[0]].astype(BF16)
        for j in range(8):
            block = jnp.broadcast_to(extra[j : j + 1], (owners, half_cols))
            if j < 6:
                block = block + mm(rows_in, ada_flat[:, j * half_cols : (j + 1) * half_cols])
            products[:, slot, j, :] = block
    exchange.start()
    ticks.run(1, 2)
    for copy in pairs[1]:
        copy.start()
    ticks.run(2, 4)
    exchange.wait()
    for half in range(2):
        mod_ref[:, half * half_cols : (half + 1) * half_cols] = jnp.sum(arrived[:, half], 0)
    entries = width // owners
    spread, owner_of = owner_maps(owners, entries, width, model)
    letters = [arrived[:, half, 6, :] for half in range(2)]
    piece = heads * entries * 2
    blocks = [
        jnp.concatenate([letter[:, r * piece : (r + 1) * piece] for letter in letters], 1) for r in range(4)
    ] + [
        letters[half][:, (4 + 2 * part) * piece : (6 + 2 * part) * piece] for half in range(2) for part in range(2)
    ]
    turned_out = mm(jnp.concatenate(blocks, 0).astype(BF16), spread)
    for r in range(8):
        row = jnp.sum(turned_out[r * owners : (r + 1) * owners] * owner_of, 0, keepdims=True)
        if r < 4:
            vecs[r : r + 1] = row
        else:
            hidden_bias[0:1, (r - 4) * model : (r - 3) * model] = row
    boosts[...] = jnp.zeros_like(boosts)
    for half in range(2):
        lift = jnp.exp(arrived[0, half, 7:8, : 2 * heads])
        for sub in range(2):
            boosts[half * 2 + sub, 0:1, 0:heads] = lift[:, sub * heads : (sub + 1) * heads]
    wait_loads(pairs[0])
    normed, _ = norm_rows(x_s[...].astype(F32))
    one_s[...] = (normed * (1.0 + mod_ref[2:3]) + mod_ref[4:5]).astype(BF16)
    acc_s[...] = jnp.zeros_like(acc_s)
    ticks.run(4, 5)
    gather.finish(0)
    gather.finish(1)
    start_loads(load_attend(0))
    start_loads(load_attend(1))
    ones = jnp.ones((x_s.shape[0], width), BF16)

    def attend(i, carry):
        @pl.when(i == 2)
        def _():
            ticks.run(5, 6)
            gather.finish(2)
            start_loads(load_attend(2))
            start_loads(load_attend(3))

        slot = lax.rem(i, 2)
        at = slot * 2 + i // 2
        wait_loads([
            pltpu.make_async_copy(
                qkv_f.at[0, :, :, :, :, pl.ds(0, 768)], w_s.at[slot, :, :, :, :, pl.ds(0, 768)], w_sem.at[slot, 0]
            ),
            pltpu.make_async_copy(
                proj_f.at[0, :, :, :, :, pl.ds(0, 256)], w_s.at[slot, :, :, :, :, pl.ds(768, 256)], w_sem.at[slot, 1]
            ),
        ])
        cols = columns(at * 256, 256)
        turned = pl.ds(pl.multiple_of(at * 256, 256), 256)
        weights = w_s[slot].reshape(model, 1024)
        projected = mm(one_s[...], weights[:, :768])
        queries = projected[:, :256] + vecs[0:1, cols]
        keys = projected[:, 256:512]
        values = (projected[:, 512:] + vecs[1:2, cols]).astype(BF16)
        vl_ref[:, cols] = values
        q_turned, k_turned = queries.T, keys.T
        boost = boosts[at]
        kmask, qmask = kmask_ref[...], qmask_ref[...]
        q_low, k_low, mixed, q_inv, k_inv, totals = [], [], [], [], [], []
        for head in range(heads):
            part = slice(head * width, (head + 1) * width)
            q_now, k_now = q_turned[part], k_turned[part]
            q_scale = lax.rsqrt(jnp.sum(q_now * q_now, 0, keepdims=True) + 1e-06)
            k_scale = lax.rsqrt(jnp.sum(k_now * k_now, 0, keepdims=True) + 1e-06)
            q_bf = (q_now * q_scale * boost[0:1, head : head + 1]).astype(BF16)
            k_bf = (k_now * k_scale).astype(BF16)
            scaled = q_bf.astype(F32) * LOG2E
            high = scaled.astype(BF16)
            rest = (scaled - high.astype(F32)).astype(BF16)
            q_all = jnp.concatenate([high, rest, qmask], 0)
            k_all = jnp.concatenate([k_bf, k_bf, kmask], 0)
            soft = jnp.exp2(mm_tn(q_all, k_all)).astype(BF16)
            summed = mm(soft, jnp.concatenate([values[:, part], ones], 1))
            total_now = summed[:, width:]
            mixed.append((summed[:, :width] / total_now).astype(BF16))
            totals.append(total_now[:, 0:1])
            q_low.append(q_bf)
            k_low.append(k_bf)
            q_inv.append(q_scale)
            k_inv.append(k_scale)
        mixed_all = jnp.concatenate(mixed, 1)
        mix_ref[:, cols] = mixed_all
        ql_ref[turned, :] = jnp.concatenate(q_low, 0)
        kl_ref[turned, :] = jnp.concatenate(k_low, 0)
        stat_ref[at, 0] = jnp.concatenate(q_inv + k_inv, 0)
        stat_ref[at, 1] = jnp.log2(jnp.concatenate(totals + totals, 1)).T
        acc_s[...] += mm_nt(mixed_all, weights[:, 768:])
        return carry

    lax.fori_loop(0, 4, attend, 0)
    saves = [
        pltpu.make_async_copy(inside, outside, save_sem.at[n])
        for n, (inside, outside) in enumerate(
            ((ql_ref, ql_f), (kl_ref, kl_f), (vl_ref, vl_f), (mix_ref, mix_f), (x_s, x_f))
        )
    ]
    start_loads(saves)
    attended = acc_s[...] + vecs[2:3]
    att_ref[...] = attended.astype(BF16)
    middle = x_s[...].astype(F32) + mod_ref[0:1] * attended
    mid_s[...] = middle
    normed, _ = norm_rows(middle)
    two = (normed * (1.0 + mod_ref[3:4]) + mod_ref[5:6]).astype(BF16)
    one_s[...] = two
    twot_s[...] = two.T
    wait_loads(pairs[1])
    back = (mod_ref[1:2] * cot_s[...].astype(F32)).astype(BF16)
    back_s[...] = back
    backt_s[...] = back.T
    acc_s[...] = jnp.zeros_like(acc_s)
    gacc_s[...] = jnp.zeros_like(gacc_s)

    def store_feed(half, part):
        return [
            pltpu.make_async_copy(
                grad_s.at[half, at], ref.at[half, :, :, :, :, columns(part * 512, 512)], grad_sem.at[half, at]
            )
            for at, ref in enumerate((g1_f, g2_f))
        ]

    def feed(i, carry):
        half, part = lax.rem(i, 2), i // 2

        def before(p):
            def act():
                ticks.run(6 + p, 7 + p)
                gather.finish(3 + p)
                start_loads(load_feed(0, p))
                start_loads(load_feed(1, p))

            return act

        switch_on(i, {2 * p: before(p) for p in range(4)})
        wait_loads(load_feed(half, part))
        weights = w_s[half].reshape(model, 1024)
        w1, w2 = weights[:, :512], weights[:, 512:]
        spot = columns(half * (hidden_bias.shape[1] // 2) + part * 512, 512)
        hidden = mm(one_s[...], w1) + hidden_bias[0:1, spot]
        square = hidden * hidden
        curve = jnp.tanh(0.7978845608028654 * hidden * (1.0 + 0.044715 * square))
        level = 0.5 * (1.0 + curve)
        activated = (hidden * level).astype(BF16)
        slope = level + 0.5 * hidden * (1.0 - curve * curve) * (
            0.7978845608028654 * (1.0 + 0.134145 * square)
        )
        acc_s[...] += mm_nt(activated, w2)

        @pl.when(i >= 2)
        def _():
            wait_loads(store_feed(half, part))

        grad_s[half, 1] = mm(backt_s[...], activated).astype(BF16).reshape(grad_s.shape[2:])
        hidden_grad = (mm(back_s[...], w2) * slope).astype(BF16)
        grad_s[half, 0] = mm(twot_s[...], hidden_grad).astype(BF16).reshape(grad_s.shape[2:])
        start_loads(store_feed(half, part))
        gb1_ref[0:1, spot] = jnp.sum(hidden_grad.astype(F32), 0, keepdims=True)
        gacc_s[...] += mm_nt(hidden_grad, w1)
        return carry

    lax.fori_loop(0, 8, feed, 0)
    middle = mid_s[...]
    out_grad = cot_s[...].astype(F32)
    branch = acc_s[...] + vecs[3:4]
    out_ref[...] = (middle + mod_ref[1:2] * branch).astype(BF16)
    normed, inverse = norm_rows(middle)
    grad = gacc_s[...]
    middle_grad = out_grad + norm_rows_back(grad * (1.0 + mod_ref[3:4]), normed, inverse)
    gmid_ref[...] = middle_grad
    rows_ref[0:1] = jnp.sum(out_grad * branch, 0, keepdims=True)
    rows_ref[1:2] = jnp.sum(grad * normed, 0, keepdims=True)
    rows_ref[2:3] = jnp.sum(grad, 0, keepdims=True)
    rows_ref[3:4] = jnp.sum(back_s[...].astype(F32), 0, keepdims=True)
    rows_ref[4:5] = jnp.sum(middle_grad * att_ref[...].astype(F32), 0, keepdims=True)
    rows_ref[5:8] = jnp.zeros((3, model), F32)
    gb1_ref[1:8] = jnp.zeros((7, gb1_ref.shape[1]), F32)
    for half in range(2):
        wait_loads(store_feed(half, 3))
    wait_loads(saves)
    gather.sent()


def run_ahead(batches, line, signals, ada, extra, segments, tok, cot, kmask, qmask, hidden_cols, width, cid):
    padded, model = tok.shape[1:]
    rows = 2 * padded
    total, count = 8 * line, sum(len(batch) for batch in batches)
    own_rows = segments[0].shape[0]
    anywhere, inside = pl.BlockSpec(memory_space=pl.ANY), pl.BlockSpec(memory_space=pltpu.VMEM)
    full = [jax.ShapeDtypeStruct((2, line, 2, 2) + s.shape, BF16) for s in segments]
    flat = jax.ShapeDtypeStruct((rows, model), BF16)
    turned = jax.ShapeDtypeStruct((model, rows), BF16)
    flat_s, turned_s, wide_s = (
        pltpu.VMEM((rows, model), BF16), pltpu.VMEM((model, rows), BF16), pltpu.VMEM((rows, model), F32)
    )
    block = (line, 2, 2, own_rows)
    dma = pltpu.SemaphoreType.DMA
    letters = pltpu.VMEM((total // 2, 2, 8, model // 2), F32)
    return pl.pallas_call(
        functools.partial(ahead_kernel, batches, line, width),
        in_specs=[inside] * 7 + [anywhere] * 2 + [inside] * 2,
        out_shape=full + [full[2], full[3], turned, turned, flat, flat, flat] + [
            jax.ShapeDtypeStruct((model // 256, 8, 128), F32), jax.ShapeDtypeStruct((8, model), F32),
            jax.ShapeDtypeStruct((model // 256, 2, 8, rows), F32), flat,
            jax.ShapeDtypeStruct((rows, model), F32), jax.ShapeDtypeStruct((8, model), F32),
            jax.ShapeDtypeStruct((8, hidden_cols), F32), jax.ShapeDtypeStruct((total // 2, 2, 8, 128), F32),
            jax.ShapeDtypeStruct((own_rows, 3 * model), BF16),
        ],
        out_specs=[anywhere] * 11 + [inside] * 9,
        scratch_shapes=[
            letters, letters, pltpu.VMEM((8, model), F32),
            pltpu.VMEM((8, hidden_cols), F32), flat_s, turned_s, turned_s, flat_s, flat_s,
            flat_s, flat_s, flat_s, wide_s, wide_s, turned_s, flat_s, turned_s, wide_s,
            pltpu.VMEM((2,) + block + (1024,), BF16), pltpu.VMEM((2, 2) + block + (512,), BF16),
            dma((total,)), dma((total,)), dma((total,)), dma((total,)), dma((5,)), dma((4,)), dma((2, 3)),
            dma((count, line - 1)), dma((count, line - 1)), dma((count, 7)), dma((count, 7)),
            dma((2, 2)), dma((2, 2)),
        ],
        compiler_params=pltpu.CompilerParams(
            collective_id=cid, has_side_effects=True, vmem_limit_bytes=VMEM_LIMIT
        ),
        name="ahead",
    )(signals, ada, extra, *segments, tok, cot, kmask, qmask)


def behind_kernel(batches, line, width, levels, *refs):
    count = sum(len(batch) for batch in batches)
    (x_f, qkv_f, proj_f, g1_f, g2_f, result, ql_f, kl_f, vl_f, mix_f,
     gmid_ref, mod_ref, feed_rows, hidden_ref, stat_ref, boosts, kmask_ref, qmask_ref) = refs[:18]
    (gqkv_f, gproj_f, act_far, tok_far) = refs[18:22]
    landing = refs[22 : 22 + count]
    (t_qkv, t_proj, t_fc1, t_fc2, mods_ref, x_s) = refs[22 + count : 28 + count]
    rest = refs[28 + count :]
    first_b, second_b, line_b = rest[:count], rest[count : 2 * count], rest[2 * count : 3 * count]
    (core_s, own_s, ga_s, gat_s, onet_s, acc_s, turn_s, flat_s, w_s, grad_s, gm_s, vec_s, rows_ref, heads_s,
     a_send, a_recv, pair_sem, x_sem, w_sem, grad_sem,
     own_sem, load_sem, send_sem, recv_sem, z_send, z_recv) = rest[3 * count :]
    z, x, c, y = where_am_i()
    total = 8 * line
    padded, model = result.shape[0] // 2, result.shape[1]
    half_cols = model // 2
    heads = 256 // width
    partner = device(z, x, c, 1 - y)
    scatter = Scatter(
        batches, line, [gqkv_f, gproj_f, g1_f, g2_f], [t_qkv, t_proj, t_fc1, t_fc2], landing, core_s, own_s,
        first_b, second_b, line_b, (own_sem, load_sem, send_sem, recv_sem, z_send, z_recv),
    )
    ticks = Ticks(len(batches), scatter.stages())
    others = pl.ds((1 - y) * padded, padded)
    pairs = [
        remote(source.at[others], target, pair_sem.at[p, 0], pair_sem.at[p, 1], partner)
        for p, (source, target) in enumerate(((result, act_far), (x_s, tok_far)))
    ]
    load_x = pltpu.make_async_copy(x_f, x_s, x_sem.at[0])
    load_x.start()
    greet_all(total)
    ticks.run(0, 1)
    pairs[0].start()

    def load_group(i):
        half = lax.rem(i, 2)
        sub, at = i // 2, half * 2 + i // 2
        turned = pl.ds(pl.multiple_of(at * 256, 256), 256)
        cols = columns(at * 256, 256)
        pieces = [
            (qkv_f.at[half, :, :, :, :, columns(sub * 768, 768)], w_s.at[:, :, :, :, pl.ds(0, 768)]),
            (proj_f.at[half, :, :, :, :, columns(sub * 256, 256)], w_s.at[:, :, :, :, pl.ds(768, 256)]),
            (ql_f.at[turned], turn_s.at[0]),
            (kl_f.at[turned], turn_s.at[1]),
            (vl_f.at[:, cols], flat_s.at[0]),
            (mix_f.at[:, cols], flat_s.at[1]),
        ]
        return [pltpu.make_async_copy(s, t, w_sem.at[n]) for n, (s, t) in enumerate(pieces)]

    def store_group(i):
        half, sub = lax.rem(i, 2), i // 2
        return [
            pltpu.make_async_copy(
                grad_s.at[:, :, :, :, pl.ds(0, 768)], gqkv_f.at[half, :, :, :, :, columns(sub * 768, 768)],
                grad_sem.at[0],
            ),
            pltpu.make_async_copy(
                grad_s.at[:, :, :, :, pl.ds(768, 256)], gproj_f.at[half, :, :, :, :, columns(sub * 256, 256)],
                grad_sem.at[1],
            ),
        ]

    def start_loads(copies):
        for copy in copies:
            copy.start()

    def wait_loads(copies):
        for copy in copies:
            copy.wait()

    start_loads(load_group(0))
    ticks.run(1, 2)
    attend_grad = (mod_ref[0:1] * gmid_ref[...]).astype(BF16)
    ga_s[...] = attend_grad
    gat_s[...] = attend_grad.T
    vec_s[2:3] = jnp.sum(attend_grad.astype(F32), 0, keepdims=True)
    vec_s[3:4] = feed_rows[3:4]
    for part in range(4):
        vec_s[4 + part : 5 + part] = hidden_ref[0:1, part * model : (part + 1) * model]
    heads_s[...] = jnp.zeros_like(heads_s)
    lane = lax.broadcasted_iota(jnp.int32, (1, half_cols), 1)
    ticks.run(2, 3)
    load_x.wait()
    normed, _ = norm_rows(x_s[...].astype(F32))
    onet_s[...] = (normed * (1.0 + mod_ref[2:3]) + mod_ref[4:5]).astype(BF16).T
    acc_s[...] = jnp.zeros_like(acc_s)
    kmask, qmask = kmask_ref[...], qmask_ref[...]
    rows = kmask.shape[1]
    place = lax.broadcasted_iota(jnp.int32, (16, rows), 0)

    def pieces_of(row, first):
        high, mid, low = split_three(row)
        zero = jnp.zeros((16, rows), BF16)
        out = jnp.where(place == first, jnp.broadcast_to(high, zero.shape), zero)
        out = jnp.where(place == first + 1, jnp.broadcast_to(mid, zero.shape), out)
        return jnp.where(place == first + 2, jnp.broadcast_to(low, zero.shape), out)

    def group(i, carry):
        slot = lax.rem(i, 2)
        at = slot * 2 + i // 2

        wait_loads(load_group(i))
        boost = boosts[at]
        weights = w_s[...].reshape(model, 1024)
        mixed = flat_s[1]
        values = flat_s[0]
        q_all_low, k_all_low = turn_s[0], turn_s[1]
        mixed_grad = mm(ga_s[...], weights[:, 768:]).astype(BF16)
        mixed_turned, v_turned, q_plain = mixed_grad.T, values.T, q_all_low.T
        dq_rows, dk_rows, dv_cols, scales = [], [], [], []
        for head in range(heads):
            part = slice(head * width, (head + 1) * width)
            lift = boost[0:1, head : head + 1]
            q_bf, k_bf = q_all_low[part], k_all_low[part]
            q_float = q_bf.astype(F32)
            scaled = q_float * LOG2E
            high = scaled.astype(BF16)
            low = (scaled - high.astype(F32)).astype(BF16)
            log_total = stat_ref[at, 1, head : head + 1]
            q_all = jnp.concatenate([high, low, qmask + pieces_of(-log_total, levels + 1)], 0)
            k_all = jnp.concatenate([k_bf, k_bf, kmask], 0)
            soft = jnp.exp2(mm_tn(k_all, q_all))
            product = soft * mm_tn(v_turned[part], mixed_turned[part])
            delta = jnp.sum(product, 0, keepdims=True)
            scores_grad = (product - soft * delta).astype(BF16)
            dv_cols.append(mm(soft.astype(BF16), mixed_grad[:, part]))
            dq_low = mm(k_bf, scores_grad)
            dk_low = mm(scores_grad, q_plain[:, part]).T
            q_inv = stat_ref[at, 0, head : head + 1]
            k_inv = stat_ref[at, 0, heads + head : heads + head + 1]
            k_unit = k_bf.astype(F32)
            along = dq_low * q_float
            scales.append(jnp.sum(along, keepdims=True))
            dq_rows.append(
                q_inv * (dq_low * lift - q_float * (1.0 / lift) * jnp.sum(along, 0, keepdims=True))
            )
            dk_rows.append(k_inv * (dk_low - k_unit * jnp.sum(dk_low * k_unit, 0, keepdims=True)))
        dq = jnp.concatenate(dq_rows, 0).T.astype(BF16)
        dk = jnp.concatenate(dk_rows, 0).T.astype(BF16)
        dv = jnp.concatenate(dv_cols, 1).astype(BF16)
        triple = jnp.concatenate([dq, dk, dv], 1)

        @pl.when(i > 0)
        def _():
            wait_loads(store_group(i))

        switch_on(i, {1: lambda: ticks.run(4, 5), 2: lambda: ticks.run(5, 6)})
        shape = grad_s.shape[:4]
        grad_s[:, :, :, :, 0:768] = mm(onet_s[...], triple).astype(BF16).reshape(shape + (768,))
        grad_s[:, :, :, :, 768:1024] = mm(gat_s[...], mixed).astype(BF16).reshape(shape + (256,))
        start_loads(store_group(i))
        acc_s[...] += mm_nt(triple, weights[:, :768])
        spot = columns(at * 256, 256)
        vec_s[0:1, spot] = jnp.sum(dq.astype(F32), 0, keepdims=True)
        vec_s[1:2, spot] = jnp.sum(dv.astype(F32), 0, keepdims=True)
        for head in range(heads):
            heads_s[0:1] += jnp.where(lane == at * heads + head, scales[head], 0.0)

        @pl.when(i < 3)
        def _():
            start_loads(load_group(i + 1))

        switch_on(i, {0: lambda: ticks.run(3, 4)})
        return carry

    lax.fori_loop(0, 4, group, 0)
    wait_loads(store_group(3))
    ticks.run(6, 7)
    grad = acc_s[...]
    normed, inverse = norm_rows(x_s[...].astype(F32))
    x_s[...] = (
        gmid_ref[...] + norm_rows_back(grad * (1.0 + mod_ref[2:3]), normed, inverse)
    ).astype(BF16)
    pairs[1].start()
    rows_ref[0:1] = jnp.sum(grad * normed, 0, keepdims=True)
    rows_ref[1:2] = jnp.sum(grad, 0, keepdims=True)
    owners = total // 2
    spread, owner_of = owner_maps(owners, width // owners, width, model)
    picked = jnp.concatenate([owner_of * vec_s[r : r + 1] for r in range(8)], 0)
    moved = sum(mm_nt(part, spread) for part in split_three(picked))
    small = jnp.concatenate([moved[r * owners : (r + 1) * owners] for r in range(8)], 1)
    mod_rows = (feed_rows[4:5], feed_rows[0:1], rows_ref[0:1], feed_rows[1:2], rows_ref[1:2], feed_rows[2:3])
    for half in range(2):
        for n, row in enumerate(mod_rows):
            gm_s[:, half, n, :] = jnp.broadcast_to(
                row[:, half * half_cols : (half + 1) * half_cols], (owners, half_cols)
            )
        gm_s[:, half, 6, :] = small
        gm_s[:, half, 7, :] = jnp.broadcast_to(heads_s[0:1], (owners, half_cols))
    exchange = Exchange(total, lambda to: gm_s.at[to // 2, to % 2], mods_ref.at[lax.axis_index("dp"), y], a_send, a_recv)
    exchange.start()
    ticks.run(7, ticks.total)
    exchange.wait()
    wait_loads(pairs)
    scatter.sent()


def run_behind(batches, line, levels, saved, inner, width, cid):
    x_f, qkv_f, proj_f, g1_f, g2_f, result, ql, kl, vl, mix = saved
    rows, model = x_f.shape
    chunks = [chunk for batch in batches for chunk in batch]
    total, count = 8 * line, len(chunks)
    own_rows = qkv_f.shape[4]
    anywhere, inside = pl.BlockSpec(memory_space=pl.ANY), pl.BlockSpec(memory_space=pltpu.VMEM)
    dma = pltpu.SemaphoreType.DMA
    landing, first_b, second_b, line_b = [], [], [], []
    for _, kind, _, cols in chunks:
        landing.append(jax.ShapeDtypeStruct((2, line, 2, own_rows, cols), BF16))
        first_b.append(pltpu.VMEM(((line, 2) if kind == 0 else (2, line)) + (own_rows, cols), BF16))
        second_b.append(pltpu.VMEM((line, own_rows, cols), BF16))
        line_b.append(pltpu.VMEM((line - 1, own_rows, cols), BF16))
    most = max(sum(chunk[3] for chunk in batch) for batch in batches)
    sources = [qkv_f, proj_f, g1_f, g2_f]
    block = (line, 2, 2, own_rows)
    made = pl.pallas_call(
        functools.partial(behind_kernel, batches, line, width, levels),
        in_specs=[anywhere] * 10 + [inside] * 8,
        out_shape=[jax.ShapeDtypeStruct(qkv_f.shape, BF16), jax.ShapeDtypeStruct(proj_f.shape, BF16)]
        + [jax.ShapeDtypeStruct((rows // 2, model), BF16)] * 2 + landing
        + [jax.ShapeDtypeStruct(s.shape[4:], F32) for s in sources]
        + [jax.ShapeDtypeStruct((total // 2, 2, 8, model // 2), F32), jax.ShapeDtypeStruct((rows, model), BF16)],
        out_specs=[anywhere] * (4 + count) + [inside] * 6,
        scratch_shapes=first_b + second_b + line_b + [
            pltpu.VMEM((3, 2, line, 2, own_rows, most), BF16), pltpu.VMEM((2, 2, line, 2, own_rows, most), BF16),
            pltpu.VMEM((rows, model), BF16), pltpu.VMEM((model, rows), BF16),
            pltpu.VMEM((model, rows), BF16), pltpu.VMEM((rows, model), F32), pltpu.VMEM((2, 256, rows), BF16),
            pltpu.VMEM((2, rows, 256), BF16), pltpu.VMEM(block + (1024,), BF16),
            pltpu.VMEM(block + (1024,), BF16), pltpu.VMEM((total // 2, 2, 8, model // 2), F32), pltpu.VMEM((8, model), F32), pltpu.VMEM((8, model), F32),
            pltpu.VMEM((8, model // 2), F32),
            dma((total,)), dma((total,)), dma((2, 2)), dma((1,)), dma((6,)), dma((2,)),
            dma((count,)), dma((count,)), dma((count, 3)), dma((count, 3)),
            dma((count, line - 1)), dma((count, line - 1)),
        ],
        compiler_params=pltpu.CompilerParams(
            collective_id=cid, has_side_effects=True, vmem_limit_bytes=VMEM_LIMIT
        ),
        name="behind",
    )(*saved, *inner)
    return made[2], made[3], made[4 + count :]


def pad_rows(values, padded):
    return jnp.pad(values, ((0, 0), (0, padded - values.shape[1]), (0, 0)))


def gather_list():
    def both(segment, start, cols):
        return [(segment, 0, start, cols, 0, 16), (segment, 1, start, cols, 16, 48)]

    attend = [both(0, 0, 512), both(0, 512, 256) + both(1, 0, 256), both(0, 768, 768) + both(1, 256, 256)]
    return attend + [
        [(2, 0, part * 512, 384, 0, 64), (2, 1, part * 512 + 384, 128, 0, 64), (3, 1, part * 512, 512, 0, 64)]
        for part in range(4)
    ]


def scatter_list():
    feed = [[(s, 0, 0, 128), (s, 1, 128, 384)] for s in (2, 3)]
    feed += [
        [(2, 0, part * 512, 384), (2, 1, part * 512 + 384, 128), (3, 1, part * 512, 512)] for part in range(1, 4)
    ]
    attend = [[(0, 0, 0, 256), (0, 1, 256, 512), (1, 1, 0, 256)], [(0, 0, 768, 256), (0, 1, 1024, 512)]]
    return feed + attend + [[(1, 0, 256, 128), (1, 1, 384, 128)]]


def on_device_paired(
    tokens, condition, scale_lengths, order, cotangent, ada_weight, ada_bias, qkv_weight, qv_bias,
    head_log_scale, proj_weight, out_bias, fc1_weight, fc1_bias, fc2_weight,
):
    n_dp, mine = lax.axis_size("dp"), lax.axis_index("mp")
    line = n_dp // 4
    slots, half_rows, model = tokens.shape
    padded = -(-half_rows // 16) * 16
    rows = 2 * padded
    local_heads, width = qv_bias.shape[1], 64
    own_cols = qkv_weight.shape[2]
    own_rows = qkv_weight.shape[1]
    hidden_cols = fc1_weight.shape[1]
    groups = 2 * own_cols // 256
    swap = order[0, 0] != 0
    entries = qv_bias.shape[2]
    vectors = 4 * local_heads + fc1_bias.shape[0]
    scale_at = vectors * entries
    n_dev = 2 * n_dp

    def to_slots(values):
        return jnp.stack([jnp.where(swap, values[1], values[0]), jnp.where(swap, values[0], values[1])])

    cond_slots = to_slots(condition).astype(F32)
    signal = jax.nn.silu(cond_slots).astype(BF16)
    signals = signal.reshape(slots, n_dp, own_rows).transpose(1, 0, 2).astype(F32)
    signals = jnp.pad(signals, ((0, 0), (0, 8 - slots), (0, 128 - own_rows)))
    bias_own = lax.dynamic_update_slice(
        jnp.zeros((6, local_heads, width), F32), ada_bias.astype(F32), (0, 0, lax.axis_index("dp") * entries)
    ).reshape(6, own_cols)
    small = jnp.concatenate([qv_bias.reshape(-1), out_bias.reshape(-1), fc1_bias.reshape(-1)]).astype(F32)
    extra = jnp.concatenate(
        [bias_own, jnp.pad(small, (0, own_cols - scale_at))[None], jnp.pad(head_log_scale, (0, own_cols - local_heads))[None]]
    )

    lengths = lax.dynamic_index_in_dim(to_slots(scale_lengths), mine, 0, keepdims=False)
    kmask, qmask = build_masks(lengths, half_rows, padded)
    segments = [
        qkv_weight.reshape(3, own_rows, 2, 256).transpose(1, 2, 0, 3).reshape(own_rows, 3 * own_cols),
        proj_weight.T, fc1_weight, fc2_weight.T,
    ]
    (qkv_f, proj_f, _, _, g1_f, g2_f, q_low, k_low, v_low, mixed, x_f, boosts, mods, stats, result, grad_middle,
     feed_rows, g_hidden, sig_all, ada_flat) = run_ahead(
        gather_list(), line, signals, ada_weight, extra, segments, pad_rows(to_slots(tokens), padded),
        pad_rows(cotangent, padded), kmask, qmask, 2 * hidden_cols, width, 1,
    )
    act_far, tok_far, (t_qkv, t_proj, t_fc1, t_fc2, arrived, token_grad) = run_behind(
        scatter_list(), line, scale_lengths.shape[1],
        [x_f, qkv_f, proj_f, g1_f, g2_f, result, q_low, k_low, v_low, mixed],
        [grad_middle, mods, feed_rows, g_hidden, stats, boosts, kmask, qmask], width, 2,
    )
    qkv_total = t_qkv.reshape(own_rows, 2, 3, 256).transpose(2, 0, 1, 3).reshape(qkv_weight.shape)

    def both_slots(image, far, swapped):
        near = jnp.where(mine == 0, image[:half_rows], image[padded : padded + half_rows])
        first = (mine == 0) != swapped
        return jnp.stack([jnp.where(first, near, far[:half_rows]), jnp.where(first, far[:half_rows], near)])

    activations = both_slots(result, act_far, False)
    tokens_grad = both_slots(token_grad, tok_far, swap)

    all_mods = arrived[:, :, :6].reshape(n_dev, 6 * own_cols)
    signal_part = lax.dot_general(
        all_mods, ada_flat.astype(F32), (((1,), (1,)), ((), ())), precision=precise, preferred_element_type=F32
    ).reshape(n_dp, 1, slots * own_rows)
    signal_part = jnp.broadcast_to(signal_part, (n_dp, 2, slots * own_rows)).reshape(n_dev, slots * own_rows)
    signal_part = lax.all_to_all(signal_part, ("dp", "mp"), 0, 0, tiled=True)
    signal_grad = signal_part.reshape(n_dp, 2, slots, own_rows).sum(1).transpose(1, 0, 2).reshape(slots, model)
    signal_rows = sig_all[:, 0, :slots, :own_rows].reshape(n_dev, own_rows)
    ada_weight_grad = lax.dot_general(
        signal_rows, all_mods, (((0,), (0,)), ((), ())), precision=precise, preferred_element_type=F32
    ).reshape(ada_weight.shape)
    small_total = arrived[:, :, 6:].sum((0, 1))
    by_head = small_total[0].reshape(8, 2 * local_heads, entries)
    bias_total = lax.dynamic_slice_in_dim(by_head[:4], mine * local_heads, local_heads, 1)
    hidden_total = lax.dynamic_slice_in_dim(by_head[4:], mine * 2, 2, 0).reshape(fc1_bias.shape)
    scale_total = lax.dynamic_slice_in_dim(small_total[1], mine * local_heads, local_heads, 0)
    ada_bias_grad = lax.dynamic_slice_in_dim(
        jnp.sum(all_mods, 0).reshape(6, local_heads, width), lax.axis_index("dp") * entries, entries, 2
    )
    pull = jax.vjp(jax.nn.silu, cond_slots)[1]
    condition_grad = to_slots(pull(signal_grad)[0]).astype(BF16)
    return (
        activations, tokens_grad, condition_grad, ada_weight_grad, ada_bias_grad, qkv_total, bias_total[:2],
        scale_total, t_proj.T, bias_total[2:], t_fc1, hidden_total, t_fc2.T,
    )


precise = lax.Precision.HIGHEST


def row_norm(values):
    centre = jnp.mean(values, -1, keepdims=True)
    shifted = values - centre
    inverse = lax.rsqrt(jnp.mean(shifted * shifted, -1, keepdims=True) + 1e-06)
    return (shifted * inverse, inverse)


def row_norm_back(incoming, normed, inverse):
    return inverse * (
        incoming
        - jnp.mean(incoming, -1, keepdims=True)
        - normed * jnp.mean(incoming * normed, -1, keepdims=True)
    )


def gelu_tanh(values):
    return jax.nn.gelu(values, approximate=True)


def spread(shard_rows):
    return lax.all_gather(shard_rows, "mp", axis=0, tiled=True)


def collect(partial_sum):
    return lax.psum_scatter(
        partial_sum.astype(jnp.bfloat16), "mp", scatter_dimension=0, tiled=True
    ).astype(jnp.float32)


def fetch(qkv_weight, qv_bias, proj_weight, out_bias, fc1_weight, fc1_bias, fc2_weight):
    return (
        lax.all_gather(qkv_weight, "dp", axis=1, tiled=True),
        lax.all_gather(qv_bias, "dp", axis=2, tiled=True),
        lax.all_gather(proj_weight, "dp", axis=1, tiled=True),
        lax.all_gather(out_bias, "dp", axis=2, tiled=True),
        lax.all_gather(fc1_weight, "dp", axis=0, tiled=True),
        lax.all_gather(fc1_bias, "dp", axis=1, tiled=True),
        lax.all_gather(fc2_weight, "dp", axis=1, tiled=True),
    )


def settle(grad_set):
    qkv_part, qv_part, proj_part, outb_part, fc1_part, fc1b_part, fc2_part = grad_set
    return (
        lax.psum_scatter(
            qkv_part.astype(jnp.bfloat16), "dp", scatter_dimension=1, tiled=True
        ).astype(jnp.float32),
        lax.psum_scatter(
            qv_part.astype(jnp.bfloat16), "dp", scatter_dimension=2, tiled=True
        ).astype(jnp.float32),
        lax.psum_scatter(
            proj_part.astype(jnp.bfloat16), "dp", scatter_dimension=1, tiled=True
        ).astype(jnp.float32),
        lax.psum_scatter(
            outb_part.astype(jnp.bfloat16), "dp", scatter_dimension=2, tiled=True
        ).astype(jnp.float32),
        lax.psum_scatter(
            fc1_part.astype(jnp.bfloat16), "dp", scatter_dimension=0, tiled=True
        ).astype(jnp.float32),
        lax.psum_scatter(
            fc1b_part.astype(jnp.bfloat16), "dp", scatter_dimension=1, tiled=True
        ).astype(jnp.float32),
        lax.psum_scatter(
            fc2_part.astype(jnp.bfloat16), "dp", scatter_dimension=1, tiled=True
        ).astype(jnp.float32),
    )


def on_device_shared(
    tokens,
    condition,
    scale_lengths,
    order,
    cotangent,
    ada_weight,
    ada_bias,
    qkv_weight,
    qv_bias,
    head_log_scale,
    proj_weight,
    out_bias,
    fc1_weight,
    fc1_bias,
    fc2_weight,
):
    image_count, shard_rows, model_width = tokens.shape
    column_count = qkv_weight.shape[2]
    local_heads = qv_bias.shape[1]
    head_width = column_count // local_heads
    hidden_cols = fc1_weight.shape[1]
    own_start = lax.axis_index("mp") * column_count
    token_count = shard_rows * lax.axis_size("mp")
    ada_full, ada_bias_full = (
        lax.all_gather(ada_weight, "dp", axis=0, tiled=True),
        lax.all_gather(ada_bias, "dp", axis=2, tiled=True),
    )
    cond_float = condition.astype(jnp.float32)
    signal = jax.nn.silu(cond_float).astype(jnp.bfloat16)
    ada_flat = ada_full.reshape(model_width, 6 * column_count)
    mod_share = jnp.dot(
        signal, ada_flat, preferred_element_type=jnp.float32
    ) + ada_bias_full.reshape(6 * column_count).astype(jnp.float32)
    modulation = lax.all_gather(
        mod_share.reshape(image_count, 6, column_count), "mp", axis=2, tiled=True
    )
    head_boost = jnp.exp(head_log_scale)[None, :, None]
    positions = jnp.arange(token_count, dtype=jnp.int32)

    def place(vector):
        return lax.dynamic_update_slice(
            jnp.zeros((model_width,), jnp.float32), vector, (own_start,)
        )

    def own_columns(matrix):
        return lax.dynamic_slice_in_dim(matrix, own_start, column_count, 1)

    def rows_now():
        return fetch(qkv_weight, qv_bias, proj_weight, out_bias, fc1_weight, fc1_bias, fc2_weight)

    full_shapes = (
        (3, model_width, column_count),
        (2, local_heads, head_width),
        (column_count, model_width),
        (2, local_heads, head_width),
        (model_width, hidden_cols),
        (hidden_cols // head_width, head_width),
        (hidden_cols, model_width),
    )
    grad_start = tuple((jnp.zeros(shape_item, jnp.float32) for shape_item in full_shapes))

    def micro_step(micro_at, state_now):
        outputs, token_grads, mod_grads, weight_grads, scale_grad = state_now
        image_at = order[0, micro_at]
        residual = lax.dynamic_index_in_dim(tokens, image_at, 0, keepdims=False).astype(jnp.float32)
        image_mods = lax.dynamic_index_in_dim(modulation, image_at, 0, keepdims=False)
        lengths = lax.dynamic_index_in_dim(scale_lengths, image_at, 0, keepdims=False)
        out_grad = lax.dynamic_index_in_dim(cotangent, micro_at, 0, keepdims=False).astype(
            jnp.float32
        )
        qkv_full, qv_full, proj_full, outb_full, fc1_full, fc1b_full, fc2_full = rows_now()
        steps = jnp.arange(lengths.shape[0], dtype=jnp.int32)
        scale_ends = jnp.sum(jnp.where(steps[None, :] <= steps[:, None], lengths[None, :], 0), 1)
        scale_of = jnp.sum((positions[:, None] >= scale_ends[None, :]).astype(jnp.int32), 1)
        allowed = (scale_of[None, :] <= scale_of[:, None])[None]
        normed_one, inverse_one = row_norm(residual)
        input_one = spread(
            (normed_one * (1.0 + image_mods[2]) + image_mods[4]).astype(jnp.bfloat16)
        )
        projected = jnp.einsum(
            "td,cde->cte", input_one, qkv_full, preferred_element_type=jnp.float32
        )
        bias_pair = qv_full.reshape(2, column_count).astype(jnp.float32)
        queries = (projected[0] + bias_pair[0]).reshape(token_count, local_heads, head_width)
        keys_raw = projected[1].reshape(token_count, local_heads, head_width)
        values_low = (
            (projected[2] + bias_pair[1])
            .astype(jnp.bfloat16)
            .reshape(token_count, local_heads, head_width)
        )
        query_inv = lax.rsqrt(jnp.sum(queries * queries, -1, keepdims=True) + 1e-06)
        key_inv = lax.rsqrt(jnp.sum(keys_raw * keys_raw, -1, keepdims=True) + 1e-06)
        query_unit = queries * query_inv
        key_unit = keys_raw * key_inv
        query_low = (query_unit * head_boost).astype(jnp.bfloat16)
        key_low = key_unit.astype(jnp.bfloat16)

        def masked_scores():
            raw_scores = jnp.einsum(
                "qhd,khd->hqk", query_low, key_low, preferred_element_type=jnp.float32
            )
            return jnp.where(allowed, raw_scores, -1e30)

        scores = masked_scores()
        row_peak = jnp.max(scores, -1, keepdims=True)
        exp_terms = jnp.exp(scores - row_peak)
        totals = jnp.sum(exp_terms, -1, keepdims=True)
        log_total = row_peak + jnp.log(totals)
        soft_weights = exp_terms / totals
        mixed_heads = (
            jnp.einsum(
                "hqk,khd->qhd",
                soft_weights.astype(jnp.bfloat16),
                values_low,
                preferred_element_type=jnp.float32,
            )
            .astype(jnp.bfloat16)
            .reshape(token_count, column_count)
        )
        attended = collect(
            jnp.dot(mixed_heads, proj_full, preferred_element_type=jnp.float32)
            + place(outb_full[0].reshape(column_count).astype(jnp.float32))
        )
        middle = residual + image_mods[0] * attended
        normed_two, inverse_two = row_norm(middle)
        input_two = spread(
            (normed_two * (1.0 + image_mods[3]) + image_mods[5]).astype(jnp.bfloat16)
        )
        hidden = jnp.dot(
            input_two, fc1_full, preferred_element_type=jnp.float32
        ) + fc1b_full.reshape(hidden_cols).astype(jnp.float32)
        activated = gelu_tanh(hidden).astype(jnp.bfloat16)
        branch_out = collect(
            jnp.dot(activated, fc2_full, preferred_element_type=jnp.float32)
            + place(outb_full[1].reshape(column_count).astype(jnp.float32))
        )
        result = (middle + image_mods[1] * branch_out).astype(jnp.bfloat16)
        outputs = lax.dynamic_update_index_in_dim(outputs, result, micro_at, 0)
        qkv_back, qv_back, proj_back, outb_back, fc1_back, fc1b_back, fc2_back = rows_now()
        grad_branch = spread((image_mods[1] * out_grad).astype(jnp.bfloat16))
        gamma_two_grad = jnp.sum(out_grad * branch_out, 0)
        fc2_grad = jnp.dot(activated.T, grad_branch, preferred_element_type=jnp.float32)
        bias_two_grad = jnp.sum(own_columns(grad_branch).astype(jnp.float32), 0)
        act_grad = jnp.dot(grad_branch, fc2_back.T, preferred_element_type=jnp.float32)
        gelu_pull = jax.vjp(gelu_tanh, hidden)[1]
        hidden_grad = gelu_pull(act_grad)[0].astype(jnp.bfloat16)
        fc1_grad = jnp.dot(input_two.T, hidden_grad, preferred_element_type=jnp.float32)
        fc1b_grad = jnp.sum(hidden_grad.astype(jnp.float32), 0).reshape(
            hidden_cols // head_width, head_width
        )
        input_two_grad = collect(
            jnp.dot(hidden_grad, fc1_back.T, preferred_element_type=jnp.float32)
        )
        scale_two_grad = jnp.sum(input_two_grad * normed_two, 0)
        shift_two_grad = jnp.sum(input_two_grad, 0)
        middle_grad = out_grad + row_norm_back(
            input_two_grad * (1.0 + image_mods[3]), normed_two, inverse_two
        )
        grad_attended = spread((image_mods[0] * middle_grad).astype(jnp.bfloat16))
        gamma_one_grad = jnp.sum(middle_grad * attended, 0)
        proj_grad = jnp.dot(mixed_heads.T, grad_attended, preferred_element_type=jnp.float32)
        bias_one_grad = jnp.sum(own_columns(grad_attended).astype(jnp.float32), 0)
        mixed_grad = (
            jnp.dot(grad_attended, proj_back.T, preferred_element_type=jnp.float32)
            .astype(jnp.bfloat16)
            .reshape(token_count, local_heads, head_width)
        )
        soft_again = jnp.exp(masked_scores() - log_total)
        value_grad = jnp.einsum(
            "hqk,qhd->khd",
            soft_again.astype(jnp.bfloat16),
            mixed_grad,
            preferred_element_type=jnp.float32,
        )
        soft_grad = jnp.einsum(
            "qhd,khd->hqk", mixed_grad, values_low, preferred_element_type=jnp.float32
        )
        score_grad = (
            soft_again * (soft_grad - jnp.sum(soft_again * soft_grad, -1, keepdims=True))
        ).astype(jnp.bfloat16)
        query_low_grad = jnp.einsum(
            "hqk,khd->qhd", score_grad, key_low, preferred_element_type=jnp.float32
        )
        key_low_grad = jnp.einsum(
            "hqk,qhd->khd", score_grad, query_low, preferred_element_type=jnp.float32
        )
        head_grad = jnp.sum(query_low_grad * query_unit * head_boost, (0, 2))
        query_unit_grad = query_low_grad * head_boost
        query_grad = query_inv * (
            query_unit_grad - query_unit * jnp.sum(query_unit_grad * query_unit, -1, keepdims=True)
        )
        key_grad = key_inv * (
            key_low_grad - key_unit * jnp.sum(key_low_grad * key_unit, -1, keepdims=True)
        )
        triple_grad = jnp.stack(
            [
                query_grad.reshape(token_count, column_count),
                key_grad.reshape(token_count, column_count),
                value_grad.reshape(token_count, column_count),
            ]
        ).astype(jnp.bfloat16)
        qkv_grad = jnp.einsum(
            "td,cte->cde", input_one, triple_grad, preferred_element_type=jnp.float32
        )
        pair_sums = jnp.sum(triple_grad.astype(jnp.float32), 1)
        qv_grad = jnp.stack([pair_sums[0], pair_sums[2]]).reshape(2, local_heads, head_width)
        input_one_grad = collect(
            jnp.einsum("cte,cde->td", triple_grad, qkv_back, preferred_element_type=jnp.float32)
        )
        scale_one_grad = jnp.sum(input_one_grad * normed_one, 0)
        shift_one_grad = jnp.sum(input_one_grad, 0)
        residual_grad = middle_grad + row_norm_back(
            input_one_grad * (1.0 + image_mods[2]), normed_one, inverse_one
        )
        token_grads = lax.dynamic_update_index_in_dim(
            token_grads, residual_grad.astype(jnp.bfloat16), image_at, 0
        )
        image_mod_grad = jnp.stack(
            [
                gamma_one_grad,
                gamma_two_grad,
                scale_one_grad,
                scale_two_grad,
                shift_one_grad,
                shift_two_grad,
            ]
        )
        mod_grads = lax.dynamic_update_index_in_dim(mod_grads, image_mod_grad, image_at, 0)
        outb_grad = jnp.stack([bias_one_grad, bias_two_grad]).reshape(2, local_heads, head_width)
        local_grads = (qkv_grad, qv_grad, proj_grad, outb_grad, fc1_grad, fc1b_grad, fc2_grad)
        weight_grads = tuple(
            (running + addend for running, addend in zip(weight_grads, local_grads))
        )
        return (outputs, token_grads, mod_grads, weight_grads, scale_grad + head_grad)

    start_state = (
        jnp.zeros(tokens.shape, jnp.bfloat16),
        jnp.zeros(tokens.shape, jnp.bfloat16),
        jnp.zeros((image_count, 6, model_width), jnp.float32),
        grad_start,
        jnp.zeros((local_heads,), jnp.float32),
    )
    outputs, token_grads, mod_grads, weight_grads, scale_grad = lax.fori_loop(
        0, image_count, micro_step, start_state
    )
    shard_grads = settle(weight_grads)
    mod_share_grad = lax.psum_scatter(
        mod_grads.astype(jnp.bfloat16), "mp", scatter_dimension=2, tiled=True
    ).astype(jnp.float32)
    flat_grad = mod_share_grad.reshape(image_count, 6 * column_count)
    ada_grad = jnp.dot(
        signal.astype(jnp.float32).T,
        flat_grad,
        precision=precise,
        preferred_element_type=jnp.float32,
    ).reshape(model_width, 6, column_count)
    ada_bias_grad = jnp.sum(mod_share_grad, 0).reshape(6, local_heads, head_width)
    signal_grad = lax.psum(
        jnp.dot(
            flat_grad,
            ada_flat.astype(jnp.float32).T,
            precision=precise,
            preferred_element_type=jnp.float32,
        ),
        "mp",
    )
    silu_pull = jax.vjp(jax.nn.silu, cond_float)[1]
    condition_grad = silu_pull(signal_grad)[0].astype(jnp.bfloat16)
    ada_shard, ada_bias_shard = (
        lax.psum_scatter(
            ada_grad.astype(jnp.bfloat16), "dp", scatter_dimension=0, tiled=True
        ).astype(jnp.float32),
        lax.psum_scatter(
            ada_bias_grad.astype(jnp.bfloat16), "dp", scatter_dimension=2, tiled=True
        ).astype(jnp.float32),
    )
    head_scale_grad = lax.psum(scale_grad, "dp")
    qkv_shard, qv_shard, proj_shard, outb_shard, fc1_shard, fc1b_shard, fc2_shard = shard_grads
    return (
        outputs,
        token_grads,
        condition_grad,
        ada_shard,
        ada_bias_shard,
        qkv_shard,
        qv_shard,
        head_scale_grad,
        proj_shard,
        outb_shard,
        fc1_shard,
        fc1b_shard,
        fc2_shard,
    )


def solution(mesh):
    in_specs = (
        P("dp", "mp", None),
        P("dp", None),
        P("dp", None),
        P("dp", None),
        P("dp", "mp", None),
        P("dp", None, "mp"),
        P(None, "mp", "dp"),
        P(None, "dp", "mp"),
        P(None, "mp", "dp"),
        P("mp"),
        P("mp", "dp"),
        P(None, "mp", "dp"),
        P("dp", "mp"),
        P("mp", "dp"),
        P("mp", "dp"),
    )
    out_specs = (
        P("dp", "mp", None),
        P("dp", "mp", None),
        P("dp", None),
        P("dp", None, "mp"),
        P(None, "mp", "dp"),
        P(None, "dp", "mp"),
        P(None, "mp", "dp"),
        P("mp"),
        P("mp", "dp"),
        P(None, "mp", "dp"),
        P("dp", "mp"),
        P("mp", "dp"),
        P("mp", "dp"),
    )
    line, spare = divmod(mesh.shape["dp"], 4)
    paired = mesh.shape["mp"] == 2 and spare == 0 and line > 1
    return jax.shard_map(
        on_device_paired if paired else on_device_shared, mesh=mesh, in_specs=in_specs, out_specs=out_specs, check_vma=False
    )
```

```python
import functools
import jax
import jax.numpy as jnp
from jax import lax
from jax.experimental import pallas as pl
from jax.experimental.pallas import tpu as pltpu
from jax.sharding import PartitionSpec as P

F32 = jnp.float32
BF16 = jnp.bfloat16
MESH = pl.DeviceIdType.MESH
LOG2E = 1.4426950408889634
VMEM_LIMIT = 60 * 1024 * 1024


def mm(a, b):
    return jnp.dot(a, b, preferred_element_type=F32)


def mm_nt(a, b):
    return lax.dot_general(a, b, (((1,), (1,)), ((), ())), preferred_element_type=F32)


def mm_tn(a, b):
    return lax.dot_general(a, b, (((0,), (0,)), ((), ())), preferred_element_type=F32)


def norm_rows(values):
    centre = jnp.mean(values, -1, keepdims=True)
    shifted = values - centre
    inverse = lax.rsqrt(jnp.mean(shifted * shifted, -1, keepdims=True) + 1e-06)
    return shifted * inverse, inverse


def norm_rows_back(incoming, normed, inverse):
    return inverse * (
        incoming
        - jnp.mean(incoming, -1, keepdims=True)
        - normed * jnp.mean(incoming * normed, -1, keepdims=True)
    )


def split_three(values):
    high = values.astype(BF16)
    rest = values - high.astype(F32)
    middle = rest.astype(BF16)
    return high, middle, (rest - middle.astype(F32)).astype(BF16)


def build_masks(lengths, half_rows, padded):
    count = lengths.shape[0]
    steps = jnp.arange(count, dtype=jnp.int32)
    ends = jnp.sum(jnp.where(steps[None, :] <= steps[:, None], lengths[None, :], 0), 1)
    place = jnp.arange(2 * padded, dtype=jnp.int32)
    part, inside = place // padded, place % padded
    token = part * half_rows + inside
    level = jnp.sum((token[None, :] >= ends[:, None]).astype(jnp.int32), 0)
    real = inside < half_rows
    entry = jnp.arange(16, dtype=jnp.int32)[:, None]
    key_level = jnp.where(real, level, count)[None]
    kmask = (entry == key_level) | ((entry > count) & (entry < count + 4))
    query_level = jnp.where(real, level, count - 1)[None]
    qmask = (entry > query_level) & (entry <= count)
    return kmask.astype(BF16), jnp.where(qmask, -32768.0, 0.0).astype(BF16)


def device(z, x, c, y):
    return (z * 4 + x * 2 + c, y)


def where_am_i():
    dp, y = lax.axis_index("dp"), lax.axis_index("mp")
    return dp // 4, (dp // 2) % 2, dp % 2, y


def remote(source, target, send, recv, to):
    return pltpu.make_async_remote_copy(source, target, send, recv, device_id=to, device_id_type=MESH)


def greet_all(total):
    me = lax.axis_index("dp") * 2 + lax.axis_index("mp")
    barrier = pltpu.get_barrier_semaphore()

    def signal(step, carry):
        to = lax.rem(me + step, total)
        pl.semaphore_signal(barrier, inc=1, device_id=(to // 2, to % 2), device_id_type=MESH)
        return carry

    lax.fori_loop(1, total, signal, 0)
    pl.semaphore_wait(barrier, total - 1)


class Exchange:
    def __init__(self, total, block_of, landing, send, recv):
        self.total, self.block_of, self.landing, self.send, self.recv = total, block_of, landing, send, recv
        self.me = lax.axis_index("dp") * 2 + lax.axis_index("mp")

    def copy(self, step):
        to = lax.rem(self.me + step, self.total)
        return remote(
            self.block_of(to), self.landing, self.send.at[step], self.recv.at[step], (to // 2, to % 2)
        )

    def own(self):
        return pltpu.make_async_copy(self.block_of(self.me), self.landing, self.send.at[0])

    def each(self, act):
        def body(step, carry):
            act(self.copy(step))
            return carry

        lax.fori_loop(1, self.total, body, 0)

    def start(self):
        self.own().start()
        self.each(lambda copy: copy.start())

    def wait(self):
        self.own().wait()
        self.each(lambda copy: copy.wait())


class Ticks:
    def __init__(self, count, stages, offsets):
        self.count, self.stages, self.offsets = count, stages, offsets
        self.total = count + offsets[-1]

    def run(self, since, until):
        for tick in range(since, until):
            for stage, offset in zip(self.stages, self.offsets):
                if 0 <= tick - offset < self.count:
                    stage(tick - offset)


class Gather:
    def __init__(self, batches, line, sources, outs, z_send, z_recv, send_sem, recv_sem):
        self.batches, self.line, self.sources, self.outs = batches, line, sources, outs
        self.chunks = [chunk for batch in batches for chunk in batch]
        self.z_send, self.z_recv, self.send_sem, self.recv_sem = z_send, z_recv, send_sem, recv_sem
        self.z, self.x, self.c, self.y = where_am_i()
        z, x, c, y = self.z, self.x, self.c, self.y
        self.x_side, self.y_side, self.sibling = device(z, 1 - x, c, y), device(z, x, c, 1 - y), device(z, x, 1 - c, y)

    def part(self, k, yy, zz, xx):
        seg, _, start, cols, row, rows = self.chunks[k]
        return self.outs[seg].at[yy, zz, xx, self.c, pl.ds(row, rows), pl.ds(start, cols)]

    def late(self, k):
        return self.chunks[k][1] >= 2

    def mine(self, k):
        seg, _, start, cols, row, rows = self.chunks[k]
        return self.sources[seg].at[pl.ds(row, rows), pl.ds(start, cols)]

    def plane(self, k, owner):
        return self.part(k, slice(None), owner, slice(None))

    def along(self, k, step):
        to = device(lax.rem(self.z + step, self.line), self.x, self.c, self.y)
        sems = (self.z_send.at[k, step - 1], self.z_recv.at[k, step - 1])
        if self.late(k):
            return remote(self.plane(k, self.z), self.plane(k, self.z), *sems, to)
        return remote(self.mine(k), self.part(k, self.y, self.z, self.x), *sems, to)

    def group(self, k, slot, at, target):
        ref = self.part(k, at[0], self.z if self.late(k) else slice(None), at[1])
        source = self.mine(k) if self.late(k) and slot < 2 else ref
        return remote(source, ref, self.send_sem.at[k, slot], self.recv_sem.at[k, slot], target)

    def aside(self, k, step):
        ref = self.plane(k, lax.rem(self.z + self.line - step, self.line))
        return remote(ref, ref, self.send_sem.at[k, 3 + step], self.recv_sem.at[k, 3 + step], self.sibling)

    def groups(self, k):
        x, y = self.x, self.y
        if self.chunks[k][1] % 2 == 0:
            return [(y, x), (y, 1 - x), (1 - y, x), (1 - y, 1 - x)], self.x_side, self.y_side
        return [(y, x), (1 - y, x), (y, 1 - x), (1 - y, 1 - x)], self.y_side, self.x_side

    def step(self, k, stage):
        order, first, second = self.groups(k)
        if self.late(k):
            if stage == 0:
                self.group(k, 0, order[0], first).start()
                self.group(k, 1, order[0], second).start()
            elif stage == 1:
                self.group(k, 0, order[1], first).wait_recv()
                self.group(k, 2, order[1], second).start()
            elif stage == 2:
                self.group(k, 1, order[2], second).wait_recv()
                self.group(k, 2, order[3], second).wait_recv()
                for step in range(1, self.line):
                    self.along(k, step).start()
                self.aside(k, 0).start()
            else:
                for step in range(1, self.line):
                    self.along(k, step).wait_recv()
                    self.aside(k, step).start()
        elif stage == 0:
            for step in range(1, self.line):
                self.along(k, step).start()
        elif stage == 1:
            for step in range(1, self.line):
                self.along(k, step).wait_recv()
            self.group(k, 0, order[0], first).start()
            self.group(k, 1, order[0], second).start()
            self.group(k, 3, order[0], self.sibling).start()
        elif stage == 2:
            self.group(k, 0, order[1], first).wait_recv()
            self.group(k, 2, order[1], second).start()
            self.group(k, 4, order[1], self.sibling).start()
        else:
            self.group(k, 1, order[2], second).wait_recv()
            self.group(k, 5, order[2], self.sibling).start()
            self.group(k, 2, order[3], second).wait_recv()
            self.group(k, 6, order[3], self.sibling).start()

    def members(self, batch):
        before = sum(len(b) for b in self.batches[:batch])
        return range(before, before + len(self.batches[batch]))

    def stages(self):
        def make(stage):
            def act(batch):
                for k in self.members(batch):
                    self.step(k, stage)

            return act

        return [make(stage) for stage in range(4)]

    def finish(self, batch):
        for k in self.members(batch):
            order, _, _ = self.groups(k)
            for slot, at in ((3, 0), (4, 1), (5, 2), (6, 3)):
                (self.aside(k, at) if self.late(k) else self.group(k, slot, order[at], self.sibling)).wait_recv()

    def sent(self):
        for k in range(len(self.chunks)):
            order, _, _ = self.groups(k)
            for step in range(1, self.line):
                self.along(k, step).wait_send()
            for slot, at in ((0, 0), (1, 0), (2, 1)):
                self.group(k, slot, order[at], self.sibling).wait_send()
            for slot, at in ((3, 0), (4, 1), (5, 2), (6, 3)):
                (self.aside(k, at) if self.late(k) else self.group(k, slot, order[at], self.sibling)).wait_send()


def add_into(target, source, pieces, target_at, source_at):
    def body(i, carry):
        t, s = target_at(i), source_at(i)
        target[t] = target[t] + source[s]
        return carry

    lax.fori_loop(0, pieces, body, 0)


class Scatter:
    def __init__(self, batches, line, sources, totals, landing, core_s, own_s, first_b, second_b, line_b, plane_b, sems):
        self.batches, self.line, self.sources, self.totals = batches, line, sources, totals
        self.chunks = [chunk for batch in batches for chunk in batch]
        self.landing, self.core_s, self.own_s = landing, core_s, own_s
        self.first_b, self.second_b, self.line_b, self.plane_b = first_b, second_b, line_b, plane_b
        self.own_sem, self.load_sem, self.send_sem, self.recv_sem, self.z_send, self.z_recv = sems
        self.z, self.x, self.c, self.y = where_am_i()
        z, x, c, y = self.z, self.x, self.c, self.y
        self.x_side, self.y_side, self.sibling = device(z, 1 - x, c, y), device(z, x, c, 1 - y), device(z, x, 1 - c, y)
        self.spot = {}
        for b, batch in enumerate(batches):
            column = 0
            for k in self.members(b):
                self.spot[k] = (b, column)
                column += self.chunks[k][3]

    def members(self, batch):
        before = sum(len(b) for b in self.batches[:batch])
        return range(before, before + len(self.batches[batch]))

    def source(self, k, c):
        seg, _, start, cols = self.chunks[k]
        return self.sources[seg].at[:, :, :, c, :, pl.ds(start, cols)]

    def core_copy(self, k):
        return remote(
            self.source(k, 1 - self.c), self.landing[k], self.send_sem.at[k, 0], self.recv_sem.at[k, 0], self.sibling
        )

    def core(self, k):
        batch, column = self.spot[k]
        return self.core_s.at[batch % 4, :, :, :, :, pl.ds(column, self.chunks[k][3])]

    def own(self, k):
        batch, column = self.spot[k]
        return self.own_s.at[batch % 2, :, :, :, :, pl.ds(column, self.chunks[k][3])]

    def own_copy(self, k):
        return pltpu.make_async_copy(self.source(k, self.c), self.own(k), self.own_sem.at[k])

    def load_copy(self, k):
        return pltpu.make_async_copy(self.landing[k], self.core(k), self.load_sem.at[k])

    def late(self, k):
        return self.chunks[k][1] >= 2

    def first_copy(self, k):
        x, y, sems = self.x, self.y, (self.send_sem.at[k, 1], self.recv_sem.at[k, 1])
        even = self.chunks[k][1] % 2 == 0
        if self.late(k):
            source = self.plane_b[k].at[1 - y] if even else self.plane_b[k].at[:, 1 - x]
        else:
            source = self.core(k).at[1 - y] if even else self.core(k).at[:, :, 1 - x]
        return remote(source, self.first_b[k], *sems, self.y_side if even else self.x_side)

    def second_copy(self, k):
        x, y, first = self.x, self.y, self.first_b[k]
        sems = (self.send_sem.at[k, 2], self.recv_sem.at[k, 2])
        even = self.chunks[k][1] % 2 == 0
        if self.late(k):
            source = first.at[1 - x] if even else first.at[1 - y]
        else:
            source = first.at[:, 1 - x] if even else first.at[1 - y]
        return remote(source, self.second_b[k], *sems, self.x_side if even else self.y_side)

    def line_copy(self, k, step):
        owner = lax.rem(self.z + step, self.line)
        source = self.core(k).at[:, owner] if self.late(k) else self.second_b[k].at[owner]
        return remote(
            source, self.line_b[k].at[step - 1],
            self.z_send.at[k, step - 1], self.z_recv.at[k, step - 1], device(owner, self.x, self.c, self.y),
        )

    def step(self, k, stage):
        line, x, y, z = self.line, self.x, self.y, self.z
        early = self.chunks[k][1] == 0
        if stage == 0:
            self.core_copy(k).start()
        elif stage == 1:
            self.core_copy(k).wait_recv()
            self.load_copy(k).start()
            self.own_copy(k).start()
        elif stage == 2:
            self.load_copy(k).wait()
            self.own_copy(k).wait()
            at = lambda i: (i // (2 * line), (i // 2) % line, i % 2)
            add_into(self.core(k), self.own(k), 4 * line, at, at)
            if self.late(k):
                for step in range(1, line):
                    self.line_copy(k, step).start()
            else:
                self.first_copy(k).start()
        elif self.late(k):
            self.late_step(k, stage)
        elif stage == 3:
            self.first_copy(k).wait_recv()
            if early:
                there, here = (lambda i: (i // 2, i % 2)), (lambda i: (y, i // 2, i % 2))
            else:
                there, here = (lambda i: (i // line, i % line)), (lambda i: (i // line, i % line, x))
            add_into(self.first_b[k], self.core(k), 2 * line, there, here)
            self.second_copy(k).start()
            self.first_copy(k).wait_send()
        elif stage == 4:
            self.second_copy(k).wait_recv()
            here = (lambda i: (i, x)) if early else (lambda i: (y, i))
            add_into(self.second_b[k], self.first_b[k], line, lambda i: (i,), here)
            for step in range(1, line):
                self.line_copy(k, step).start()
        else:
            seg, _, start, cols = self.chunks[k]
            total = self.second_b[k][z].astype(F32)
            for step in range(1, line):
                self.line_copy(k, step).wait_recv()
                total = total + self.line_b[k][step - 1].astype(F32)
            self.totals[seg][:, pl.ds(start, cols)] = total

    def late_step(self, k, stage):
        line, x, y, z = self.line, self.x, self.y, self.z
        even = self.chunks[k][1] % 2 == 0
        if stage == 3:
            for step in range(1, line):
                self.line_copy(k, step).wait_recv()

            def body(i, carry):
                at = (i // 2, i % 2)
                total = self.core(k)[i // 2, z, i % 2].astype(F32)
                for step in range(1, line):
                    total = total + self.line_b[k][(step - 1, *at)].astype(F32)
                self.plane_b[k][at] = total.astype(BF16)
                return carry

            lax.fori_loop(0, 4, body, 0)
            self.first_copy(k).start()
            for step in range(1, line):
                self.line_copy(k, step).wait_send()
        elif stage == 4:
            self.first_copy(k).wait_recv()
            here = (lambda i: (y, i)) if even else (lambda i: (i, x))
            add_into(self.first_b[k], self.plane_b[k], 2, lambda i: (i,), here)
            self.second_copy(k).start()
        else:
            seg, _, start, cols = self.chunks[k]
            self.second_copy(k).wait_recv()
            near = self.first_b[k][x if even else y]
            self.totals[seg][:, pl.ds(start, cols)] = near.astype(F32) + self.second_b[k][...].astype(F32)

    def stages(self):
        def make(stage):
            def act(batch):
                for k in self.members(batch):
                    self.step(k, stage)

            return act

        return [make(stage) for stage in range(6)]

    def sent(self):
        for k in range(len(self.chunks)):
            self.core_copy(k).wait_send()
            self.second_copy(k).wait_send()
            if self.late(k):
                self.first_copy(k).wait_send()
                continue
            for step in range(1, self.line):
                self.line_copy(k, step).wait_send()


def switch_on(index, cases):
    for at, act in cases.items():
        pl.when(index == at)(act)


def columns(start, size):
    return pl.ds(pl.multiple_of(start, 128), size)


def owner_maps(owners, entries, width, model):
    inner = model // width * entries
    at = lax.broadcasted_iota(jnp.int32, (inner, model), 1)
    place = lax.broadcasted_iota(jnp.int32, (inner, model), 0)
    spread = jnp.where(at // width * entries + at % entries == place, 1.0, 0.0).astype(BF16)
    at = lax.broadcasted_iota(jnp.int32, (owners, model), 1)
    owner = lax.broadcasted_iota(jnp.int32, (owners, model), 0)
    return spread, jnp.where(at % width // entries == owner, 1.0, 0.0)


def ahead_kernel(batches, line, width, *refs):
    (signals, ada, extra, seg_qkv, seg_proj, seg_fc1, seg_fc2, tok_near, tok_away, cot, kmask_ref, qmask_ref,
     qkv_f, proj_f, fc1_f, fc2_f, g1_f, g2_f, ql_f, kl_f, vl_f, mix_f, x_f,
     boosts, mod_ref, stat_ref, out_ref, gmid_ref, rows_ref, gb1_ref, sig_s, ada_flat,
     products, arrived, vecs, hidden_bias, x_s, ql_ref, kl_ref, vl_ref, mix_ref, att_ref, cot_s, one_s, acc_s, mid_s, twot_s, back_s, backt_s, gacc_s, w_s, grad_s,
     a_send, a_recv, b_send, b_recv, save_sem, local_sem, pair_sem, z_send, z_recv, send_sem, recv_sem, w_sem, grad_sem) = refs
    z, x, c, y = where_am_i()
    total = 8 * line
    padded, model = tok_near.shape
    half_cols = mod_ref.shape[1] // 2
    heads = 256 // width
    outs = [qkv_f, proj_f, fc1_f, fc2_f]
    own = [
        pltpu.make_async_copy(i, o.at[y, z, x, c], local_sem.at[s])
        for s, (i, o) in enumerate(zip([seg_qkv, seg_proj, seg_fc1, seg_fc2], outs))
    ]
    for copy in own:
        copy.start()
    mine = pl.ds(y * padded, padded)
    pairs = [
        (
            pltpu.make_async_copy(near, inside.at[mine], pair_sem.at[p, 0]),
            remote(away, inside.at[mine], pair_sem.at[p, 1], pair_sem.at[p, 2], device(z, x, c, 1 - y)),
        )
        for p, (near, away, inside) in enumerate(((tok_near, tok_away, x_s), (cot.at[y], cot.at[1 - y], cot_s)))
    ]
    me = (lax.axis_index("dp"), y)
    signal_exchange = Exchange(total, lambda to: signals.at[to // 2], sig_s.at[me], b_send, b_recv)
    exchange = Exchange(total, lambda to: products.at[to // 2, to % 2], arrived.at[me], a_send, a_recv)
    gather = Gather(
        batches, line, [seg_qkv, seg_proj, seg_fc1, seg_fc2], outs, z_send, z_recv, send_sem, recv_sem
    )
    ticks = Ticks(len(batches), gather.stages(), (0, 1, 3, 5))
    greet_all(total)
    signal_exchange.start()
    ticks.run(0, 1)
    for copy in pairs[0]:
        copy.start()
    for copy in own:
        copy.wait()

    def load_attend(i):
        half, sub, slot = i % 2, i // 2, i % 2
        return [
            pltpu.make_async_copy(
                qkv_f.at[half, :, :, :, :, pl.ds(sub * 768, 768)], w_s.at[slot, :, :, :, :, pl.ds(0, 768)],
                w_sem.at[slot, 0],
            ),
            pltpu.make_async_copy(
                proj_f.at[half, :, :, :, :, pl.ds(sub * 256, 256)], w_s.at[slot, :, :, :, :, pl.ds(768, 256)],
                w_sem.at[slot, 1],
            ),
        ]

    def load_feed(half, start, cols):
        return [
            pltpu.make_async_copy(
                ref.at[half, :, :, :, :, columns(start, cols)],
                w_s.at[half, :, :, :, :, pl.ds(at * 512, cols)], w_sem.at[half, at],
            )
            for at, ref in enumerate((fc1_f, fc2_f))
        ]

    def start_loads(copies):
        for copy in copies:
            copy.start()

    def wait_loads(copies):
        for copy in copies:
            copy.wait()

    for j in range(6):
        ada_flat[:, j * half_cols : (j + 1) * half_cols] = ada[:, j, :]
    signal_exchange.wait()
    slots, owners = sig_s.shape[1], sig_s.shape[0]
    for slot in range(slots):
        rows_in = sig_s[:, 0, slot, : ada.shape[0]].astype(BF16)
        for j in range(8):
            block = jnp.broadcast_to(extra[j : j + 1], (owners, half_cols))
            if j < 6:
                block = block + mm(rows_in, ada_flat[:, j * half_cols : (j + 1) * half_cols])
            products[:, slot, j, :] = block
    exchange.start()
    ticks.run(1, 2)
    for copy in pairs[1]:
        copy.start()
    ticks.run(2, 4)
    exchange.wait()
    for half in range(2):
        mod_ref[:, half * half_cols : (half + 1) * half_cols] = jnp.sum(arrived[:, half], 0)
    entries = width // owners
    spread, owner_of = owner_maps(owners, entries, width, model)
    letters = [arrived[:, half, 6, :] for half in range(2)]
    piece = heads * entries * 2
    blocks = [
        jnp.concatenate([letter[:, r * piece : (r + 1) * piece] for letter in letters], 1) for r in range(4)
    ] + [
        letters[half][:, (4 + 2 * part) * piece : (6 + 2 * part) * piece] for half in range(2) for part in range(2)
    ]
    turned_out = mm(jnp.concatenate(blocks, 0).astype(BF16), spread)
    for r in range(8):
        row = jnp.sum(turned_out[r * owners : (r + 1) * owners] * owner_of, 0, keepdims=True)
        if r < 4:
            vecs[r : r + 1] = row
        else:
            hidden_bias[0:1, (r - 4) * model : (r - 3) * model] = row
    boosts[...] = jnp.zeros_like(boosts)
    for half in range(2):
        lift = jnp.exp(arrived[0, half, 7:8, : 2 * heads])
        for sub in range(2):
            boosts[half * 2 + sub, 0:1, 0:heads] = lift[:, sub * heads : (sub + 1) * heads]
    wait_loads(pairs[0])
    normed, _ = norm_rows(x_s[...].astype(F32))
    one_s[...] = (normed * (1.0 + mod_ref[2:3]) + mod_ref[4:5]).astype(BF16)
    acc_s[...] = jnp.zeros_like(acc_s)
    ticks.run(4, 7)
    gather.finish(0)
    gather.finish(1)
    start_loads(load_attend(0))
    start_loads(load_attend(1))
    ones = jnp.ones((x_s.shape[0], width), BF16)

    def attend(i, carry):
        def second_half():
            ticks.run(8, 9)
            gather.finish(2)
            gather.finish(3)
            start_loads(load_attend(2))
            start_loads(load_attend(3))

        switch_on(i, {1: lambda: ticks.run(7, 8), 2: second_half, 3: lambda: ticks.run(9, 10)})

        slot = lax.rem(i, 2)
        at = slot * 2 + i // 2
        wait_loads([
            pltpu.make_async_copy(
                qkv_f.at[0, :, :, :, :, pl.ds(0, 768)], w_s.at[slot, :, :, :, :, pl.ds(0, 768)], w_sem.at[slot, 0]
            ),
            pltpu.make_async_copy(
                proj_f.at[0, :, :, :, :, pl.ds(0, 256)], w_s.at[slot, :, :, :, :, pl.ds(768, 256)], w_sem.at[slot, 1]
            ),
        ])
        cols = columns(at * 256, 256)
        turned = pl.ds(pl.multiple_of(at * 256, 256), 256)
        weights = w_s[slot].reshape(model, 1024)
        projected = mm(one_s[...], weights[:, :768])
        queries = projected[:, :256] + vecs[0:1, cols]
        keys = projected[:, 256:512]
        values = (projected[:, 512:] + vecs[1:2, cols]).astype(BF16)
        vl_ref[:, cols] = values
        q_turned, k_turned = queries.T, keys.T
        boost = boosts[at]
        kmask, qmask = kmask_ref[...], qmask_ref[...]
        q_low, k_low, mixed, q_inv, k_inv, totals = [], [], [], [], [], []
        for head in range(heads):
            part = slice(head * width, (head + 1) * width)
            q_now, k_now = q_turned[part], k_turned[part]
            q_scale = lax.rsqrt(jnp.sum(q_now * q_now, 0, keepdims=True) + 1e-06)
            k_scale = lax.rsqrt(jnp.sum(k_now * k_now, 0, keepdims=True) + 1e-06)
            q_bf = (q_now * q_scale * boost[0:1, head : head + 1]).astype(BF16)
            k_bf = (k_now * k_scale).astype(BF16)
            scaled = q_bf.astype(F32) * LOG2E
            high = scaled.astype(BF16)
            rest = (scaled - high.astype(F32)).astype(BF16)
            q_all = jnp.concatenate([high, rest, qmask], 0)
            k_all = jnp.concatenate([k_bf, k_bf, kmask], 0)
            soft = jnp.exp2(mm_tn(q_all, k_all)).astype(BF16)
            summed = mm(soft, jnp.concatenate([values[:, part], ones], 1))
            total_now = summed[:, width:]
            mixed.append((summed[:, :width] / total_now).astype(BF16))
            totals.append(total_now[:, 0:1])
            q_low.append(q_bf)
            k_low.append(k_bf)
            q_inv.append(q_scale)
            k_inv.append(k_scale)
        mixed_all = jnp.concatenate(mixed, 1)
        mix_ref[:, cols] = mixed_all
        ql_ref[turned, :] = jnp.concatenate(q_low, 0)
        kl_ref[turned, :] = jnp.concatenate(k_low, 0)
        stat_ref[at, 0] = jnp.concatenate(q_inv + k_inv, 0)
        stat_ref[at, 1] = jnp.log2(jnp.concatenate(totals + totals, 1)).T
        acc_s[...] += mm_nt(mixed_all, weights[:, 768:])
        return carry

    lax.fori_loop(0, 4, attend, 0)
    saves = [
        pltpu.make_async_copy(inside, outside, save_sem.at[n])
        for n, (inside, outside) in enumerate(
            ((ql_ref, ql_f), (kl_ref, kl_f), (vl_ref, vl_f), (mix_ref, mix_f), (x_s, x_f))
        )
    ]
    start_loads(saves)
    attended = acc_s[...] + vecs[2:3]
    att_ref[...] = attended.astype(BF16)
    middle = x_s[...].astype(F32) + mod_ref[0:1] * attended
    mid_s[...] = middle
    normed, _ = norm_rows(middle)
    two = (normed * (1.0 + mod_ref[3:4]) + mod_ref[5:6]).astype(BF16)
    one_s[...] = two
    twot_s[...] = two.T
    wait_loads(pairs[1])
    back = (mod_ref[1:2] * cot_s[...].astype(F32)).astype(BF16)
    back_s[...] = back
    backt_s[...] = back.T
    acc_s[...] = jnp.zeros_like(acc_s)
    gacc_s[...] = jnp.zeros_like(gacc_s)

    def store_feed(half, start, cols):
        return [
            pltpu.make_async_copy(
                grad_s.at[half, at, :, :, :, :, pl.ds(0, cols)], ref.at[half, :, :, :, :, columns(start, cols)],
                grad_sem.at[half, at],
            )
            for at, ref in enumerate((g1_f, g2_f))
        ]

    def feed_step(half, start, cols, stored):
        wait_loads(load_feed(half, start, cols))
        weights = w_s[half].reshape(model, 1024)
        w1, w2 = weights[:, :cols], weights[:, 512 : 512 + cols]
        spot = columns(half * (hidden_bias.shape[1] // 2) + start, cols)
        hidden = mm(one_s[...], w1) + hidden_bias[0:1, spot]
        square = hidden * hidden
        curve = jnp.tanh(0.7978845608028654 * hidden * (1.0 + 0.044715 * square))
        level = 0.5 * (1.0 + curve)
        activated = (hidden * level).astype(BF16)
        slope = level + 0.5 * hidden * (1.0 - curve * curve) * (
            0.7978845608028654 * (1.0 + 0.134145 * square)
        )
        acc_s[...] += mm_nt(activated, w2)
        stored()
        shape = grad_s.shape[2:6] + (cols,)
        grad_s[half, 1, :, :, :, :, 0:cols] = mm(backt_s[...], activated).astype(BF16).reshape(shape)
        hidden_grad = (mm(back_s[...], w2) * slope).astype(BF16)
        grad_s[half, 0, :, :, :, :, 0:cols] = mm(twot_s[...], hidden_grad).astype(BF16).reshape(shape)
        start_loads(store_feed(half, start, cols))
        gb1_ref[0:1, spot] = jnp.sum(hidden_grad.astype(F32), 0, keepdims=True)
        gacc_s[...] += mm_nt(hidden_grad, w1)

    def feed(i, carry):
        half, part = lax.rem(i, 2), i // 2

        def before(p):
            def act():
                ticks.run(10 + 2 * p, 11 + 2 * p)
                gather.finish(4 + 2 * p)
                gather.finish(5 + 2 * p)
                start_loads(load_feed(0, p * 512, 512))
                start_loads(load_feed(1, p * 512, 512))

            return act

        switch_on(i, {2 * p: before(p) for p in range(3)})
        switch_on(i, {2 * p + 1: (lambda p=p: ticks.run(11 + 2 * p, 12 + 2 * p)) for p in range(3)})
        feed_step(half, part * 512, 512, lambda: pl.when(i >= 2)(lambda: wait_loads(store_feed(half, 0, 512))))
        return carry

    def feed_last(i, carry):
        half, part = lax.rem(i, 2), i // 2

        def before(p):
            def act():
                gather.finish(10 + p)
                start_loads(load_feed(0, 1536 + p * 256, 256))
                start_loads(load_feed(1, 1536 + p * 256, 256))

            return act

        def stored():
            pl.when(i < 2)(lambda: wait_loads(store_feed(half, 0, 512)))
            pl.when(i >= 2)(lambda: wait_loads(store_feed(half, 0, 256)))

        switch_on(i, {0: before(0), 1: lambda: ticks.run(16, 17), 2: before(1)})
        feed_step(half, 1536 + part * 256, 256, stored)
        return carry

    lax.fori_loop(0, 6, feed, 0)
    lax.fori_loop(0, 4, feed_last, 0)
    middle = mid_s[...]
    out_grad = cot_s[...].astype(F32)
    branch = acc_s[...] + vecs[3:4]
    out_ref[...] = (middle + mod_ref[1:2] * branch).astype(BF16)
    normed, inverse = norm_rows(middle)
    grad = gacc_s[...]
    middle_grad = out_grad + norm_rows_back(grad * (1.0 + mod_ref[3:4]), normed, inverse)
    gmid_ref[...] = middle_grad
    rows_ref[0:1] = jnp.sum(out_grad * branch, 0, keepdims=True)
    rows_ref[1:2] = jnp.sum(grad * normed, 0, keepdims=True)
    rows_ref[2:3] = jnp.sum(grad, 0, keepdims=True)
    rows_ref[3:4] = jnp.sum(back_s[...].astype(F32), 0, keepdims=True)
    rows_ref[4:5] = jnp.sum(middle_grad * att_ref[...].astype(F32), 0, keepdims=True)
    rows_ref[5:8] = jnp.zeros((3, model), F32)
    gb1_ref[1:8] = jnp.zeros((7, gb1_ref.shape[1]), F32)
    for half in range(2):
        wait_loads(store_feed(half, 0, 256))
    wait_loads(saves)
    gather.sent()


def run_ahead(batches, line, signals, ada, extra, segments, tok_near, tok_away, cot, kmask, qmask, hidden_cols, width, cid):
    padded, model = tok_near.shape
    rows = 2 * padded
    total, count = 8 * line, sum(len(batch) for batch in batches)
    own_rows = segments[0].shape[0]
    anywhere, inside = pl.BlockSpec(memory_space=pl.ANY), pl.BlockSpec(memory_space=pltpu.VMEM)
    full = [jax.ShapeDtypeStruct((2, line, 2, 2) + s.shape, BF16) for s in segments]
    flat = jax.ShapeDtypeStruct((rows, model), BF16)
    turned = jax.ShapeDtypeStruct((model, rows), BF16)
    flat_s, turned_s, wide_s = (
        pltpu.VMEM((rows, model), BF16), pltpu.VMEM((model, rows), BF16), pltpu.VMEM((rows, model), F32)
    )
    block = (line, 2, 2, own_rows)
    dma = pltpu.SemaphoreType.DMA
    letters = pltpu.VMEM((total // 2, 2, 8, model // 2), F32)
    return pl.pallas_call(
        functools.partial(ahead_kernel, batches, line, width),
        in_specs=[inside] * 7 + [anywhere] * 3 + [inside] * 2,
        out_shape=full + [full[2], full[3], turned, turned, flat, flat, flat] + [
            jax.ShapeDtypeStruct((model // 256, 8, 128), F32), jax.ShapeDtypeStruct((8, model), F32),
            jax.ShapeDtypeStruct((model // 256, 2, 8, rows), F32), flat,
            jax.ShapeDtypeStruct((rows, model), F32), jax.ShapeDtypeStruct((8, model), F32),
            jax.ShapeDtypeStruct((8, hidden_cols), F32), jax.ShapeDtypeStruct((total // 2, 2, 8, 128), F32),
            jax.ShapeDtypeStruct((own_rows, 3 * model), BF16),
        ],
        out_specs=[anywhere] * 11 + [inside] * 9,
        scratch_shapes=[
            letters, letters, pltpu.VMEM((8, model), F32),
            pltpu.VMEM((8, hidden_cols), F32), flat_s, turned_s, turned_s, flat_s, flat_s,
            flat_s, flat_s, flat_s, wide_s, wide_s, turned_s, flat_s, turned_s, wide_s,
            pltpu.VMEM((2,) + block + (1024,), BF16), pltpu.VMEM((2, 2) + block + (512,), BF16),
            dma((total,)), dma((total,)), dma((total,)), dma((total,)), dma((5,)), dma((4,)), dma((2, 3)),
            dma((count, line - 1)), dma((count, line - 1)), dma((count, 7)), dma((count, 7)),
            dma((2, 2)), dma((2, 2)),
        ],
        compiler_params=pltpu.CompilerParams(
            collective_id=cid, has_side_effects=True, vmem_limit_bytes=VMEM_LIMIT
        ),
        name="ahead",
    )(signals, ada, extra, *segments, tok_near, tok_away, cot, kmask, qmask)


def behind_kernel(batches, line, width, levels, *refs):
    count = sum(len(batch) for batch in batches)
    (x_f, qkv_f, proj_f, g1_f, g2_f, result, ql_f, kl_f, vl_f, mix_f,
     gmid_ref, mod_ref, feed_rows, hidden_ref, stat_ref, boosts, kmask_ref, qmask_ref) = refs[:18]
    (gqkv_f, gproj_f, act_far, tok_far) = refs[18:22]
    landing = refs[22 : 22 + count]
    (t_qkv, t_proj, t_fc1, t_fc2, mods_ref, x_s) = refs[22 + count : 28 + count]
    rest = refs[28 + count :]
    first_b, second_b, line_b, plane_b = (rest[n * count : (n + 1) * count] for n in range(4))
    (core_s, own_s, ga_s, gat_s, onet_s, acc_s, turn_s, flat_s, w_s, grad_s, gm_s, vec_s, rows_ref, heads_s,
     a_send, a_recv, pair_sem, x_sem, w_sem, grad_sem,
     own_sem, load_sem, send_sem, recv_sem, z_send, z_recv) = rest[4 * count :]
    z, x, c, y = where_am_i()
    total = 8 * line
    padded, model = result.shape[0] // 2, result.shape[1]
    half_cols = model // 2
    heads = 256 // width
    partner = device(z, x, c, 1 - y)
    scatter = Scatter(
        batches, line, [gqkv_f, gproj_f, g1_f, g2_f], [t_qkv, t_proj, t_fc1, t_fc2], landing, core_s, own_s,
        first_b, second_b, line_b, plane_b, (own_sem, load_sem, send_sem, recv_sem, z_send, z_recv),
    )
    ticks = Ticks(len(batches), scatter.stages(), (0, 1, 2, 4, 6, 8))
    others = pl.ds((1 - y) * padded, padded)
    pairs = [
        remote(source.at[others], target, pair_sem.at[p, 0], pair_sem.at[p, 1], partner)
        for p, (source, target) in enumerate(((result, act_far), (x_s, tok_far)))
    ]
    load_x = pltpu.make_async_copy(x_f, x_s, x_sem.at[0])
    load_x.start()
    greet_all(total)
    ticks.run(0, 1)
    pairs[0].start()

    def load_group(i):
        half = lax.rem(i, 2)
        sub, at = i // 2, half * 2 + i // 2
        turned = pl.ds(pl.multiple_of(at * 256, 256), 256)
        cols = columns(at * 256, 256)
        pieces = [
            (qkv_f.at[half, :, :, :, :, columns(sub * 768, 768)], w_s.at[:, :, :, :, pl.ds(0, 768)]),
            (proj_f.at[half, :, :, :, :, columns(sub * 256, 256)], w_s.at[:, :, :, :, pl.ds(768, 256)]),
            (ql_f.at[turned], turn_s.at[0]),
            (kl_f.at[turned], turn_s.at[1]),
            (vl_f.at[:, cols], flat_s.at[0]),
            (mix_f.at[:, cols], flat_s.at[1]),
        ]
        return [pltpu.make_async_copy(s, t, w_sem.at[n]) for n, (s, t) in enumerate(pieces)]

    def store_group(i):
        half, sub = lax.rem(i, 2), i // 2
        return [
            pltpu.make_async_copy(
                grad_s.at[:, :, :, :, pl.ds(0, 768)], gqkv_f.at[half, :, :, :, :, columns(sub * 768, 768)],
                grad_sem.at[0],
            ),
            pltpu.make_async_copy(
                grad_s.at[:, :, :, :, pl.ds(768, 256)], gproj_f.at[half, :, :, :, :, columns(sub * 256, 256)],
                grad_sem.at[1],
            ),
        ]

    def start_loads(copies):
        for copy in copies:
            copy.start()

    def wait_loads(copies):
        for copy in copies:
            copy.wait()

    start_loads(load_group(0))
    ticks.run(1, 2)
    attend_grad = (mod_ref[0:1] * gmid_ref[...]).astype(BF16)
    ga_s[...] = attend_grad
    gat_s[...] = attend_grad.T
    vec_s[2:3] = jnp.sum(attend_grad.astype(F32), 0, keepdims=True)
    vec_s[3:4] = feed_rows[3:4]
    for part in range(4):
        vec_s[4 + part : 5 + part] = hidden_ref[0:1, part * model : (part + 1) * model]
    heads_s[...] = jnp.zeros_like(heads_s)
    lane = lax.broadcasted_iota(jnp.int32, (1, half_cols), 1)
    ticks.run(2, 3)
    load_x.wait()
    normed, _ = norm_rows(x_s[...].astype(F32))
    onet_s[...] = (normed * (1.0 + mod_ref[2:3]) + mod_ref[4:5]).astype(BF16).T
    acc_s[...] = jnp.zeros_like(acc_s)
    kmask, qmask = kmask_ref[...], qmask_ref[...]
    rows = kmask.shape[1]
    place = lax.broadcasted_iota(jnp.int32, (16, rows), 0)

    def pieces_of(row, first):
        high, mid, low = split_three(row)
        zero = jnp.zeros((16, rows), BF16)
        out = jnp.where(place == first, jnp.broadcast_to(high, zero.shape), zero)
        out = jnp.where(place == first + 1, jnp.broadcast_to(mid, zero.shape), out)
        return jnp.where(place == first + 2, jnp.broadcast_to(low, zero.shape), out)

    def group(i, carry):
        slot = lax.rem(i, 2)
        at = slot * 2 + i // 2

        wait_loads(load_group(i))
        boost = boosts[at]
        weights = w_s[...].reshape(model, 1024)
        mixed = flat_s[1]
        values = flat_s[0]
        q_all_low, k_all_low = turn_s[0], turn_s[1]
        mixed_grad = mm(ga_s[...], weights[:, 768:]).astype(BF16)
        mixed_turned, v_turned, q_plain = mixed_grad.T, values.T, q_all_low.T
        dq_rows, dk_rows, dv_cols, scales = [], [], [], []
        for head in range(heads):
            if head == 2:
                switch_on(i, {n: (lambda n=n: ticks.run(3 + 2 * n, 4 + 2 * n)) for n in range(4)})
            part = slice(head * width, (head + 1) * width)
            lift = boost[0:1, head : head + 1]
            q_bf, k_bf = q_all_low[part], k_all_low[part]
            q_float = q_bf.astype(F32)
            scaled = q_float * LOG2E
            high = scaled.astype(BF16)
            low = (scaled - high.astype(F32)).astype(BF16)
            log_total = stat_ref[at, 1, head : head + 1]
            q_all = jnp.concatenate([high, low, qmask + pieces_of(-log_total, levels + 1)], 0)
            k_all = jnp.concatenate([k_bf, k_bf, kmask], 0)
            soft = jnp.exp2(mm_tn(k_all, q_all))
            product = soft * mm_tn(v_turned[part], mixed_turned[part])
            delta = jnp.sum(product, 0, keepdims=True)
            scores_grad = (product - soft * delta).astype(BF16)
            dv_cols.append(mm(soft.astype(BF16), mixed_grad[:, part]))
            dq_low = mm(k_bf, scores_grad)
            dk_low = mm(scores_grad, q_plain[:, part]).T
            q_inv = stat_ref[at, 0, head : head + 1]
            k_inv = stat_ref[at, 0, heads + head : heads + head + 1]
            k_unit = k_bf.astype(F32)
            along = dq_low * q_float
            scales.append(jnp.sum(along, keepdims=True))
            dq_rows.append(
                q_inv * (dq_low * lift - q_float * (1.0 / lift) * jnp.sum(along, 0, keepdims=True))
            )
            dk_rows.append(k_inv * (dk_low - k_unit * jnp.sum(dk_low * k_unit, 0, keepdims=True)))
        dq = jnp.concatenate(dq_rows, 0).T.astype(BF16)
        dk = jnp.concatenate(dk_rows, 0).T.astype(BF16)
        dv = jnp.concatenate(dv_cols, 1).astype(BF16)
        triple = jnp.concatenate([dq, dk, dv], 1)

        @pl.when(i > 0)
        def _():
            wait_loads(store_group(i))

        switch_on(i, {n: (lambda n=n: ticks.run(4 + 2 * n, 5 + 2 * n)) for n in range(3)})
        shape = grad_s.shape[:4]
        grad_s[:, :, :, :, 0:768] = mm(onet_s[...], triple).astype(BF16).reshape(shape + (768,))
        grad_s[:, :, :, :, 768:1024] = mm(gat_s[...], mixed).astype(BF16).reshape(shape + (256,))
        start_loads(store_group(i))
        acc_s[...] += mm_nt(triple, weights[:, :768])
        spot = columns(at * 256, 256)
        vec_s[0:1, spot] = jnp.sum(dq.astype(F32), 0, keepdims=True)
        vec_s[1:2, spot] = jnp.sum(dv.astype(F32), 0, keepdims=True)
        for head in range(heads):
            heads_s[0:1] += jnp.where(lane == at * heads + head, scales[head], 0.0)

        @pl.when(i < 3)
        def _():
            start_loads(load_group(i + 1))

        return carry

    lax.fori_loop(0, 4, group, 0)
    wait_loads(store_group(3))
    ticks.run(10, 12)
    grad = acc_s[...]
    normed, inverse = norm_rows(x_s[...].astype(F32))
    x_s[...] = (
        gmid_ref[...] + norm_rows_back(grad * (1.0 + mod_ref[2:3]), normed, inverse)
    ).astype(BF16)
    pairs[1].start()
    rows_ref[0:1] = jnp.sum(grad * normed, 0, keepdims=True)
    rows_ref[1:2] = jnp.sum(grad, 0, keepdims=True)
    owners = total // 2
    spread, owner_of = owner_maps(owners, width // owners, width, model)
    picked = jnp.concatenate([owner_of * vec_s[r : r + 1] for r in range(8)], 0)
    moved = sum(mm_nt(part, spread) for part in split_three(picked))
    small = jnp.concatenate([moved[r * owners : (r + 1) * owners] for r in range(8)], 1)
    mod_rows = (feed_rows[4:5], feed_rows[0:1], rows_ref[0:1], feed_rows[1:2], rows_ref[1:2], feed_rows[2:3])
    for half in range(2):
        for n, row in enumerate(mod_rows):
            gm_s[:, half, n, :] = jnp.broadcast_to(
                row[:, half * half_cols : (half + 1) * half_cols], (owners, half_cols)
            )
        gm_s[:, half, 6, :] = small
        gm_s[:, half, 7, :] = jnp.broadcast_to(heads_s[0:1], (owners, half_cols))
    exchange = Exchange(total, lambda to: gm_s.at[to // 2, to % 2], mods_ref.at[lax.axis_index("dp"), y], a_send, a_recv)
    exchange.start()
    ticks.run(12, ticks.total)
    exchange.wait()
    wait_loads(pairs)
    scatter.sent()


def run_behind(batches, line, levels, saved, inner, width, cid):
    x_f, qkv_f, proj_f, g1_f, g2_f, result, ql, kl, vl, mix = saved
    rows, model = x_f.shape
    chunks = [chunk for batch in batches for chunk in batch]
    total, count = 8 * line, len(chunks)
    own_rows = qkv_f.shape[4]
    anywhere, inside = pl.BlockSpec(memory_space=pl.ANY), pl.BlockSpec(memory_space=pltpu.VMEM)
    dma = pltpu.SemaphoreType.DMA
    landing, first_b, second_b, line_b, plane_b = [], [], [], [], []
    for _, kind, _, cols in chunks:
        tail = (own_rows, cols)
        landing.append(jax.ShapeDtypeStruct((2, line, 2) + tail, BF16))
        if kind >= 2:
            shapes = (2,), (), (line - 1, 2, 2)
        else:
            shapes = (line, 2) if kind == 0 else (2, line), (line,), (line - 1,)
        for held, shape in zip((first_b, second_b, line_b), shapes):
            held.append(pltpu.VMEM(shape + tail, BF16))
        plane_b.append(pltpu.VMEM((2, 2) + tail if kind >= 2 else (16, 128), BF16))
    most = max(sum(chunk[3] for chunk in batch) for batch in batches)
    sources = [qkv_f, proj_f, g1_f, g2_f]
    block = (line, 2, 2, own_rows)
    made = pl.pallas_call(
        functools.partial(behind_kernel, batches, line, width, levels),
        in_specs=[anywhere] * 10 + [inside] * 8,
        out_shape=[jax.ShapeDtypeStruct(qkv_f.shape, BF16), jax.ShapeDtypeStruct(proj_f.shape, BF16)]
        + [jax.ShapeDtypeStruct((rows // 2, model), BF16)] * 2 + landing
        + [jax.ShapeDtypeStruct(s.shape[4:], F32) for s in sources]
        + [jax.ShapeDtypeStruct((total // 2, 2, 8, model // 2), F32), jax.ShapeDtypeStruct((rows, model), BF16)],
        out_specs=[anywhere] * (4 + count) + [inside] * 6,
        scratch_shapes=first_b + second_b + line_b + plane_b + [
            pltpu.VMEM((4, 2, line, 2, own_rows, most), BF16), pltpu.VMEM((2, 2, line, 2, own_rows, most), BF16),
            pltpu.VMEM((rows, model), BF16), pltpu.VMEM((model, rows), BF16),
            pltpu.VMEM((model, rows), BF16), pltpu.VMEM((rows, model), F32), pltpu.VMEM((2, 256, rows), BF16),
            pltpu.VMEM((2, rows, 256), BF16), pltpu.VMEM(block + (1024,), BF16),
            pltpu.VMEM(block + (1024,), BF16), pltpu.VMEM((total // 2, 2, 8, model // 2), F32), pltpu.VMEM((8, model), F32), pltpu.VMEM((8, model), F32),
            pltpu.VMEM((8, model // 2), F32),
            dma((total,)), dma((total,)), dma((2, 2)), dma((1,)), dma((6,)), dma((2,)),
            dma((count,)), dma((count,)), dma((count, 3)), dma((count, 3)),
            dma((count, line - 1)), dma((count, line - 1)),
        ],
        compiler_params=pltpu.CompilerParams(
            collective_id=cid, has_side_effects=True, vmem_limit_bytes=VMEM_LIMIT
        ),
        name="behind",
    )(*saved, *inner)
    return made[2], made[3], made[4 + count :]


def pad_rows(values, padded):
    return jnp.pad(values, ((0, 0), (0, padded - values.shape[1]), (0, 0)))


def gather_list():
    def both(segment, start, cols):
        return [(segment, 0, start, cols, 0, 16), (segment, 1, start, cols, 16, 48)]

    attend = []
    for sub in range(2):
        start = sub * 768
        attend += [both(0, start, 512), both(0, start + 512, 256) + both(1, sub * 256, 256)]
    return attend + [
        [(s, 0, part * 512, wide, 0, 64), (s, 1, part * 512 + wide, 512 - wide, 0, 64)]
        for part in range(3)
        for s, wide in ((2, 256), (3, 128))
    ] + [[(2, 1, start, 256, 0, 64), (3, 0, start, 256, 0, 64)] for start in (1536, 1792)]


def scatter_list():
    def three(segment, start):
        return [(segment, 0, start, 128), (segment, 1, start + 128, 256), (segment, 3, start + 384, 128)]

    feed = []
    for part in range(4):
        feed += [three(2, part * 512), [(3, 0, part * 512, 128), (3, 1, part * 512 + 128, 384)]]
    attend = []
    for sub in range(2):
        start = sub * 768
        attend += [
            three(0, start), [(0, 0, start + 512, 128), (0, 1, start + 640, 128), (1, 1, sub * 256, 256)]
        ]
    return feed + attend


def on_device_paired(
    tokens, condition, scale_lengths, order, cotangent, ada_weight, ada_bias, qkv_weight, qv_bias,
    head_log_scale, proj_weight, out_bias, fc1_weight, fc1_bias, fc2_weight,
):
    n_dp, mine = lax.axis_size("dp"), lax.axis_index("mp")
    line = n_dp // 4
    slots, half_rows, model = tokens.shape
    padded = -(-half_rows // 16) * 16
    rows = 2 * padded
    local_heads, width = qv_bias.shape[1], 64
    own_cols = qkv_weight.shape[2]
    own_rows = qkv_weight.shape[1]
    hidden_cols = fc1_weight.shape[1]
    groups = 2 * own_cols // 256
    swap = order[0, 0] != 0
    entries = qv_bias.shape[2]
    vectors = 4 * local_heads + fc1_bias.shape[0]
    scale_at = vectors * entries
    n_dev = 2 * n_dp

    def to_slots(values):
        return jnp.stack([jnp.where(swap, values[1], values[0]), jnp.where(swap, values[0], values[1])])

    cond_slots = to_slots(condition).astype(F32)
    signal = jax.nn.silu(cond_slots).astype(BF16)
    signals = signal.reshape(slots, n_dp, own_rows).transpose(1, 0, 2).astype(F32)
    signals = jnp.pad(signals, ((0, 0), (0, 8 - slots), (0, 128 - own_rows)))
    bias_own = lax.dynamic_update_slice(
        jnp.zeros((6, local_heads, width), F32), ada_bias.astype(F32), (0, 0, lax.axis_index("dp") * entries)
    ).reshape(6, own_cols)
    small = jnp.concatenate([qv_bias.reshape(-1), out_bias.reshape(-1), fc1_bias.reshape(-1)]).astype(F32)
    extra = jnp.concatenate(
        [bias_own, jnp.pad(small, (0, own_cols - scale_at))[None], jnp.pad(head_log_scale, (0, own_cols - local_heads))[None]]
    )

    token_halves = pad_rows(tokens, padded)
    first = (mine == 0) != swap
    tok_near = jnp.where(first, token_halves[0], token_halves[1])
    tok_away = jnp.where(first, token_halves[1], token_halves[0])
    lengths = lax.dynamic_index_in_dim(to_slots(scale_lengths), mine, 0, keepdims=False)
    kmask, qmask = build_masks(lengths, half_rows, padded)
    segments = [
        qkv_weight.reshape(3, own_rows, 2, 256).transpose(1, 2, 0, 3).reshape(own_rows, 3 * own_cols),
        proj_weight.T, fc1_weight, fc2_weight.T,
    ]
    (qkv_f, proj_f, _, _, g1_f, g2_f, q_low, k_low, v_low, mixed, x_f, boosts, mods, stats, result, grad_middle,
     feed_rows, g_hidden, sig_all, ada_flat) = run_ahead(
        gather_list(), line, signals, ada_weight, extra, segments, tok_near, tok_away,
        pad_rows(cotangent, padded), kmask, qmask, 2 * hidden_cols, width, 1,
    )
    act_far, tok_far, (t_qkv, t_proj, t_fc1, t_fc2, arrived, token_grad) = run_behind(
        scatter_list(), line, scale_lengths.shape[1],
        [x_f, qkv_f, proj_f, g1_f, g2_f, result, q_low, k_low, v_low, mixed],
        [grad_middle, mods, feed_rows, g_hidden, stats, boosts, kmask, qmask], width, 2,
    )
    qkv_total = t_qkv.reshape(own_rows, 2, 3, 256).transpose(2, 0, 1, 3).reshape(qkv_weight.shape)

    def both_slots(image, far, swapped):
        near = jnp.where(mine == 0, image[:half_rows], image[padded : padded + half_rows])
        first = (mine == 0) != swapped
        return jnp.stack([jnp.where(first, near, far[:half_rows]), jnp.where(first, far[:half_rows], near)])

    activations = both_slots(result, act_far, False)
    tokens_grad = both_slots(token_grad, tok_far, swap)

    all_mods = arrived[:, :, :6].reshape(n_dev, 6 * own_cols)
    signal_part = lax.dot_general(
        all_mods, ada_flat.astype(F32), (((1,), (1,)), ((), ())), precision=precise, preferred_element_type=F32
    ).reshape(n_dp, 1, slots * own_rows)
    signal_part = jnp.broadcast_to(signal_part, (n_dp, 2, slots * own_rows)).reshape(n_dev, slots * own_rows)
    signal_part = lax.all_to_all(signal_part, ("dp", "mp"), 0, 0, tiled=True)
    signal_grad = signal_part.reshape(n_dp, 2, slots, own_rows).sum(1).transpose(1, 0, 2).reshape(slots, model)
    signal_rows = sig_all[:, 0, :slots, :own_rows].reshape(n_dev, own_rows)
    ada_weight_grad = lax.dot_general(
        signal_rows, all_mods, (((0,), (0,)), ((), ())), precision=precise, preferred_element_type=F32
    ).reshape(ada_weight.shape)
    small_total = arrived[:, :, 6:].sum((0, 1))
    by_head = small_total[0].reshape(8, 2 * local_heads, entries)
    bias_total = lax.dynamic_slice_in_dim(by_head[:4], mine * local_heads, local_heads, 1)
    hidden_total = lax.dynamic_slice_in_dim(by_head[4:], mine * 2, 2, 0).reshape(fc1_bias.shape)
    scale_total = lax.dynamic_slice_in_dim(small_total[1], mine * local_heads, local_heads, 0)
    ada_bias_grad = lax.dynamic_slice_in_dim(
        jnp.sum(all_mods, 0).reshape(6, local_heads, width), lax.axis_index("dp") * entries, entries, 2
    )
    pull = jax.vjp(jax.nn.silu, cond_slots)[1]
    condition_grad = to_slots(pull(signal_grad)[0]).astype(BF16)
    return (
        activations, tokens_grad, condition_grad, ada_weight_grad, ada_bias_grad, qkv_total, bias_total[:2],
        scale_total, t_proj.T, bias_total[2:], t_fc1, hidden_total, t_fc2.T,
    )


precise = lax.Precision.HIGHEST


def row_norm(values):
    centre = jnp.mean(values, -1, keepdims=True)
    shifted = values - centre
    inverse = lax.rsqrt(jnp.mean(shifted * shifted, -1, keepdims=True) + 1e-06)
    return (shifted * inverse, inverse)


def row_norm_back(incoming, normed, inverse):
    return inverse * (
        incoming
        - jnp.mean(incoming, -1, keepdims=True)
        - normed * jnp.mean(incoming * normed, -1, keepdims=True)
    )


def gelu_tanh(values):
    return jax.nn.gelu(values, approximate=True)


def spread(shard_rows):
    return lax.all_gather(shard_rows, "mp", axis=0, tiled=True)


def collect(partial_sum):
    return lax.psum_scatter(
        partial_sum.astype(jnp.bfloat16), "mp", scatter_dimension=0, tiled=True
    ).astype(jnp.float32)


def fetch(qkv_weight, qv_bias, proj_weight, out_bias, fc1_weight, fc1_bias, fc2_weight):
    return (
        lax.all_gather(qkv_weight, "dp", axis=1, tiled=True),
        lax.all_gather(qv_bias, "dp", axis=2, tiled=True),
        lax.all_gather(proj_weight, "dp", axis=1, tiled=True),
        lax.all_gather(out_bias, "dp", axis=2, tiled=True),
        lax.all_gather(fc1_weight, "dp", axis=0, tiled=True),
        lax.all_gather(fc1_bias, "dp", axis=1, tiled=True),
        lax.all_gather(fc2_weight, "dp", axis=1, tiled=True),
    )


def settle(grad_set):
    qkv_part, qv_part, proj_part, outb_part, fc1_part, fc1b_part, fc2_part = grad_set
    return (
        lax.psum_scatter(
            qkv_part.astype(jnp.bfloat16), "dp", scatter_dimension=1, tiled=True
        ).astype(jnp.float32),
        lax.psum_scatter(
            qv_part.astype(jnp.bfloat16), "dp", scatter_dimension=2, tiled=True
        ).astype(jnp.float32),
        lax.psum_scatter(
            proj_part.astype(jnp.bfloat16), "dp", scatter_dimension=1, tiled=True
        ).astype(jnp.float32),
        lax.psum_scatter(
            outb_part.astype(jnp.bfloat16), "dp", scatter_dimension=2, tiled=True
        ).astype(jnp.float32),
        lax.psum_scatter(
            fc1_part.astype(jnp.bfloat16), "dp", scatter_dimension=0, tiled=True
        ).astype(jnp.float32),
        lax.psum_scatter(
            fc1b_part.astype(jnp.bfloat16), "dp", scatter_dimension=1, tiled=True
        ).astype(jnp.float32),
        lax.psum_scatter(
            fc2_part.astype(jnp.bfloat16), "dp", scatter_dimension=1, tiled=True
        ).astype(jnp.float32),
    )


def on_device_shared(
    tokens,
    condition,
    scale_lengths,
    order,
    cotangent,
    ada_weight,
    ada_bias,
    qkv_weight,
    qv_bias,
    head_log_scale,
    proj_weight,
    out_bias,
    fc1_weight,
    fc1_bias,
    fc2_weight,
):
    image_count, shard_rows, model_width = tokens.shape
    column_count = qkv_weight.shape[2]
    local_heads = qv_bias.shape[1]
    head_width = column_count // local_heads
    hidden_cols = fc1_weight.shape[1]
    own_start = lax.axis_index("mp") * column_count
    token_count = shard_rows * lax.axis_size("mp")
    ada_full, ada_bias_full = (
        lax.all_gather(ada_weight, "dp", axis=0, tiled=True),
        lax.all_gather(ada_bias, "dp", axis=2, tiled=True),
    )
    cond_float = condition.astype(jnp.float32)
    signal = jax.nn.silu(cond_float).astype(jnp.bfloat16)
    ada_flat = ada_full.reshape(model_width, 6 * column_count)
    mod_share = jnp.dot(
        signal, ada_flat, preferred_element_type=jnp.float32
    ) + ada_bias_full.reshape(6 * column_count).astype(jnp.float32)
    modulation = lax.all_gather(
        mod_share.reshape(image_count, 6, column_count), "mp", axis=2, tiled=True
    )
    head_boost = jnp.exp(head_log_scale)[None, :, None]
    positions = jnp.arange(token_count, dtype=jnp.int32)

    def place(vector):
        return lax.dynamic_update_slice(
            jnp.zeros((model_width,), jnp.float32), vector, (own_start,)
        )

    def own_columns(matrix):
        return lax.dynamic_slice_in_dim(matrix, own_start, column_count, 1)

    def rows_now():
        return fetch(qkv_weight, qv_bias, proj_weight, out_bias, fc1_weight, fc1_bias, fc2_weight)

    full_shapes = (
        (3, model_width, column_count),
        (2, local_heads, head_width),
        (column_count, model_width),
        (2, local_heads, head_width),
        (model_width, hidden_cols),
        (hidden_cols // head_width, head_width),
        (hidden_cols, model_width),
    )
    grad_start = tuple((jnp.zeros(shape_item, jnp.float32) for shape_item in full_shapes))

    def micro_step(micro_at, state_now):
        outputs, token_grads, mod_grads, weight_grads, scale_grad = state_now
        image_at = order[0, micro_at]
        residual = lax.dynamic_index_in_dim(tokens, image_at, 0, keepdims=False).astype(jnp.float32)
        image_mods = lax.dynamic_index_in_dim(modulation, image_at, 0, keepdims=False)
        lengths = lax.dynamic_index_in_dim(scale_lengths, image_at, 0, keepdims=False)
        out_grad = lax.dynamic_index_in_dim(cotangent, micro_at, 0, keepdims=False).astype(
            jnp.float32
        )
        qkv_full, qv_full, proj_full, outb_full, fc1_full, fc1b_full, fc2_full = rows_now()
        steps = jnp.arange(lengths.shape[0], dtype=jnp.int32)
        scale_ends = jnp.sum(jnp.where(steps[None, :] <= steps[:, None], lengths[None, :], 0), 1)
        scale_of = jnp.sum((positions[:, None] >= scale_ends[None, :]).astype(jnp.int32), 1)
        allowed = (scale_of[None, :] <= scale_of[:, None])[None]
        normed_one, inverse_one = row_norm(residual)
        input_one = spread(
            (normed_one * (1.0 + image_mods[2]) + image_mods[4]).astype(jnp.bfloat16)
        )
        projected = jnp.einsum(
            "td,cde->cte", input_one, qkv_full, preferred_element_type=jnp.float32
        )
        bias_pair = qv_full.reshape(2, column_count).astype(jnp.float32)
        queries = (projected[0] + bias_pair[0]).reshape(token_count, local_heads, head_width)
        keys_raw = projected[1].reshape(token_count, local_heads, head_width)
        values_low = (
            (projected[2] + bias_pair[1])
            .astype(jnp.bfloat16)
            .reshape(token_count, local_heads, head_width)
        )
        query_inv = lax.rsqrt(jnp.sum(queries * queries, -1, keepdims=True) + 1e-06)
        key_inv = lax.rsqrt(jnp.sum(keys_raw * keys_raw, -1, keepdims=True) + 1e-06)
        query_unit = queries * query_inv
        key_unit = keys_raw * key_inv
        query_low = (query_unit * head_boost).astype(jnp.bfloat16)
        key_low = key_unit.astype(jnp.bfloat16)

        def masked_scores():
            raw_scores = jnp.einsum(
                "qhd,khd->hqk", query_low, key_low, preferred_element_type=jnp.float32
            )
            return jnp.where(allowed, raw_scores, -1e30)

        scores = masked_scores()
        row_peak = jnp.max(scores, -1, keepdims=True)
        exp_terms = jnp.exp(scores - row_peak)
        totals = jnp.sum(exp_terms, -1, keepdims=True)
        log_total = row_peak + jnp.log(totals)
        soft_weights = exp_terms / totals
        mixed_heads = (
            jnp.einsum(
                "hqk,khd->qhd",
                soft_weights.astype(jnp.bfloat16),
                values_low,
                preferred_element_type=jnp.float32,
            )
            .astype(jnp.bfloat16)
            .reshape(token_count, column_count)
        )
        attended = collect(
            jnp.dot(mixed_heads, proj_full, preferred_element_type=jnp.float32)
            + place(outb_full[0].reshape(column_count).astype(jnp.float32))
        )
        middle = residual + image_mods[0] * attended
        normed_two, inverse_two = row_norm(middle)
        input_two = spread(
            (normed_two * (1.0 + image_mods[3]) + image_mods[5]).astype(jnp.bfloat16)
        )
        hidden = jnp.dot(
            input_two, fc1_full, preferred_element_type=jnp.float32
        ) + fc1b_full.reshape(hidden_cols).astype(jnp.float32)
        activated = gelu_tanh(hidden).astype(jnp.bfloat16)
        branch_out = collect(
            jnp.dot(activated, fc2_full, preferred_element_type=jnp.float32)
            + place(outb_full[1].reshape(column_count).astype(jnp.float32))
        )
        result = (middle + image_mods[1] * branch_out).astype(jnp.bfloat16)
        outputs = lax.dynamic_update_index_in_dim(outputs, result, micro_at, 0)
        qkv_back, qv_back, proj_back, outb_back, fc1_back, fc1b_back, fc2_back = rows_now()
        grad_branch = spread((image_mods[1] * out_grad).astype(jnp.bfloat16))
        gamma_two_grad = jnp.sum(out_grad * branch_out, 0)
        fc2_grad = jnp.dot(activated.T, grad_branch, preferred_element_type=jnp.float32)
        bias_two_grad = jnp.sum(own_columns(grad_branch).astype(jnp.float32), 0)
        act_grad = jnp.dot(grad_branch, fc2_back.T, preferred_element_type=jnp.float32)
        gelu_pull = jax.vjp(gelu_tanh, hidden)[1]
        hidden_grad = gelu_pull(act_grad)[0].astype(jnp.bfloat16)
        fc1_grad = jnp.dot(input_two.T, hidden_grad, preferred_element_type=jnp.float32)
        fc1b_grad = jnp.sum(hidden_grad.astype(jnp.float32), 0).reshape(
            hidden_cols // head_width, head_width
        )
        input_two_grad = collect(
            jnp.dot(hidden_grad, fc1_back.T, preferred_element_type=jnp.float32)
        )
        scale_two_grad = jnp.sum(input_two_grad * normed_two, 0)
        shift_two_grad = jnp.sum(input_two_grad, 0)
        middle_grad = out_grad + row_norm_back(
            input_two_grad * (1.0 + image_mods[3]), normed_two, inverse_two
        )
        grad_attended = spread((image_mods[0] * middle_grad).astype(jnp.bfloat16))
        gamma_one_grad = jnp.sum(middle_grad * attended, 0)
        proj_grad = jnp.dot(mixed_heads.T, grad_attended, preferred_element_type=jnp.float32)
        bias_one_grad = jnp.sum(own_columns(grad_attended).astype(jnp.float32), 0)
        mixed_grad = (
            jnp.dot(grad_attended, proj_back.T, preferred_element_type=jnp.float32)
            .astype(jnp.bfloat16)
            .reshape(token_count, local_heads, head_width)
        )
        soft_again = jnp.exp(masked_scores() - log_total)
        value_grad = jnp.einsum(
            "hqk,qhd->khd",
            soft_again.astype(jnp.bfloat16),
            mixed_grad,
            preferred_element_type=jnp.float32,
        )
        soft_grad = jnp.einsum(
            "qhd,khd->hqk", mixed_grad, values_low, preferred_element_type=jnp.float32
        )
        score_grad = (
            soft_again * (soft_grad - jnp.sum(soft_again * soft_grad, -1, keepdims=True))
        ).astype(jnp.bfloat16)
        query_low_grad = jnp.einsum(
            "hqk,khd->qhd", score_grad, key_low, preferred_element_type=jnp.float32
        )
        key_low_grad = jnp.einsum(
            "hqk,qhd->khd", score_grad, query_low, preferred_element_type=jnp.float32
        )
        head_grad = jnp.sum(query_low_grad * query_unit * head_boost, (0, 2))
        query_unit_grad = query_low_grad * head_boost
        query_grad = query_inv * (
            query_unit_grad - query_unit * jnp.sum(query_unit_grad * query_unit, -1, keepdims=True)
        )
        key_grad = key_inv * (
            key_low_grad - key_unit * jnp.sum(key_low_grad * key_unit, -1, keepdims=True)
        )
        triple_grad = jnp.stack(
            [
                query_grad.reshape(token_count, column_count),
                key_grad.reshape(token_count, column_count),
                value_grad.reshape(token_count, column_count),
            ]
        ).astype(jnp.bfloat16)
        qkv_grad = jnp.einsum(
            "td,cte->cde", input_one, triple_grad, preferred_element_type=jnp.float32
        )
        pair_sums = jnp.sum(triple_grad.astype(jnp.float32), 1)
        qv_grad = jnp.stack([pair_sums[0], pair_sums[2]]).reshape(2, local_heads, head_width)
        input_one_grad = collect(
            jnp.einsum("cte,cde->td", triple_grad, qkv_back, preferred_element_type=jnp.float32)
        )
        scale_one_grad = jnp.sum(input_one_grad * normed_one, 0)
        shift_one_grad = jnp.sum(input_one_grad, 0)
        residual_grad = middle_grad + row_norm_back(
            input_one_grad * (1.0 + image_mods[2]), normed_one, inverse_one
        )
        token_grads = lax.dynamic_update_index_in_dim(
            token_grads, residual_grad.astype(jnp.bfloat16), image_at, 0
        )
        image_mod_grad = jnp.stack(
            [
                gamma_one_grad,
                gamma_two_grad,
                scale_one_grad,
                scale_two_grad,
                shift_one_grad,
                shift_two_grad,
            ]
        )
        mod_grads = lax.dynamic_update_index_in_dim(mod_grads, image_mod_grad, image_at, 0)
        outb_grad = jnp.stack([bias_one_grad, bias_two_grad]).reshape(2, local_heads, head_width)
        local_grads = (qkv_grad, qv_grad, proj_grad, outb_grad, fc1_grad, fc1b_grad, fc2_grad)
        weight_grads = tuple(
            (running + addend for running, addend in zip(weight_grads, local_grads))
        )
        return (outputs, token_grads, mod_grads, weight_grads, scale_grad + head_grad)

    start_state = (
        jnp.zeros(tokens.shape, jnp.bfloat16),
        jnp.zeros(tokens.shape, jnp.bfloat16),
        jnp.zeros((image_count, 6, model_width), jnp.float32),
        grad_start,
        jnp.zeros((local_heads,), jnp.float32),
    )
    outputs, token_grads, mod_grads, weight_grads, scale_grad = lax.fori_loop(
        0, image_count, micro_step, start_state
    )
    shard_grads = settle(weight_grads)
    mod_share_grad = lax.psum_scatter(
        mod_grads.astype(jnp.bfloat16), "mp", scatter_dimension=2, tiled=True
    ).astype(jnp.float32)
    flat_grad = mod_share_grad.reshape(image_count, 6 * column_count)
    ada_grad = jnp.dot(
        signal.astype(jnp.float32).T,
        flat_grad,
        precision=precise,
        preferred_element_type=jnp.float32,
    ).reshape(model_width, 6, column_count)
    ada_bias_grad = jnp.sum(mod_share_grad, 0).reshape(6, local_heads, head_width)
    signal_grad = lax.psum(
        jnp.dot(
            flat_grad,
            ada_flat.astype(jnp.float32).T,
            precision=precise,
            preferred_element_type=jnp.float32,
        ),
        "mp",
    )
    silu_pull = jax.vjp(jax.nn.silu, cond_float)[1]
    condition_grad = silu_pull(signal_grad)[0].astype(jnp.bfloat16)
    ada_shard, ada_bias_shard = (
        lax.psum_scatter(
            ada_grad.astype(jnp.bfloat16), "dp", scatter_dimension=0, tiled=True
        ).astype(jnp.float32),
        lax.psum_scatter(
            ada_bias_grad.astype(jnp.bfloat16), "dp", scatter_dimension=2, tiled=True
        ).astype(jnp.float32),
    )
    head_scale_grad = lax.psum(scale_grad, "dp")
    qkv_shard, qv_shard, proj_shard, outb_shard, fc1_shard, fc1b_shard, fc2_shard = shard_grads
    return (
        outputs,
        token_grads,
        condition_grad,
        ada_shard,
        ada_bias_shard,
        qkv_shard,
        qv_shard,
        head_scale_grad,
        proj_shard,
        outb_shard,
        fc1_shard,
        fc1b_shard,
        fc2_shard,
    )


def solution(mesh):
    in_specs = (
        P("dp", "mp", None),
        P("dp", None),
        P("dp", None),
        P("dp", None),
        P("dp", "mp", None),
        P("dp", None, "mp"),
        P(None, "mp", "dp"),
        P(None, "dp", "mp"),
        P(None, "mp", "dp"),
        P("mp"),
        P("mp", "dp"),
        P(None, "mp", "dp"),
        P("dp", "mp"),
        P("mp", "dp"),
        P("mp", "dp"),
    )
    out_specs = (
        P("dp", "mp", None),
        P("dp", "mp", None),
        P("dp", None),
        P("dp", None, "mp"),
        P(None, "mp", "dp"),
        P(None, "dp", "mp"),
        P(None, "mp", "dp"),
        P("mp"),
        P("mp", "dp"),
        P(None, "mp", "dp"),
        P("dp", "mp"),
        P("mp", "dp"),
        P("mp", "dp"),
    )
    line, spare = divmod(mesh.shape["dp"], 4)
    paired = mesh.shape["mp"] == 2 and spare == 0 and line > 1
    return jax.shard_map(
        on_device_paired if paired else on_device_shared, mesh=mesh, in_specs=in_specs, out_specs=out_specs, check_vma=False
    )
```

```python
import functools
import jax
import jax.numpy as jnp
from jax import lax
from jax.experimental import pallas as pl
from jax.experimental.pallas import tpu as pltpu
from jax.sharding import PartitionSpec as P

F32 = jnp.float32
BF16 = jnp.bfloat16
MESH = pl.DeviceIdType.MESH
LOG2E = 1.4426950408889634
VMEM_LIMIT = 60 * 1024 * 1024


def mm(a, b):
    return jnp.dot(a, b, preferred_element_type=F32)


def mm_nt(a, b):
    return lax.dot_general(a, b, (((1,), (1,)), ((), ())), preferred_element_type=F32)


def mm_tn(a, b):
    return lax.dot_general(a, b, (((0,), (0,)), ((), ())), preferred_element_type=F32)


def norm_rows(values):
    centre = jnp.mean(values, -1, keepdims=True)
    shifted = values - centre
    inverse = lax.rsqrt(jnp.mean(shifted * shifted, -1, keepdims=True) + 1e-06)
    return shifted * inverse, inverse


def norm_rows_back(incoming, normed, inverse):
    return inverse * (
        incoming
        - jnp.mean(incoming, -1, keepdims=True)
        - normed * jnp.mean(incoming * normed, -1, keepdims=True)
    )


def split_three(values):
    high = values.astype(BF16)
    rest = values - high.astype(F32)
    middle = rest.astype(BF16)
    return high, middle, (rest - middle.astype(F32)).astype(BF16)


def build_masks(lengths, half_rows, padded):
    count = lengths.shape[0]
    steps = jnp.arange(count, dtype=jnp.int32)
    ends = jnp.sum(jnp.where(steps[None, :] <= steps[:, None], lengths[None, :], 0), 1)
    place = jnp.arange(2 * padded, dtype=jnp.int32)
    part, inside = place // padded, place % padded
    token = part * half_rows + inside
    level = jnp.sum((token[None, :] >= ends[:, None]).astype(jnp.int32), 0)
    real = inside < half_rows
    entry = jnp.arange(16, dtype=jnp.int32)[:, None]
    key_level = jnp.where(real, level, count)[None]
    kmask = (entry == key_level) | ((entry > count) & (entry < count + 4))
    query_level = jnp.where(real, level, count - 1)[None]
    qmask = (entry > query_level) & (entry <= count)
    return kmask.astype(BF16), jnp.where(qmask, -32768.0, 0.0).astype(BF16)


def device(z, x, c, y):
    return (z * 4 + x * 2 + c, y)


def where_am_i():
    dp, y = lax.axis_index("dp"), lax.axis_index("mp")
    return dp // 4, (dp // 2) % 2, dp % 2, y


def remote(source, target, send, recv, to):
    return pltpu.make_async_remote_copy(source, target, send, recv, device_id=to, device_id_type=MESH)


def greet_all(total):
    me = lax.axis_index("dp") * 2 + lax.axis_index("mp")
    barrier = pltpu.get_barrier_semaphore()

    def signal(step, carry):
        to = lax.rem(me + step, total)
        pl.semaphore_signal(barrier, inc=1, device_id=(to // 2, to % 2), device_id_type=MESH)
        return carry

    lax.fori_loop(1, total, signal, 0)
    pl.semaphore_wait(barrier, total - 1)


class Exchange:
    def __init__(self, total, block_of, landing, send, recv):
        self.total, self.block_of, self.landing, self.send, self.recv = total, block_of, landing, send, recv
        self.me = lax.axis_index("dp") * 2 + lax.axis_index("mp")

    def copy(self, step):
        to = lax.rem(self.me + step, self.total)
        return remote(
            self.block_of(to), self.landing, self.send.at[step], self.recv.at[step], (to // 2, to % 2)
        )

    def own(self):
        return pltpu.make_async_copy(self.block_of(self.me), self.landing, self.send.at[0])

    def each(self, act):
        def body(step, carry):
            act(self.copy(step))
            return carry

        lax.fori_loop(1, self.total, body, 0)

    def start(self):
        self.own().start()
        self.each(lambda copy: copy.start())

    def wait(self):
        self.own().wait()
        self.each(lambda copy: copy.wait())


class Ticks:
    def __init__(self, count, stages, offsets):
        self.count, self.stages, self.offsets = count, stages, offsets
        self.total = count + offsets[-1]

    def run(self, since, until):
        for tick in range(since, until):
            for stage, offset in zip(self.stages, self.offsets):
                if 0 <= tick - offset < self.count:
                    stage(tick - offset)


class Gather:
    def __init__(self, batches, line, sources, outs, z_send, z_recv, send_sem, recv_sem):
        self.batches, self.line, self.sources, self.outs = batches, line, sources, outs
        self.chunks = [chunk for batch in batches for chunk in batch]
        self.z_send, self.z_recv, self.send_sem, self.recv_sem = z_send, z_recv, send_sem, recv_sem
        self.z, self.x, self.c, self.y = where_am_i()
        z, x, c, y = self.z, self.x, self.c, self.y
        self.x_side, self.y_side, self.sibling = device(z, 1 - x, c, y), device(z, x, c, 1 - y), device(z, x, 1 - c, y)

    def part(self, k, yy, zz, xx):
        seg, _, start, cols, row, rows = self.chunks[k]
        return self.outs[seg].at[yy, zz, xx, self.c, pl.ds(row, rows), pl.ds(start, cols)]

    def late(self, k):
        return self.chunks[k][1] >= 2

    def mine(self, k):
        seg, _, start, cols, row, rows = self.chunks[k]
        return self.sources[seg].at[pl.ds(row, rows), pl.ds(start, cols)]

    def plane(self, k, owner):
        return self.part(k, slice(None), owner, slice(None))

    def along(self, k, step):
        to = device(lax.rem(self.z + step, self.line), self.x, self.c, self.y)
        sems = (self.z_send.at[k, step - 1], self.z_recv.at[k, step - 1])
        if self.late(k):
            return remote(self.plane(k, self.z), self.plane(k, self.z), *sems, to)
        return remote(self.mine(k), self.part(k, self.y, self.z, self.x), *sems, to)

    def group(self, k, slot, at, target):
        ref = self.part(k, at[0], self.z if self.late(k) else slice(None), at[1])
        source = self.mine(k) if self.late(k) and slot < 2 else ref
        return remote(source, ref, self.send_sem.at[k, slot], self.recv_sem.at[k, slot], target)

    def aside(self, k, step):
        ref = self.plane(k, lax.rem(self.z + self.line - step, self.line))
        return remote(ref, ref, self.send_sem.at[k, 3 + step], self.recv_sem.at[k, 3 + step], self.sibling)

    def groups(self, k):
        x, y = self.x, self.y
        if self.chunks[k][1] % 2 == 0:
            return [(y, x), (y, 1 - x), (1 - y, x), (1 - y, 1 - x)], self.x_side, self.y_side
        return [(y, x), (1 - y, x), (y, 1 - x), (1 - y, 1 - x)], self.y_side, self.x_side

    def step(self, k, stage):
        order, first, second = self.groups(k)
        if self.late(k):
            if stage == 0:
                self.group(k, 0, order[0], first).start()
                self.group(k, 1, order[0], second).start()
            elif stage == 1:
                self.group(k, 0, order[1], first).wait_recv()
                self.group(k, 2, order[1], second).start()
            elif stage == 2:
                self.group(k, 1, order[2], second).wait_recv()
                self.group(k, 2, order[3], second).wait_recv()
                for step in range(1, self.line):
                    self.along(k, step).start()
                self.aside(k, 0).start()
            else:
                for step in range(1, self.line):
                    self.along(k, step).wait_recv()
                    self.aside(k, step).start()
        elif stage == 0:
            for step in range(1, self.line):
                self.along(k, step).start()
        elif stage == 1:
            for step in range(1, self.line):
                self.along(k, step).wait_recv()
            self.group(k, 0, order[0], first).start()
            self.group(k, 1, order[0], second).start()
            self.group(k, 3, order[0], self.sibling).start()
        elif stage == 2:
            self.group(k, 0, order[1], first).wait_recv()
            self.group(k, 2, order[1], second).start()
            self.group(k, 4, order[1], self.sibling).start()
        else:
            self.group(k, 1, order[2], second).wait_recv()
            self.group(k, 5, order[2], self.sibling).start()
            self.group(k, 2, order[3], second).wait_recv()
            self.group(k, 6, order[3], self.sibling).start()

    def members(self, batch):
        before = sum(len(b) for b in self.batches[:batch])
        return range(before, before + len(self.batches[batch]))

    def stages(self):
        def make(stage):
            def act(batch):
                for k in self.members(batch):
                    self.step(k, stage)

            return act

        return [make(stage) for stage in range(4)]

    def finish(self, batch):
        for k in self.members(batch):
            order, _, _ = self.groups(k)
            for slot, at in ((3, 0), (4, 1), (5, 2), (6, 3)):
                (self.aside(k, at) if self.late(k) else self.group(k, slot, order[at], self.sibling)).wait_recv()

    def sent(self):
        for k in range(len(self.chunks)):
            order, _, _ = self.groups(k)
            for step in range(1, self.line):
                self.along(k, step).wait_send()
            for slot, at in ((0, 0), (1, 0), (2, 1)):
                self.group(k, slot, order[at], self.sibling).wait_send()
            for slot, at in ((3, 0), (4, 1), (5, 2), (6, 3)):
                (self.aside(k, at) if self.late(k) else self.group(k, slot, order[at], self.sibling)).wait_send()


def add_into(target, source, pieces, target_at, source_at):
    def body(i, carry):
        t, s = target_at(i), source_at(i)
        target[t] = target[t] + source[s]
        return carry

    lax.fori_loop(0, pieces, body, 0)


class Scatter:
    def __init__(self, batches, line, sources, totals, landing, core_s, own_s, first_b, second_b, line_b, plane_b, sems):
        self.batches, self.line, self.sources, self.totals = batches, line, sources, totals
        self.chunks = [chunk for batch in batches for chunk in batch]
        self.landing, self.core_s, self.own_s = landing, core_s, own_s
        self.first_b, self.second_b, self.line_b, self.plane_b = first_b, second_b, line_b, plane_b
        self.own_sem, self.load_sem, self.send_sem, self.recv_sem, self.z_send, self.z_recv = sems
        self.z, self.x, self.c, self.y = where_am_i()
        z, x, c, y = self.z, self.x, self.c, self.y
        self.x_side, self.y_side, self.sibling = device(z, 1 - x, c, y), device(z, x, c, 1 - y), device(z, x, 1 - c, y)
        self.spot = {}
        for b, batch in enumerate(batches):
            column = 0
            for k in self.members(b):
                self.spot[k] = (b, column)
                column += self.chunks[k][3]

    def members(self, batch):
        before = sum(len(b) for b in self.batches[:batch])
        return range(before, before + len(self.batches[batch]))

    def source(self, k, c):
        seg, _, start, cols = self.chunks[k]
        return self.sources[seg].at[:, :, :, c, :, pl.ds(start, cols)]

    def core_copy(self, k):
        return remote(
            self.source(k, 1 - self.c), self.landing[k], self.send_sem.at[k, 0], self.recv_sem.at[k, 0], self.sibling
        )

    def core(self, k):
        batch, column = self.spot[k]
        return self.core_s.at[batch % 4, :, :, :, :, pl.ds(column, self.chunks[k][3])]

    def own(self, k):
        batch, column = self.spot[k]
        return self.own_s.at[batch % 2, :, :, :, :, pl.ds(column, self.chunks[k][3])]

    def own_copy(self, k):
        return pltpu.make_async_copy(self.source(k, self.c), self.own(k), self.own_sem.at[k])

    def load_copy(self, k):
        return pltpu.make_async_copy(self.landing[k], self.core(k), self.load_sem.at[k])

    def late(self, k):
        return self.chunks[k][1] >= 2

    def first_copy(self, k):
        x, y, sems = self.x, self.y, (self.send_sem.at[k, 1], self.recv_sem.at[k, 1])
        even = self.chunks[k][1] % 2 == 0
        if self.late(k):
            source = self.plane_b[k].at[1 - y] if even else self.plane_b[k].at[:, 1 - x]
        else:
            source = self.core(k).at[1 - y] if even else self.core(k).at[:, :, 1 - x]
        return remote(source, self.first_b[k], *sems, self.y_side if even else self.x_side)

    def second_copy(self, k):
        x, y, first = self.x, self.y, self.first_b[k]
        sems = (self.send_sem.at[k, 2], self.recv_sem.at[k, 2])
        even = self.chunks[k][1] % 2 == 0
        if self.late(k):
            source = first.at[1 - x] if even else first.at[1 - y]
        else:
            source = first.at[:, 1 - x] if even else first.at[1 - y]
        return remote(source, self.second_b[k], *sems, self.x_side if even else self.y_side)

    def line_copy(self, k, step):
        owner = lax.rem(self.z + step, self.line)
        source = self.core(k).at[:, owner] if self.late(k) else self.second_b[k].at[owner]
        return remote(
            source, self.line_b[k].at[step - 1],
            self.z_send.at[k, step - 1], self.z_recv.at[k, step - 1], device(owner, self.x, self.c, self.y),
        )

    def step(self, k, stage):
        line, x, y, z = self.line, self.x, self.y, self.z
        early = self.chunks[k][1] == 0
        if stage == 0:
            self.core_copy(k).start()
        elif stage == 1:
            self.core_copy(k).wait_recv()
            self.load_copy(k).start()
            self.own_copy(k).start()
        elif stage == 2:
            self.load_copy(k).wait()
            self.own_copy(k).wait()
            at = lambda i: (i // (2 * line), (i // 2) % line, i % 2)
            add_into(self.core(k), self.own(k), 4 * line, at, at)
            if self.late(k):
                for step in range(1, line):
                    self.line_copy(k, step).start()
            else:
                self.first_copy(k).start()
        elif self.late(k):
            self.late_step(k, stage)
        elif stage == 3:
            self.first_copy(k).wait_recv()
            if early:
                there, here = (lambda i: (i // 2, i % 2)), (lambda i: (y, i // 2, i % 2))
            else:
                there, here = (lambda i: (i // line, i % line)), (lambda i: (i // line, i % line, x))
            add_into(self.first_b[k], self.core(k), 2 * line, there, here)
            self.second_copy(k).start()
            self.first_copy(k).wait_send()
        elif stage == 4:
            self.second_copy(k).wait_recv()
            here = (lambda i: (i, x)) if early else (lambda i: (y, i))
            add_into(self.second_b[k], self.first_b[k], line, lambda i: (i,), here)
            for step in range(1, line):
                self.line_copy(k, step).start()
        else:
            seg, _, start, cols = self.chunks[k]
            total = self.second_b[k][z].astype(F32)
            for step in range(1, line):
                self.line_copy(k, step).wait_recv()
                total = total + self.line_b[k][step - 1].astype(F32)
            self.totals[seg][:, pl.ds(start, cols)] = total

    def late_step(self, k, stage):
        line, x, y, z = self.line, self.x, self.y, self.z
        even = self.chunks[k][1] % 2 == 0
        if stage == 3:
            for step in range(1, line):
                self.line_copy(k, step).wait_recv()

            def body(i, carry):
                at = (i // 2, i % 2)
                total = self.core(k)[i // 2, z, i % 2].astype(F32)
                for step in range(1, line):
                    total = total + self.line_b[k][(step - 1, *at)].astype(F32)
                self.plane_b[k][at] = total.astype(BF16)
                return carry

            lax.fori_loop(0, 4, body, 0)
            self.first_copy(k).start()
            for step in range(1, line):
                self.line_copy(k, step).wait_send()
        elif stage == 4:
            self.first_copy(k).wait_recv()
            here = (lambda i: (y, i)) if even else (lambda i: (i, x))
            add_into(self.first_b[k], self.plane_b[k], 2, lambda i: (i,), here)
            self.second_copy(k).start()
        else:
            seg, _, start, cols = self.chunks[k]
            self.second_copy(k).wait_recv()
            near = self.first_b[k][x if even else y]
            self.totals[seg][:, pl.ds(start, cols)] = near.astype(F32) + self.second_b[k][...].astype(F32)

    def stages(self):
        def make(stage):
            def act(batch):
                for k in self.members(batch):
                    self.step(k, stage)

            return act

        return [make(stage) for stage in range(6)]

    def sent(self):
        for k in range(len(self.chunks)):
            self.core_copy(k).wait_send()
            self.second_copy(k).wait_send()
            if self.late(k):
                self.first_copy(k).wait_send()
                continue
            for step in range(1, self.line):
                self.line_copy(k, step).wait_send()


def switch_on(index, cases):
    for at, act in cases.items():
        pl.when(index == at)(act)


def columns(start, size):
    return pl.ds(pl.multiple_of(start, 128), size)


def owner_maps(owners, entries, width, model):
    inner = model // width * entries
    at = lax.broadcasted_iota(jnp.int32, (inner, model), 1)
    place = lax.broadcasted_iota(jnp.int32, (inner, model), 0)
    spread = jnp.where(at // width * entries + at % entries == place, 1.0, 0.0).astype(BF16)
    at = lax.broadcasted_iota(jnp.int32, (owners, model), 1)
    owner = lax.broadcasted_iota(jnp.int32, (owners, model), 0)
    return spread, jnp.where(at % width // entries == owner, 1.0, 0.0)


def ahead_kernel(batches, line, width, *refs):
    (signals, ada, extra, seg_qkv, seg_proj, seg_fc1, seg_fc2, tok_near, tok_away, cot, kmask_ref, qmask_ref,
     qkv_f, proj_f, fc1_f, fc2_f, g1_f, g2_f, ql_f, kl_f, vl_f, mix_f, x_f,
     boosts, mod_ref, stat_ref, out_ref, gmid_ref, rows_ref, gb1_ref, sig_s, ada_flat,
     products, arrived, vecs, hidden_bias, x_s, ql_ref, kl_ref, vl_ref, mix_ref, att_ref, cot_s, one_s, acc_s, mid_s, twot_s, back_s, backt_s, gacc_s, w_s, grad_s,
     a_send, a_recv, b_send, b_recv, save_sem, local_sem, pair_sem, z_send, z_recv, send_sem, recv_sem, w_sem, grad_sem) = refs
    z, x, c, y = where_am_i()
    total = 8 * line
    padded, model = tok_near.shape
    half_cols = mod_ref.shape[1] // 2
    heads = 256 // width
    outs = [qkv_f, proj_f, fc1_f, fc2_f]
    own = [
        pltpu.make_async_copy(i, o.at[y, z, x, c], local_sem.at[s])
        for s, (i, o) in enumerate(zip([seg_qkv, seg_proj, seg_fc1, seg_fc2], outs))
    ]
    for copy in own:
        copy.start()
    mine = pl.ds(y * padded, padded)
    pairs = [
        (
            pltpu.make_async_copy(near, inside.at[mine], pair_sem.at[p, 0]),
            remote(away, inside.at[mine], pair_sem.at[p, 1], pair_sem.at[p, 2], device(z, x, c, 1 - y)),
        )
        for p, (near, away, inside) in enumerate(((tok_near, tok_away, x_s), (cot.at[y], cot.at[1 - y], cot_s)))
    ]
    me = (lax.axis_index("dp"), y)
    signal_exchange = Exchange(total, lambda to: signals.at[to // 2], sig_s.at[me], b_send, b_recv)
    exchange = Exchange(total, lambda to: products.at[to // 2, to % 2], arrived.at[me], a_send, a_recv)
    gather = Gather(
        batches, line, [seg_qkv, seg_proj, seg_fc1, seg_fc2], outs, z_send, z_recv, send_sem, recv_sem
    )
    ticks = Ticks(len(batches), gather.stages(), (0, 1, 3, 5))
    greet_all(total)
    signal_exchange.start()
    ticks.run(0, 1)
    for copy in pairs[0]:
        copy.start()
    for copy in own:
        copy.wait()

    def load_attend(i):
        half, sub, slot = i % 2, i // 2, i % 2
        return [
            pltpu.make_async_copy(
                qkv_f.at[half, :, :, :, :, pl.ds(sub * 768, 768)], w_s.at[slot, :, :, :, :, pl.ds(0, 768)],
                w_sem.at[slot, 0],
            ),
            pltpu.make_async_copy(
                proj_f.at[half, :, :, :, :, pl.ds(sub * 256, 256)], w_s.at[slot, :, :, :, :, pl.ds(768, 256)],
                w_sem.at[slot, 1],
            ),
        ]

    def load_feed(half, part):
        return [
            pltpu.make_async_copy(
                ref.at[half, :, :, :, :, columns(part * 512, 512)],
                w_s.at[half, :, :, :, :, pl.ds(at * 512, 512)], w_sem.at[half, at],
            )
            for at, ref in enumerate((fc1_f, fc2_f))
        ]

    def start_loads(copies):
        for copy in copies:
            copy.start()

    def wait_loads(copies):
        for copy in copies:
            copy.wait()

    for j in range(6):
        ada_flat[:, j * half_cols : (j + 1) * half_cols] = ada[:, j, :]
    signal_exchange.wait()
    slots, owners = sig_s.shape[1], sig_s.shape[0]
    for slot in range(slots):
        rows_in = sig_s[:, 0, slot, : ada.shape[0]].astype(BF16)
        for j in range(8):
            block = jnp.broadcast_to(extra[j : j + 1], (owners, half_cols))
            if j < 6:
                block = block + mm(rows_in, ada_flat[:, j * half_cols : (j + 1) * half_cols])
            products[:, slot, j, :] = block
    exchange.start()
    ticks.run(1, 2)
    ticks.run(2, 4)
    exchange.wait()
    for half in range(2):
        mod_ref[:, half * half_cols : (half + 1) * half_cols] = jnp.sum(arrived[:, half], 0)
    entries = width // owners
    spread, owner_of = owner_maps(owners, entries, width, model)
    letters = [arrived[:, half, 6, :] for half in range(2)]
    piece = heads * entries * 2
    blocks = [
        jnp.concatenate([letter[:, r * piece : (r + 1) * piece] for letter in letters], 1) for r in range(4)
    ] + [
        letters[half][:, (4 + 2 * part) * piece : (6 + 2 * part) * piece] for half in range(2) for part in range(2)
    ]
    turned_out = mm(jnp.concatenate(blocks, 0).astype(BF16), spread)
    for r in range(8):
        row = jnp.sum(turned_out[r * owners : (r + 1) * owners] * owner_of, 0, keepdims=True)
        if r < 4:
            vecs[r : r + 1] = row
        else:
            hidden_bias[0:1, (r - 4) * model : (r - 3) * model] = row
    boosts[...] = jnp.zeros_like(boosts)
    for half in range(2):
        lift = jnp.exp(arrived[0, half, 7:8, : 2 * heads])
        for sub in range(2):
            boosts[half * 2 + sub, 0:1, 0:heads] = lift[:, sub * heads : (sub + 1) * heads]
    wait_loads(pairs[0])
    normed, _ = norm_rows(x_s[...].astype(F32))
    one_s[...] = (normed * (1.0 + mod_ref[2:3]) + mod_ref[4:5]).astype(BF16)
    acc_s[...] = jnp.zeros_like(acc_s)
    ticks.run(4, 7)
    gather.finish(0)
    gather.finish(1)
    start_loads(load_attend(0))
    start_loads(load_attend(1))
    ones = jnp.ones((x_s.shape[0], width), BF16)

    def attend(i, carry):
        def second_half():
            ticks.run(8, 9)
            gather.finish(2)
            gather.finish(3)
            start_loads(load_attend(2))
            start_loads(load_attend(3))

        def with_pair():
            start_loads(pairs[1])
            ticks.run(7, 8)

        switch_on(i, {1: with_pair, 2: second_half, 3: lambda: ticks.run(9, 10)})

        slot = lax.rem(i, 2)
        at = slot * 2 + i // 2
        wait_loads([
            pltpu.make_async_copy(
                qkv_f.at[0, :, :, :, :, pl.ds(0, 768)], w_s.at[slot, :, :, :, :, pl.ds(0, 768)], w_sem.at[slot, 0]
            ),
            pltpu.make_async_copy(
                proj_f.at[0, :, :, :, :, pl.ds(0, 256)], w_s.at[slot, :, :, :, :, pl.ds(768, 256)], w_sem.at[slot, 1]
            ),
        ])
        cols = columns(at * 256, 256)
        turned = pl.ds(pl.multiple_of(at * 256, 256), 256)
        weights = w_s[slot].reshape(model, 1024)
        projected = mm(one_s[...], weights[:, :768])
        queries = projected[:, :256] + vecs[0:1, cols]
        keys = projected[:, 256:512]
        values = (projected[:, 512:] + vecs[1:2, cols]).astype(BF16)
        vl_ref[:, cols] = values
        q_turned, k_turned = queries.T, keys.T
        boost = boosts[at]
        kmask, qmask = kmask_ref[...], qmask_ref[...]
        q_low, k_low, mixed, q_inv, k_inv, totals = [], [], [], [], [], []
        for head in range(heads):
            part = slice(head * width, (head + 1) * width)
            q_now, k_now = q_turned[part], k_turned[part]
            q_scale = lax.rsqrt(jnp.sum(q_now * q_now, 0, keepdims=True) + 1e-06)
            k_scale = lax.rsqrt(jnp.sum(k_now * k_now, 0, keepdims=True) + 1e-06)
            q_bf = (q_now * q_scale * boost[0:1, head : head + 1]).astype(BF16)
            k_bf = (k_now * k_scale).astype(BF16)
            scaled = q_bf.astype(F32) * LOG2E
            high = scaled.astype(BF16)
            rest = (scaled - high.astype(F32)).astype(BF16)
            q_all = jnp.concatenate([high, rest, qmask], 0)
            k_all = jnp.concatenate([k_bf, k_bf, kmask], 0)
            soft = jnp.exp2(mm_tn(q_all, k_all)).astype(BF16)
            summed = mm(soft, jnp.concatenate([values[:, part], ones], 1))
            total_now = summed[:, width:]
            mixed.append((summed[:, :width] / total_now).astype(BF16))
            totals.append(total_now[:, 0:1])
            q_low.append(q_bf)
            k_low.append(k_bf)
            q_inv.append(q_scale)
            k_inv.append(k_scale)
        mixed_all = jnp.concatenate(mixed, 1)
        mix_ref[:, cols] = mixed_all
        ql_ref[turned, :] = jnp.concatenate(q_low, 0)
        kl_ref[turned, :] = jnp.concatenate(k_low, 0)
        stat_ref[at, 0] = jnp.concatenate(q_inv + k_inv, 0)
        stat_ref[at, 1] = jnp.log2(jnp.concatenate(totals + totals, 1)).T
        acc_s[...] += mm_nt(mixed_all, weights[:, 768:])
        return carry

    lax.fori_loop(0, 4, attend, 0)
    saves = [
        pltpu.make_async_copy(inside, outside, save_sem.at[n])
        for n, (inside, outside) in enumerate(
            ((ql_ref, ql_f), (kl_ref, kl_f), (vl_ref, vl_f), (mix_ref, mix_f), (x_s, x_f))
        )
    ]
    start_loads(saves)
    attended = acc_s[...] + vecs[2:3]
    att_ref[...] = attended.astype(BF16)
    middle = x_s[...].astype(F32) + mod_ref[0:1] * attended
    mid_s[...] = middle
    normed, _ = norm_rows(middle)
    two = (normed * (1.0 + mod_ref[3:4]) + mod_ref[5:6]).astype(BF16)
    one_s[...] = two
    twot_s[...] = two.T
    wait_loads(pairs[1])
    back = (mod_ref[1:2] * cot_s[...].astype(F32)).astype(BF16)
    back_s[...] = back
    backt_s[...] = back.T
    acc_s[...] = jnp.zeros_like(acc_s)
    gacc_s[...] = jnp.zeros_like(gacc_s)

    def store_feed(half, part):
        return [
            pltpu.make_async_copy(
                grad_s.at[half, at], ref.at[half, :, :, :, :, columns(part * 512, 512)], grad_sem.at[half, at]
            )
            for at, ref in enumerate((g1_f, g2_f))
        ]

    def feed(i, carry):
        half, part = lax.rem(i, 2), i // 2

        def before(p):
            def act():
                ticks.run(10 + 2 * p, 11 + 2 * p)
                gather.finish(4 + 2 * p)
                gather.finish(5 + 2 * p)
                start_loads(load_feed(0, p))
                start_loads(load_feed(1, p))

            return act

        switch_on(i, {2 * p: before(p) for p in range(4)})
        switch_on(i, {2 * p + 1: (lambda p=p: ticks.run(11 + 2 * p, 12 + 2 * p)) for p in range(3)})
        wait_loads(load_feed(half, part))
        weights = w_s[half].reshape(model, 1024)
        w1, w2 = weights[:, :512], weights[:, 512:]
        spot = columns(half * (hidden_bias.shape[1] // 2) + part * 512, 512)
        hidden = mm(one_s[...], w1) + hidden_bias[0:1, spot]
        square = hidden * hidden
        curve = jnp.tanh(0.7978845608028654 * hidden * (1.0 + 0.044715 * square))
        level = 0.5 * (1.0 + curve)
        activated = (hidden * level).astype(BF16)
        slope = level + 0.5 * hidden * (1.0 - curve * curve) * (
            0.7978845608028654 * (1.0 + 0.134145 * square)
        )
        acc_s[...] += mm_nt(activated, w2)

        @pl.when(i >= 2)
        def _():
            wait_loads(store_feed(half, part))

        grad_s[half, 1] = mm(backt_s[...], activated).astype(BF16).reshape(grad_s.shape[2:])
        hidden_grad = (mm(back_s[...], w2) * slope).astype(BF16)
        grad_s[half, 0] = mm(twot_s[...], hidden_grad).astype(BF16).reshape(grad_s.shape[2:])
        start_loads(store_feed(half, part))
        gb1_ref[0:1, spot] = jnp.sum(hidden_grad.astype(F32), 0, keepdims=True)
        gacc_s[...] += mm_nt(hidden_grad, w1)
        return carry

    lax.fori_loop(0, 8, feed, 0)
    middle = mid_s[...]
    out_grad = cot_s[...].astype(F32)
    branch = acc_s[...] + vecs[3:4]
    out_ref[...] = (middle + mod_ref[1:2] * branch).astype(BF16)
    normed, inverse = norm_rows(middle)
    grad = gacc_s[...]
    middle_grad = out_grad + norm_rows_back(grad * (1.0 + mod_ref[3:4]), normed, inverse)
    gmid_ref[...] = middle_grad
    rows_ref[0:1] = jnp.sum(out_grad * branch, 0, keepdims=True)
    rows_ref[1:2] = jnp.sum(grad * normed, 0, keepdims=True)
    rows_ref[2:3] = jnp.sum(grad, 0, keepdims=True)
    rows_ref[3:4] = jnp.sum(back_s[...].astype(F32), 0, keepdims=True)
    rows_ref[4:5] = jnp.sum(middle_grad * att_ref[...].astype(F32), 0, keepdims=True)
    rows_ref[5:8] = jnp.zeros((3, model), F32)
    gb1_ref[1:8] = jnp.zeros((7, gb1_ref.shape[1]), F32)
    for half in range(2):
        wait_loads(store_feed(half, 3))
    wait_loads(saves)
    gather.sent()


def run_ahead(batches, line, signals, ada, extra, segments, tok_near, tok_away, cot, kmask, qmask, hidden_cols, width, cid):
    padded, model = tok_near.shape
    rows = 2 * padded
    total, count = 8 * line, sum(len(batch) for batch in batches)
    own_rows = segments[0].shape[0]
    anywhere, inside = pl.BlockSpec(memory_space=pl.ANY), pl.BlockSpec(memory_space=pltpu.VMEM)
    full = [jax.ShapeDtypeStruct((2, line, 2, 2) + s.shape, BF16) for s in segments]
    flat = jax.ShapeDtypeStruct((rows, model), BF16)
    turned = jax.ShapeDtypeStruct((model, rows), BF16)
    flat_s, turned_s, wide_s = (
        pltpu.VMEM((rows, model), BF16), pltpu.VMEM((model, rows), BF16), pltpu.VMEM((rows, model), F32)
    )
    block = (line, 2, 2, own_rows)
    dma = pltpu.SemaphoreType.DMA
    letters = pltpu.VMEM((total // 2, 2, 8, model // 2), F32)
    return pl.pallas_call(
        functools.partial(ahead_kernel, batches, line, width),
        in_specs=[inside] * 7 + [anywhere] * 3 + [inside] * 2,
        out_shape=full + [full[2], full[3], turned, turned, flat, flat, flat] + [
            jax.ShapeDtypeStruct((model // 256, 8, 128), F32), jax.ShapeDtypeStruct((8, model), F32),
            jax.ShapeDtypeStruct((model // 256, 2, 8, rows), F32), flat,
            jax.ShapeDtypeStruct((rows, model), F32), jax.ShapeDtypeStruct((8, model), F32),
            jax.ShapeDtypeStruct((8, hidden_cols), F32), jax.ShapeDtypeStruct((total // 2, 2, 8, 128), F32),
            jax.ShapeDtypeStruct((own_rows, 3 * model), BF16),
        ],
        out_specs=[anywhere] * 11 + [inside] * 9,
        scratch_shapes=[
            letters, letters, pltpu.VMEM((8, model), F32),
            pltpu.VMEM((8, hidden_cols), F32), flat_s, turned_s, turned_s, flat_s, flat_s,
            flat_s, flat_s, flat_s, wide_s, wide_s, turned_s, flat_s, turned_s, wide_s,
            pltpu.VMEM((2,) + block + (1024,), BF16), pltpu.VMEM((2, 2) + block + (512,), BF16),
            dma((total,)), dma((total,)), dma((total,)), dma((total,)), dma((5,)), dma((4,)), dma((2, 3)),
            dma((count, line - 1)), dma((count, line - 1)), dma((count, 7)), dma((count, 7)),
            dma((2, 2)), dma((2, 2)),
        ],
        compiler_params=pltpu.CompilerParams(
            collective_id=cid, has_side_effects=True, vmem_limit_bytes=VMEM_LIMIT
        ),
        name="ahead",
    )(signals, ada, extra, *segments, tok_near, tok_away, cot, kmask, qmask)


def behind_kernel(batches, line, width, levels, *refs):
    count = sum(len(batch) for batch in batches)
    (x_f, qkv_f, proj_f, g1_f, g2_f, result, ql_f, kl_f, vl_f, mix_f,
     gmid_ref, mod_ref, feed_rows, hidden_ref, stat_ref, boosts, kmask_ref, qmask_ref) = refs[:18]
    (gqkv_f, gproj_f, act_far, tok_far) = refs[18:22]
    landing = refs[22 : 22 + count]
    (t_qkv, t_proj, t_fc1, t_fc2, mods_ref, x_s) = refs[22 + count : 28 + count]
    rest = refs[28 + count :]
    first_b, second_b, line_b, plane_b = (rest[n * count : (n + 1) * count] for n in range(4))
    (core_s, own_s, ga_s, gat_s, onet_s, acc_s, turn_s, flat_s, w_s, grad_s, gm_s, vec_s, rows_ref, heads_s,
     a_send, a_recv, pair_sem, x_sem, w_sem, grad_sem,
     own_sem, load_sem, send_sem, recv_sem, z_send, z_recv) = rest[4 * count :]
    z, x, c, y = where_am_i()
    total = 8 * line
    padded, model = result.shape[0] // 2, result.shape[1]
    half_cols = model // 2
    heads = 256 // width
    partner = device(z, x, c, 1 - y)
    scatter = Scatter(
        batches, line, [gqkv_f, gproj_f, g1_f, g2_f], [t_qkv, t_proj, t_fc1, t_fc2], landing, core_s, own_s,
        first_b, second_b, line_b, plane_b, (own_sem, load_sem, send_sem, recv_sem, z_send, z_recv),
    )
    ticks = Ticks(len(batches), scatter.stages(), (0, 1, 2, 4, 6, 8))
    others = pl.ds((1 - y) * padded, padded)
    pairs = [
        remote(source.at[others], target, pair_sem.at[p, 0], pair_sem.at[p, 1], partner)
        for p, (source, target) in enumerate(((result, act_far), (x_s, tok_far)))
    ]
    load_x = pltpu.make_async_copy(x_f, x_s, x_sem.at[0])
    load_x.start()
    greet_all(total)
    ticks.run(0, 1)
    pairs[0].start()

    def load_group(i):
        half = lax.rem(i, 2)
        sub, at = i // 2, half * 2 + i // 2
        turned = pl.ds(pl.multiple_of(at * 256, 256), 256)
        cols = columns(at * 256, 256)
        pieces = [
            (qkv_f.at[half, :, :, :, :, columns(sub * 768, 768)], w_s.at[:, :, :, :, pl.ds(0, 768)]),
            (proj_f.at[half, :, :, :, :, columns(sub * 256, 256)], w_s.at[:, :, :, :, pl.ds(768, 256)]),
            (ql_f.at[turned], turn_s.at[0]),
            (kl_f.at[turned], turn_s.at[1]),
            (vl_f.at[:, cols], flat_s.at[0]),
            (mix_f.at[:, cols], flat_s.at[1]),
        ]
        return [pltpu.make_async_copy(s, t, w_sem.at[n]) for n, (s, t) in enumerate(pieces)]

    def store_group(i):
        half, sub = lax.rem(i, 2), i // 2
        return [
            pltpu.make_async_copy(
                grad_s.at[:, :, :, :, pl.ds(0, 768)], gqkv_f.at[half, :, :, :, :, columns(sub * 768, 768)],
                grad_sem.at[0],
            ),
            pltpu.make_async_copy(
                grad_s.at[:, :, :, :, pl.ds(768, 256)], gproj_f.at[half, :, :, :, :, columns(sub * 256, 256)],
                grad_sem.at[1],
            ),
        ]

    def start_loads(copies):
        for copy in copies:
            copy.start()

    def wait_loads(copies):
        for copy in copies:
            copy.wait()

    start_loads(load_group(0))
    ticks.run(1, 2)
    attend_grad = (mod_ref[0:1] * gmid_ref[...]).astype(BF16)
    ga_s[...] = attend_grad
    gat_s[...] = attend_grad.T
    vec_s[2:3] = jnp.sum(attend_grad.astype(F32), 0, keepdims=True)
    vec_s[3:4] = feed_rows[3:4]
    for part in range(4):
        vec_s[4 + part : 5 + part] = hidden_ref[0:1, part * model : (part + 1) * model]
    heads_s[...] = jnp.zeros_like(heads_s)
    lane = lax.broadcasted_iota(jnp.int32, (1, half_cols), 1)
    ticks.run(2, 3)
    load_x.wait()
    normed, _ = norm_rows(x_s[...].astype(F32))
    onet_s[...] = (normed * (1.0 + mod_ref[2:3]) + mod_ref[4:5]).astype(BF16).T
    acc_s[...] = jnp.zeros_like(acc_s)
    kmask, qmask = kmask_ref[...], qmask_ref[...]
    rows = kmask.shape[1]
    place = lax.broadcasted_iota(jnp.int32, (16, rows), 0)

    def pieces_of(row, first):
        high, mid, low = split_three(row)
        zero = jnp.zeros((16, rows), BF16)
        out = jnp.where(place == first, jnp.broadcast_to(high, zero.shape), zero)
        out = jnp.where(place == first + 1, jnp.broadcast_to(mid, zero.shape), out)
        return jnp.where(place == first + 2, jnp.broadcast_to(low, zero.shape), out)

    def group(i, carry):
        slot = lax.rem(i, 2)
        at = slot * 2 + i // 2

        wait_loads(load_group(i))
        boost = boosts[at]
        weights = w_s[...].reshape(model, 1024)
        mixed = flat_s[1]
        values = flat_s[0]
        q_all_low, k_all_low = turn_s[0], turn_s[1]
        mixed_grad = mm(ga_s[...], weights[:, 768:]).astype(BF16)
        mixed_turned, v_turned, q_plain = mixed_grad.T, values.T, q_all_low.T
        dq_rows, dk_rows, dv_cols, scales = [], [], [], []
        for head in range(heads):
            if head == 2:
                switch_on(i, {n: (lambda n=n: ticks.run(3 + 2 * n, 4 + 2 * n)) for n in range(4)})
            part = slice(head * width, (head + 1) * width)
            lift = boost[0:1, head : head + 1]
            q_bf, k_bf = q_all_low[part], k_all_low[part]
            q_float = q_bf.astype(F32)
            scaled = q_float * LOG2E
            high = scaled.astype(BF16)
            low = (scaled - high.astype(F32)).astype(BF16)
            log_total = stat_ref[at, 1, head : head + 1]
            q_all = jnp.concatenate([high, low, qmask + pieces_of(-log_total, levels + 1)], 0)
            k_all = jnp.concatenate([k_bf, k_bf, kmask], 0)
            soft = jnp.exp2(mm_tn(k_all, q_all))
            product = soft * mm_tn(v_turned[part], mixed_turned[part])
            delta = jnp.sum(product, 0, keepdims=True)
            scores_grad = (product - soft * delta).astype(BF16)
            dv_cols.append(mm(soft.astype(BF16), mixed_grad[:, part]))
            dq_low = mm(k_bf, scores_grad)
            dk_low = mm(scores_grad, q_plain[:, part]).T
            q_inv = stat_ref[at, 0, head : head + 1]
            k_inv = stat_ref[at, 0, heads + head : heads + head + 1]
            k_unit = k_bf.astype(F32)
            along = dq_low * q_float
            scales.append(jnp.sum(along, keepdims=True))
            dq_rows.append(
                q_inv * (dq_low * lift - q_float * (1.0 / lift) * jnp.sum(along, 0, keepdims=True))
            )
            dk_rows.append(k_inv * (dk_low - k_unit * jnp.sum(dk_low * k_unit, 0, keepdims=True)))
        dq = jnp.concatenate(dq_rows, 0).T.astype(BF16)
        dk = jnp.concatenate(dk_rows, 0).T.astype(BF16)
        dv = jnp.concatenate(dv_cols, 1).astype(BF16)
        triple = jnp.concatenate([dq, dk, dv], 1)

        @pl.when(i > 0)
        def _():
            wait_loads(store_group(i))

        switch_on(i, {n: (lambda n=n: ticks.run(4 + 2 * n, 5 + 2 * n)) for n in range(3)})
        shape = grad_s.shape[:4]
        grad_s[:, :, :, :, 0:768] = mm(onet_s[...], triple).astype(BF16).reshape(shape + (768,))
        grad_s[:, :, :, :, 768:1024] = mm(gat_s[...], mixed).astype(BF16).reshape(shape + (256,))
        start_loads(store_group(i))
        acc_s[...] += mm_nt(triple, weights[:, :768])
        spot = columns(at * 256, 256)
        vec_s[0:1, spot] = jnp.sum(dq.astype(F32), 0, keepdims=True)
        vec_s[1:2, spot] = jnp.sum(dv.astype(F32), 0, keepdims=True)
        for head in range(heads):
            heads_s[0:1] += jnp.where(lane == at * heads + head, scales[head], 0.0)

        @pl.when(i < 3)
        def _():
            start_loads(load_group(i + 1))

        return carry

    lax.fori_loop(0, 4, group, 0)
    wait_loads(store_group(3))
    ticks.run(10, 12)
    grad = acc_s[...]
    normed, inverse = norm_rows(x_s[...].astype(F32))
    x_s[...] = (
        gmid_ref[...] + norm_rows_back(grad * (1.0 + mod_ref[2:3]), normed, inverse)
    ).astype(BF16)
    pairs[1].start()
    rows_ref[0:1] = jnp.sum(grad * normed, 0, keepdims=True)
    rows_ref[1:2] = jnp.sum(grad, 0, keepdims=True)
    owners = total // 2
    spread, owner_of = owner_maps(owners, width // owners, width, model)
    picked = jnp.concatenate([owner_of * vec_s[r : r + 1] for r in range(8)], 0)
    moved = sum(mm_nt(part, spread) for part in split_three(picked))
    small = jnp.concatenate([moved[r * owners : (r + 1) * owners] for r in range(8)], 1)
    mod_rows = (feed_rows[4:5], feed_rows[0:1], rows_ref[0:1], feed_rows[1:2], rows_ref[1:2], feed_rows[2:3])
    for half in range(2):
        for n, row in enumerate(mod_rows):
            gm_s[:, half, n, :] = jnp.broadcast_to(
                row[:, half * half_cols : (half + 1) * half_cols], (owners, half_cols)
            )
        gm_s[:, half, 6, :] = small
        gm_s[:, half, 7, :] = jnp.broadcast_to(heads_s[0:1], (owners, half_cols))
    exchange = Exchange(total, lambda to: gm_s.at[to // 2, to % 2], mods_ref.at[lax.axis_index("dp"), y], a_send, a_recv)
    exchange.start()
    ticks.run(12, ticks.total)
    exchange.wait()
    wait_loads(pairs)
    scatter.sent()


def run_behind(batches, line, levels, saved, inner, width, cid):
    x_f, qkv_f, proj_f, g1_f, g2_f, result, ql, kl, vl, mix = saved
    rows, model = x_f.shape
    chunks = [chunk for batch in batches for chunk in batch]
    total, count = 8 * line, len(chunks)
    own_rows = qkv_f.shape[4]
    anywhere, inside = pl.BlockSpec(memory_space=pl.ANY), pl.BlockSpec(memory_space=pltpu.VMEM)
    dma = pltpu.SemaphoreType.DMA
    landing, first_b, second_b, line_b, plane_b = [], [], [], [], []
    for _, kind, _, cols in chunks:
        tail = (own_rows, cols)
        landing.append(jax.ShapeDtypeStruct((2, line, 2) + tail, BF16))
        if kind >= 2:
            shapes = (2,), (), (line - 1, 2, 2)
        else:
            shapes = (line, 2) if kind == 0 else (2, line), (line,), (line - 1,)
        for held, shape in zip((first_b, second_b, line_b), shapes):
            held.append(pltpu.VMEM(shape + tail, BF16))
        plane_b.append(pltpu.VMEM((2, 2) + tail if kind >= 2 else (16, 128), BF16))
    most = max(sum(chunk[3] for chunk in batch) for batch in batches)
    sources = [qkv_f, proj_f, g1_f, g2_f]
    block = (line, 2, 2, own_rows)
    made = pl.pallas_call(
        functools.partial(behind_kernel, batches, line, width, levels),
        in_specs=[anywhere] * 10 + [inside] * 8,
        out_shape=[jax.ShapeDtypeStruct(qkv_f.shape, BF16), jax.ShapeDtypeStruct(proj_f.shape, BF16)]
        + [jax.ShapeDtypeStruct((rows // 2, model), BF16)] * 2 + landing
        + [jax.ShapeDtypeStruct(s.shape[4:], F32) for s in sources]
        + [jax.ShapeDtypeStruct((total // 2, 2, 8, model // 2), F32), jax.ShapeDtypeStruct((rows, model), BF16)],
        out_specs=[anywhere] * (4 + count) + [inside] * 6,
        scratch_shapes=first_b + second_b + line_b + plane_b + [
            pltpu.VMEM((4, 2, line, 2, own_rows, most), BF16), pltpu.VMEM((2, 2, line, 2, own_rows, most), BF16),
            pltpu.VMEM((rows, model), BF16), pltpu.VMEM((model, rows), BF16),
            pltpu.VMEM((model, rows), BF16), pltpu.VMEM((rows, model), F32), pltpu.VMEM((2, 256, rows), BF16),
            pltpu.VMEM((2, rows, 256), BF16), pltpu.VMEM(block + (1024,), BF16),
            pltpu.VMEM(block + (1024,), BF16), pltpu.VMEM((total // 2, 2, 8, model // 2), F32), pltpu.VMEM((8, model), F32), pltpu.VMEM((8, model), F32),
            pltpu.VMEM((8, model // 2), F32),
            dma((total,)), dma((total,)), dma((2, 2)), dma((1,)), dma((6,)), dma((2,)),
            dma((count,)), dma((count,)), dma((count, 3)), dma((count, 3)),
            dma((count, line - 1)), dma((count, line - 1)),
        ],
        compiler_params=pltpu.CompilerParams(
            collective_id=cid, has_side_effects=True, vmem_limit_bytes=VMEM_LIMIT
        ),
        name="behind",
    )(*saved, *inner)
    return made[2], made[3], made[4 + count :]


def pad_rows(values, padded):
    return jnp.pad(values, ((0, 0), (0, padded - values.shape[1]), (0, 0)))


def gather_list():
    def both(segment, start, cols):
        return [(segment, 0, start, cols, 0, 16), (segment, 1, start, cols, 16, 48)]

    attend = []
    for sub in range(2):
        start = sub * 768
        attend += [both(0, start, 512), both(0, start + 512, 256) + both(1, sub * 256, 256)]
    return attend + [
        [(s, 0, part * 512, wide, 0, 64), (s, 1, part * 512 + wide, 512 - wide, 0, 64)]
        for part in range(4)
        for s, wide in ((2, 256), (3, 128))
    ]


def scatter_list():
    def three(segment, start):
        return [(segment, 0, start, 128), (segment, 1, start + 128, 256), (segment, 3, start + 384, 128)]

    feed = []
    for part in range(4):
        feed += [three(2, part * 512), [(3, 0, part * 512, 128), (3, 1, part * 512 + 128, 384)]]
    attend = []
    for sub in range(2):
        start = sub * 768
        attend += [
            three(0, start), [(0, 0, start + 512, 128), (0, 1, start + 640, 128), (1, 1, sub * 256, 256)]
        ]
    return feed + attend


def on_device_paired(
    tokens, condition, scale_lengths, order, cotangent, ada_weight, ada_bias, qkv_weight, qv_bias,
    head_log_scale, proj_weight, out_bias, fc1_weight, fc1_bias, fc2_weight,
):
    n_dp, mine = lax.axis_size("dp"), lax.axis_index("mp")
    line = n_dp // 4
    slots, half_rows, model = tokens.shape
    padded = -(-half_rows // 16) * 16
    rows = 2 * padded
    local_heads, width = qv_bias.shape[1], 64
    own_cols = qkv_weight.shape[2]
    own_rows = qkv_weight.shape[1]
    hidden_cols = fc1_weight.shape[1]
    groups = 2 * own_cols // 256
    swap = order[0, 0] != 0
    entries = qv_bias.shape[2]
    vectors = 4 * local_heads + fc1_bias.shape[0]
    scale_at = vectors * entries
    n_dev = 2 * n_dp

    def to_slots(values):
        return jnp.stack([jnp.where(swap, values[1], values[0]), jnp.where(swap, values[0], values[1])])

    cond_slots = to_slots(condition).astype(F32)
    signal = jax.nn.silu(cond_slots).astype(BF16)
    signals = signal.reshape(slots, n_dp, own_rows).transpose(1, 0, 2).astype(F32)
    signals = jnp.pad(signals, ((0, 0), (0, 8 - slots), (0, 128 - own_rows)))
    bias_own = lax.dynamic_update_slice(
        jnp.zeros((6, local_heads, width), F32), ada_bias.astype(F32), (0, 0, lax.axis_index("dp") * entries)
    ).reshape(6, own_cols)
    small = jnp.concatenate([qv_bias.reshape(-1), out_bias.reshape(-1), fc1_bias.reshape(-1)]).astype(F32)
    extra = jnp.concatenate(
        [bias_own, jnp.pad(small, (0, own_cols - scale_at))[None], jnp.pad(head_log_scale, (0, own_cols - local_heads))[None]]
    )

    token_halves = pad_rows(tokens, padded)
    first = (mine == 0) != swap
    tok_near = jnp.where(first, token_halves[0], token_halves[1])
    tok_away = jnp.where(first, token_halves[1], token_halves[0])
    lengths = lax.dynamic_index_in_dim(to_slots(scale_lengths), mine, 0, keepdims=False)
    kmask, qmask = build_masks(lengths, half_rows, padded)
    segments = [
        qkv_weight.reshape(3, own_rows, 2, 256).transpose(1, 2, 0, 3).reshape(own_rows, 3 * own_cols),
        proj_weight.T, fc1_weight, fc2_weight.T,
    ]
    (qkv_f, proj_f, _, _, g1_f, g2_f, q_low, k_low, v_low, mixed, x_f, boosts, mods, stats, result, grad_middle,
     feed_rows, g_hidden, sig_all, ada_flat) = run_ahead(
        gather_list(), line, signals, ada_weight, extra, segments, tok_near, tok_away,
        pad_rows(cotangent, padded), kmask, qmask, 2 * hidden_cols, width, 1,
    )
    act_far, tok_far, (t_qkv, t_proj, t_fc1, t_fc2, arrived, token_grad) = run_behind(
        scatter_list(), line, scale_lengths.shape[1],
        [x_f, qkv_f, proj_f, g1_f, g2_f, result, q_low, k_low, v_low, mixed],
        [grad_middle, mods, feed_rows, g_hidden, stats, boosts, kmask, qmask], width, 2,
    )
    qkv_total = t_qkv.reshape(own_rows, 2, 3, 256).transpose(2, 0, 1, 3).reshape(qkv_weight.shape)

    def both_slots(image, far, swapped):
        near = jnp.where(mine == 0, image[:half_rows], image[padded : padded + half_rows])
        first = (mine == 0) != swapped
        return jnp.stack([jnp.where(first, near, far[:half_rows]), jnp.where(first, far[:half_rows], near)])

    activations = both_slots(result, act_far, False)
    tokens_grad = both_slots(token_grad, tok_far, swap)

    all_mods = arrived[:, :, :6].reshape(n_dev, 6 * own_cols)
    signal_part = lax.dot_general(
        all_mods, ada_flat.astype(F32), (((1,), (1,)), ((), ())), precision=precise, preferred_element_type=F32
    ).reshape(n_dp, 1, slots * own_rows)
    signal_part = jnp.broadcast_to(signal_part, (n_dp, 2, slots * own_rows)).reshape(n_dev, slots * own_rows)
    signal_part = lax.all_to_all(signal_part, ("dp", "mp"), 0, 0, tiled=True)
    signal_grad = signal_part.reshape(n_dp, 2, slots, own_rows).sum(1).transpose(1, 0, 2).reshape(slots, model)
    signal_rows = sig_all[:, 0, :slots, :own_rows].reshape(n_dev, own_rows)
    ada_weight_grad = lax.dot_general(
        signal_rows, all_mods, (((0,), (0,)), ((), ())), precision=precise, preferred_element_type=F32
    ).reshape(ada_weight.shape)
    small_total = arrived[:, :, 6:].sum((0, 1))
    by_head = small_total[0].reshape(8, 2 * local_heads, entries)
    bias_total = lax.dynamic_slice_in_dim(by_head[:4], mine * local_heads, local_heads, 1)
    hidden_total = lax.dynamic_slice_in_dim(by_head[4:], mine * 2, 2, 0).reshape(fc1_bias.shape)
    scale_total = lax.dynamic_slice_in_dim(small_total[1], mine * local_heads, local_heads, 0)
    ada_bias_grad = lax.dynamic_slice_in_dim(
        jnp.sum(all_mods, 0).reshape(6, local_heads, width), lax.axis_index("dp") * entries, entries, 2
    )
    pull = jax.vjp(jax.nn.silu, cond_slots)[1]
    condition_grad = to_slots(pull(signal_grad)[0]).astype(BF16)
    return (
        activations, tokens_grad, condition_grad, ada_weight_grad, ada_bias_grad, qkv_total, bias_total[:2],
        scale_total, t_proj.T, bias_total[2:], t_fc1, hidden_total, t_fc2.T,
    )


precise = lax.Precision.HIGHEST


def row_norm(values):
    centre = jnp.mean(values, -1, keepdims=True)
    shifted = values - centre
    inverse = lax.rsqrt(jnp.mean(shifted * shifted, -1, keepdims=True) + 1e-06)
    return (shifted * inverse, inverse)


def row_norm_back(incoming, normed, inverse):
    return inverse * (
        incoming
        - jnp.mean(incoming, -1, keepdims=True)
        - normed * jnp.mean(incoming * normed, -1, keepdims=True)
    )


def gelu_tanh(values):
    return jax.nn.gelu(values, approximate=True)


def spread(shard_rows):
    return lax.all_gather(shard_rows, "mp", axis=0, tiled=True)


def collect(partial_sum):
    return lax.psum_scatter(
        partial_sum.astype(jnp.bfloat16), "mp", scatter_dimension=0, tiled=True
    ).astype(jnp.float32)


def fetch(qkv_weight, qv_bias, proj_weight, out_bias, fc1_weight, fc1_bias, fc2_weight):
    return (
        lax.all_gather(qkv_weight, "dp", axis=1, tiled=True),
        lax.all_gather(qv_bias, "dp", axis=2, tiled=True),
        lax.all_gather(proj_weight, "dp", axis=1, tiled=True),
        lax.all_gather(out_bias, "dp", axis=2, tiled=True),
        lax.all_gather(fc1_weight, "dp", axis=0, tiled=True),
        lax.all_gather(fc1_bias, "dp", axis=1, tiled=True),
        lax.all_gather(fc2_weight, "dp", axis=1, tiled=True),
    )


def settle(grad_set):
    qkv_part, qv_part, proj_part, outb_part, fc1_part, fc1b_part, fc2_part = grad_set
    return (
        lax.psum_scatter(
            qkv_part.astype(jnp.bfloat16), "dp", scatter_dimension=1, tiled=True
        ).astype(jnp.float32),
        lax.psum_scatter(
            qv_part.astype(jnp.bfloat16), "dp", scatter_dimension=2, tiled=True
        ).astype(jnp.float32),
        lax.psum_scatter(
            proj_part.astype(jnp.bfloat16), "dp", scatter_dimension=1, tiled=True
        ).astype(jnp.float32),
        lax.psum_scatter(
            outb_part.astype(jnp.bfloat16), "dp", scatter_dimension=2, tiled=True
        ).astype(jnp.float32),
        lax.psum_scatter(
            fc1_part.astype(jnp.bfloat16), "dp", scatter_dimension=0, tiled=True
        ).astype(jnp.float32),
        lax.psum_scatter(
            fc1b_part.astype(jnp.bfloat16), "dp", scatter_dimension=1, tiled=True
        ).astype(jnp.float32),
        lax.psum_scatter(
            fc2_part.astype(jnp.bfloat16), "dp", scatter_dimension=1, tiled=True
        ).astype(jnp.float32),
    )


def on_device_shared(
    tokens,
    condition,
    scale_lengths,
    order,
    cotangent,
    ada_weight,
    ada_bias,
    qkv_weight,
    qv_bias,
    head_log_scale,
    proj_weight,
    out_bias,
    fc1_weight,
    fc1_bias,
    fc2_weight,
):
    image_count, shard_rows, model_width = tokens.shape
    column_count = qkv_weight.shape[2]
    local_heads = qv_bias.shape[1]
    head_width = column_count // local_heads
    hidden_cols = fc1_weight.shape[1]
    own_start = lax.axis_index("mp") * column_count
    token_count = shard_rows * lax.axis_size("mp")
    ada_full, ada_bias_full = (
        lax.all_gather(ada_weight, "dp", axis=0, tiled=True),
        lax.all_gather(ada_bias, "dp", axis=2, tiled=True),
    )
    cond_float = condition.astype(jnp.float32)
    signal = jax.nn.silu(cond_float).astype(jnp.bfloat16)
    ada_flat = ada_full.reshape(model_width, 6 * column_count)
    mod_share = jnp.dot(
        signal, ada_flat, preferred_element_type=jnp.float32
    ) + ada_bias_full.reshape(6 * column_count).astype(jnp.float32)
    modulation = lax.all_gather(
        mod_share.reshape(image_count, 6, column_count), "mp", axis=2, tiled=True
    )
    head_boost = jnp.exp(head_log_scale)[None, :, None]
    positions = jnp.arange(token_count, dtype=jnp.int32)

    def place(vector):
        return lax.dynamic_update_slice(
            jnp.zeros((model_width,), jnp.float32), vector, (own_start,)
        )

    def own_columns(matrix):
        return lax.dynamic_slice_in_dim(matrix, own_start, column_count, 1)

    def rows_now():
        return fetch(qkv_weight, qv_bias, proj_weight, out_bias, fc1_weight, fc1_bias, fc2_weight)

    full_shapes = (
        (3, model_width, column_count),
        (2, local_heads, head_width),
        (column_count, model_width),
        (2, local_heads, head_width),
        (model_width, hidden_cols),
        (hidden_cols // head_width, head_width),
        (hidden_cols, model_width),
    )
    grad_start = tuple((jnp.zeros(shape_item, jnp.float32) for shape_item in full_shapes))

    def micro_step(micro_at, state_now):
        outputs, token_grads, mod_grads, weight_grads, scale_grad = state_now
        image_at = order[0, micro_at]
        residual = lax.dynamic_index_in_dim(tokens, image_at, 0, keepdims=False).astype(jnp.float32)
        image_mods = lax.dynamic_index_in_dim(modulation, image_at, 0, keepdims=False)
        lengths = lax.dynamic_index_in_dim(scale_lengths, image_at, 0, keepdims=False)
        out_grad = lax.dynamic_index_in_dim(cotangent, micro_at, 0, keepdims=False).astype(
            jnp.float32
        )
        qkv_full, qv_full, proj_full, outb_full, fc1_full, fc1b_full, fc2_full = rows_now()
        steps = jnp.arange(lengths.shape[0], dtype=jnp.int32)
        scale_ends = jnp.sum(jnp.where(steps[None, :] <= steps[:, None], lengths[None, :], 0), 1)
        scale_of = jnp.sum((positions[:, None] >= scale_ends[None, :]).astype(jnp.int32), 1)
        allowed = (scale_of[None, :] <= scale_of[:, None])[None]
        normed_one, inverse_one = row_norm(residual)
        input_one = spread(
            (normed_one * (1.0 + image_mods[2]) + image_mods[4]).astype(jnp.bfloat16)
        )
        projected = jnp.einsum(
            "td,cde->cte", input_one, qkv_full, preferred_element_type=jnp.float32
        )
        bias_pair = qv_full.reshape(2, column_count).astype(jnp.float32)
        queries = (projected[0] + bias_pair[0]).reshape(token_count, local_heads, head_width)
        keys_raw = projected[1].reshape(token_count, local_heads, head_width)
        values_low = (
            (projected[2] + bias_pair[1])
            .astype(jnp.bfloat16)
            .reshape(token_count, local_heads, head_width)
        )
        query_inv = lax.rsqrt(jnp.sum(queries * queries, -1, keepdims=True) + 1e-06)
        key_inv = lax.rsqrt(jnp.sum(keys_raw * keys_raw, -1, keepdims=True) + 1e-06)
        query_unit = queries * query_inv
        key_unit = keys_raw * key_inv
        query_low = (query_unit * head_boost).astype(jnp.bfloat16)
        key_low = key_unit.astype(jnp.bfloat16)

        def masked_scores():
            raw_scores = jnp.einsum(
                "qhd,khd->hqk", query_low, key_low, preferred_element_type=jnp.float32
            )
            return jnp.where(allowed, raw_scores, -1e30)

        scores = masked_scores()
        row_peak = jnp.max(scores, -1, keepdims=True)
        exp_terms = jnp.exp(scores - row_peak)
        totals = jnp.sum(exp_terms, -1, keepdims=True)
        log_total = row_peak + jnp.log(totals)
        soft_weights = exp_terms / totals
        mixed_heads = (
            jnp.einsum(
                "hqk,khd->qhd",
                soft_weights.astype(jnp.bfloat16),
                values_low,
                preferred_element_type=jnp.float32,
            )
            .astype(jnp.bfloat16)
            .reshape(token_count, column_count)
        )
        attended = collect(
            jnp.dot(mixed_heads, proj_full, preferred_element_type=jnp.float32)
            + place(outb_full[0].reshape(column_count).astype(jnp.float32))
        )
        middle = residual + image_mods[0] * attended
        normed_two, inverse_two = row_norm(middle)
        input_two = spread(
            (normed_two * (1.0 + image_mods[3]) + image_mods[5]).astype(jnp.bfloat16)
        )
        hidden = jnp.dot(
            input_two, fc1_full, preferred_element_type=jnp.float32
        ) + fc1b_full.reshape(hidden_cols).astype(jnp.float32)
        activated = gelu_tanh(hidden).astype(jnp.bfloat16)
        branch_out = collect(
            jnp.dot(activated, fc2_full, preferred_element_type=jnp.float32)
            + place(outb_full[1].reshape(column_count).astype(jnp.float32))
        )
        result = (middle + image_mods[1] * branch_out).astype(jnp.bfloat16)
        outputs = lax.dynamic_update_index_in_dim(outputs, result, micro_at, 0)
        qkv_back, qv_back, proj_back, outb_back, fc1_back, fc1b_back, fc2_back = rows_now()
        grad_branch = spread((image_mods[1] * out_grad).astype(jnp.bfloat16))
        gamma_two_grad = jnp.sum(out_grad * branch_out, 0)
        fc2_grad = jnp.dot(activated.T, grad_branch, preferred_element_type=jnp.float32)
        bias_two_grad = jnp.sum(own_columns(grad_branch).astype(jnp.float32), 0)
        act_grad = jnp.dot(grad_branch, fc2_back.T, preferred_element_type=jnp.float32)
        gelu_pull = jax.vjp(gelu_tanh, hidden)[1]
        hidden_grad = gelu_pull(act_grad)[0].astype(jnp.bfloat16)
        fc1_grad = jnp.dot(input_two.T, hidden_grad, preferred_element_type=jnp.float32)
        fc1b_grad = jnp.sum(hidden_grad.astype(jnp.float32), 0).reshape(
            hidden_cols // head_width, head_width
        )
        input_two_grad = collect(
            jnp.dot(hidden_grad, fc1_back.T, preferred_element_type=jnp.float32)
        )
        scale_two_grad = jnp.sum(input_two_grad * normed_two, 0)
        shift_two_grad = jnp.sum(input_two_grad, 0)
        middle_grad = out_grad + row_norm_back(
            input_two_grad * (1.0 + image_mods[3]), normed_two, inverse_two
        )
        grad_attended = spread((image_mods[0] * middle_grad).astype(jnp.bfloat16))
        gamma_one_grad = jnp.sum(middle_grad * attended, 0)
        proj_grad = jnp.dot(mixed_heads.T, grad_attended, preferred_element_type=jnp.float32)
        bias_one_grad = jnp.sum(own_columns(grad_attended).astype(jnp.float32), 0)
        mixed_grad = (
            jnp.dot(grad_attended, proj_back.T, preferred_element_type=jnp.float32)
            .astype(jnp.bfloat16)
            .reshape(token_count, local_heads, head_width)
        )
        soft_again = jnp.exp(masked_scores() - log_total)
        value_grad = jnp.einsum(
            "hqk,qhd->khd",
            soft_again.astype(jnp.bfloat16),
            mixed_grad,
            preferred_element_type=jnp.float32,
        )
        soft_grad = jnp.einsum(
            "qhd,khd->hqk", mixed_grad, values_low, preferred_element_type=jnp.float32
        )
        score_grad = (
            soft_again * (soft_grad - jnp.sum(soft_again * soft_grad, -1, keepdims=True))
        ).astype(jnp.bfloat16)
        query_low_grad = jnp.einsum(
            "hqk,khd->qhd", score_grad, key_low, preferred_element_type=jnp.float32
        )
        key_low_grad = jnp.einsum(
            "hqk,qhd->khd", score_grad, query_low, preferred_element_type=jnp.float32
        )
        head_grad = jnp.sum(query_low_grad * query_unit * head_boost, (0, 2))
        query_unit_grad = query_low_grad * head_boost
        query_grad = query_inv * (
            query_unit_grad - query_unit * jnp.sum(query_unit_grad * query_unit, -1, keepdims=True)
        )
        key_grad = key_inv * (
            key_low_grad - key_unit * jnp.sum(key_low_grad * key_unit, -1, keepdims=True)
        )
        triple_grad = jnp.stack(
            [
                query_grad.reshape(token_count, column_count),
                key_grad.reshape(token_count, column_count),
                value_grad.reshape(token_count, column_count),
            ]
        ).astype(jnp.bfloat16)
        qkv_grad = jnp.einsum(
            "td,cte->cde", input_one, triple_grad, preferred_element_type=jnp.float32
        )
        pair_sums = jnp.sum(triple_grad.astype(jnp.float32), 1)
        qv_grad = jnp.stack([pair_sums[0], pair_sums[2]]).reshape(2, local_heads, head_width)
        input_one_grad = collect(
            jnp.einsum("cte,cde->td", triple_grad, qkv_back, preferred_element_type=jnp.float32)
        )
        scale_one_grad = jnp.sum(input_one_grad * normed_one, 0)
        shift_one_grad = jnp.sum(input_one_grad, 0)
        residual_grad = middle_grad + row_norm_back(
            input_one_grad * (1.0 + image_mods[2]), normed_one, inverse_one
        )
        token_grads = lax.dynamic_update_index_in_dim(
            token_grads, residual_grad.astype(jnp.bfloat16), image_at, 0
        )
        image_mod_grad = jnp.stack(
            [
                gamma_one_grad,
                gamma_two_grad,
                scale_one_grad,
                scale_two_grad,
                shift_one_grad,
                shift_two_grad,
            ]
        )
        mod_grads = lax.dynamic_update_index_in_dim(mod_grads, image_mod_grad, image_at, 0)
        outb_grad = jnp.stack([bias_one_grad, bias_two_grad]).reshape(2, local_heads, head_width)
        local_grads = (qkv_grad, qv_grad, proj_grad, outb_grad, fc1_grad, fc1b_grad, fc2_grad)
        weight_grads = tuple(
            (running + addend for running, addend in zip(weight_grads, local_grads))
        )
        return (outputs, token_grads, mod_grads, weight_grads, scale_grad + head_grad)

    start_state = (
        jnp.zeros(tokens.shape, jnp.bfloat16),
        jnp.zeros(tokens.shape, jnp.bfloat16),
        jnp.zeros((image_count, 6, model_width), jnp.float32),
        grad_start,
        jnp.zeros((local_heads,), jnp.float32),
    )
    outputs, token_grads, mod_grads, weight_grads, scale_grad = lax.fori_loop(
        0, image_count, micro_step, start_state
    )
    shard_grads = settle(weight_grads)
    mod_share_grad = lax.psum_scatter(
        mod_grads.astype(jnp.bfloat16), "mp", scatter_dimension=2, tiled=True
    ).astype(jnp.float32)
    flat_grad = mod_share_grad.reshape(image_count, 6 * column_count)
    ada_grad = jnp.dot(
        signal.astype(jnp.float32).T,
        flat_grad,
        precision=precise,
        preferred_element_type=jnp.float32,
    ).reshape(model_width, 6, column_count)
    ada_bias_grad = jnp.sum(mod_share_grad, 0).reshape(6, local_heads, head_width)
    signal_grad = lax.psum(
        jnp.dot(
            flat_grad,
            ada_flat.astype(jnp.float32).T,
            precision=precise,
            preferred_element_type=jnp.float32,
        ),
        "mp",
    )
    silu_pull = jax.vjp(jax.nn.silu, cond_float)[1]
    condition_grad = silu_pull(signal_grad)[0].astype(jnp.bfloat16)
    ada_shard, ada_bias_shard = (
        lax.psum_scatter(
            ada_grad.astype(jnp.bfloat16), "dp", scatter_dimension=0, tiled=True
        ).astype(jnp.float32),
        lax.psum_scatter(
            ada_bias_grad.astype(jnp.bfloat16), "dp", scatter_dimension=2, tiled=True
        ).astype(jnp.float32),
    )
    head_scale_grad = lax.psum(scale_grad, "dp")
    qkv_shard, qv_shard, proj_shard, outb_shard, fc1_shard, fc1b_shard, fc2_shard = shard_grads
    return (
        outputs,
        token_grads,
        condition_grad,
        ada_shard,
        ada_bias_shard,
        qkv_shard,
        qv_shard,
        head_scale_grad,
        proj_shard,
        outb_shard,
        fc1_shard,
        fc1b_shard,
        fc2_shard,
    )


def solution(mesh):
    in_specs = (
        P("dp", "mp", None),
        P("dp", None),
        P("dp", None),
        P("dp", None),
        P("dp", "mp", None),
        P("dp", None, "mp"),
        P(None, "mp", "dp"),
        P(None, "dp", "mp"),
        P(None, "mp", "dp"),
        P("mp"),
        P("mp", "dp"),
        P(None, "mp", "dp"),
        P("dp", "mp"),
        P("mp", "dp"),
        P("mp", "dp"),
    )
    out_specs = (
        P("dp", "mp", None),
        P("dp", "mp", None),
        P("dp", None),
        P("dp", None, "mp"),
        P(None, "mp", "dp"),
        P(None, "dp", "mp"),
        P(None, "mp", "dp"),
        P("mp"),
        P("mp", "dp"),
        P(None, "mp", "dp"),
        P("dp", "mp"),
        P("mp", "dp"),
        P("mp", "dp"),
    )
    line, spare = divmod(mesh.shape["dp"], 4)
    paired = mesh.shape["mp"] == 2 and spare == 0 and line > 1
    return jax.shard_map(
        on_device_paired if paired else on_device_shared, mesh=mesh, in_specs=in_specs, out_specs=out_specs, check_vma=False
    )
```
